256 devices in a mesh: section: 8 (over x, y_lo), expert: 16 (over z, core), dp: 2 (over y_hi).
Axes of the slice: x: 4, y: 4 (y_hi: 2, y_lo: 2; y = y_hi * 2 + y_lo), z: 8, core: 2. Of those that a mesh axis runs over, the one named last changes fastest.
Arguments:
- fwd_input: bfloat16 [8, 1536, 3584], P('section', ('expert', 'dp')), may hold values from -24 to 24
- back_saved: bfloat16 [2, 8, 1536, 3584], P(None, 'section', ('expert', 'dp')), may hold values from -24 to 24
- back_grad: bfloat16 [8, 1536, 3584], P('section', ('expert', 'dp')), may hold values from -6 to 6
- norm_gain: float32 [8, 3584], P('section'), may hold values from 0.3 to 3
- gate_weight: bfloat16 [8, 16, 3584, 1024], P('section', 'expert', 'dp'), may hold values from -0.09375 to 0.09375
- up_weight: bfloat16 [8, 16, 3584, 1024], P('section', 'expert', 'dp'), may hold values from -0.09375 to 0.09375
- down_weight: bfloat16 [8, 16, 1024, 3584], P('section', 'expert', None, 'dp'), may hold values from -0.1875 to 0.1875
- routes: int32 [4, 8, 1536, 2], P(None, 'section', ('expert', 'dp')), may hold values from 0 to 15, as said below
- slots: int32 [4, 8, 1536, 2], P(None, 'section', ('expert', 'dp')), may hold values from 0 to 6, as said below
- affinity: float32 [4, 8, 1536, 2], P(None, 'section', ('expert', 'dp')), may hold values from 0.05 to 1
Outputs:
- fwd_output: bfloat16 [8, 1536, 3584], P('section', ('expert', 'dp'))
- back_output: bfloat16 [8, 1536, 3584], P('section', ('expert', 'dp'))
The draws below stay inside these ranges and needn't reach their ends.
Inputs may be any that keep to these rules, and one draw needn't show every extreme that they name: A token's routes name distinct experts. In each aligned block of 48 tokens of one index of the first dimension and one section, each expert is named at most 7 times, and one expert exactly 7 times; that expert is the same for all blocks of one index of the first dimension, one section and one dp index. Within one aligned block of 48 tokens, the routes to one expert hold distinct slots.
All inputs are finite; a program needn't handle non-finite values.
Results may differ from the reference program's by a relative error of at most 0.012.
Values may be sent and summed in bfloat16 or wider, within the bound.
No kernel may reach another device: no remote copies, remote signals or barrier semaphores. Data moves between devices by JAX's collectives and lax.ppermute only.
A program may use at most 128 MiB of HBM per device.

```python
import math
import jax
import jax.numpy as jnp
from jax import lax

D = 3584
H = 1024
TOPK = 2
TOK_DEV = 48
EXPERTS = 16
TOKENS = 1536
CAP = 7
N_SECTION = 8
N_EXPERT = 16
N_DP = 2


def route_cells(key):
    blocks = 4 * N_SECTION * N_EXPERT * N_DP
    cells = EXPERTS * CAP
    chosen_count = TOK_DEV * TOPK
    key_full, key_rank, key_order, key_turn = jax.random.split(key, 4)
    full = jax.random.randint(key_full, (4, N_SECTION, 1, N_DP), 0, EXPERTS)
    full = jnp.broadcast_to(full, (4, N_SECTION, N_EXPERT, N_DP)).reshape(blocks, 1)
    cell_ids = jnp.arange(cells, dtype=jnp.int32)[None, :]
    ranking = jax.random.randint(key_rank, (blocks, cells), 0, 1 << 20) * cells + cell_ids
    ranking = jnp.where(cell_ids // CAP == full, -1, ranking)
    picked = jnp.argsort(ranking, axis=1, stable=True)[:, :chosen_count].astype(jnp.int32)
    picked = jnp.sort(picked, axis=1)
    layout = jnp.transpose(picked.reshape(blocks, TOPK, TOK_DEV), (0, 2, 1))
    token_ids = jnp.arange(TOK_DEV, dtype=jnp.int32)[None, :]
    order = jnp.argsort(jax.random.randint(key_order, (blocks, TOK_DEV), 0, 1 << 20) * TOK_DEV + token_ids, axis=1)
    layout = jnp.take_along_axis(layout, order[:, :, None].astype(jnp.int32), axis=1)
    turn = jax.random.randint(key_turn, (blocks, TOK_DEV, 1), 0, TOPK)
    columns = (jnp.arange(TOPK, dtype=jnp.int32)[None, None, :] + turn) % TOPK
    layout = jnp.take_along_axis(layout, columns, axis=2)
    return layout.reshape(4, N_SECTION, N_EXPERT * N_DP * TOK_DEV, TOPK)


def draw_routes(key, part):
    return (route_cells(key) // CAP).astype(jnp.int32)


def draw_slots(key, part):
    return (route_cells(key) % CAP).astype(jnp.int32)


def feature_field(key, shape):
    key_normal = jax.random.fold_in(key, 0)
    key_rows = jax.random.fold_in(key, 2)
    key_cols = jax.random.fold_in(key, 3)
    base = jax.random.normal(key_normal, shape, jnp.float32)
    row_scale = jnp.exp(jax.random.uniform(key_rows, shape[:-1] + (1,), jnp.float32, minval=math.log(0.3), maxval=math.log(3.0)))
    col_scale = jnp.exp(jax.random.uniform(key_cols, (shape[-1],), jnp.float32, minval=math.log(0.3), maxval=math.log(3.0)))
    return jnp.clip(base * row_scale * col_scale, -24.0, 24.0)


def draw_fwd_input(key, part):
    key = jax.random.fold_in(key, 1)
    field = feature_field(key, (N_SECTION, TOKENS, D))
    return field.astype(jnp.bfloat16)


def draw_back_saved(key, part):
    key = jax.random.fold_in(key, 2)
    field = feature_field(key, (2, N_SECTION, TOKENS, D))
    return field.astype(jnp.bfloat16)


def levels(own_key, extent, cuts, least, top_value):
    def one(dim, blocks):
        steps = jax.random.uniform(jax.random.fold_in(jax.random.fold_in(own_key, 6), dim), (blocks,), jnp.float32, least / len(cuts), top_value / len(cuts))
        return jnp.repeat(jnp.exp(steps), extent[dim] // blocks).reshape((-1,) + (1,) * (len(extent) - dim - 1))

    factor_of = one(*cuts[0])
    for cut in cuts[1:]:
        factor_of = factor_of * one(*cut)
    return factor_of


def bell_draw(own_key, shape, scale, most, cuts=(), held_as=jnp.bfloat16):
    level = levels(own_key, shape, cuts, -0.22, 0.18) if cuts else 1.0
    drawn = jax.random.normal(own_key, shape, jnp.float32) * scale * level
    return jnp.minimum(jnp.maximum(drawn, -most), most).astype(held_as)


def setup_inputs(seed: int = 0) -> dict:
    seeds = jax.random.split(jax.random.key(seed), 11)
    fwd_input = draw_fwd_input(jax.random.fold_in(seeds[10], 71), 0)
    back_saved = draw_back_saved(jax.random.fold_in(seeds[10], 71), 0)
    back_grad = bell_draw(seeds[2], (N_SECTION, TOKENS, D), 1.0, 6.0, ((0, 8), (1, 32)))
    norm_gain = jnp.clip(jnp.exp(math.log(3.0) - 2.3025851 * jax.random.uniform(seeds[3], (N_SECTION, D), jnp.float32) ** levels(seeds[3], (N_SECTION, D), ((0, 8),), -0.2, 0.2)), 0.3, 3.0)
    gate_weight = bell_draw(seeds[4], (N_SECTION, EXPERTS, D, H), D ** -0.5, 0.09375, ((0, 8), (1, 16), (2, 2)))
    up_weight = bell_draw(seeds[5], (N_SECTION, EXPERTS, D, H), D ** -0.5, 0.09375, ((0, 8), (1, 16), (2, 2)))
    down_weight = bell_draw(seeds[6], (N_SECTION, EXPERTS, H, D), H ** -0.5, 0.1875, ((0, 8), (1, 16), (3, 2)))
    routes = draw_routes(jax.random.fold_in(seeds[10], 71), 0)
    slots = draw_slots(jax.random.fold_in(seeds[10], 71), 0)
    affinity = jnp.clip(0.05 + 0.95 * jax.random.uniform(seeds[9], (4, N_SECTION, TOKENS, TOPK), jnp.float32) ** levels(seeds[9], (4, N_SECTION, TOKENS, TOPK), ((1, 8), (2, 32)), -0.2, 0.2), 0.05, 1.0)
    return dict(fwd_input=fwd_input, back_saved=back_saved, back_grad=back_grad, norm_gain=norm_gain, gate_weight=gate_weight, up_weight=up_weight, down_weight=down_weight, routes=routes, slots=slots, affinity=affinity)


ROUTE_SCALE = 2.5
EPSILON = 1e-06

def normalize(inputs, gain):
    widened = inputs.astype(jnp.float32)
    inverse = lax.rsqrt(lax.optimization_barrier(jnp.mean(widened * widened, axis=-1, keepdims=True)) + EPSILON)
    return (widened, inverse, (widened * inverse * gain).astype(jnp.bfloat16))

def contract_last(left, right):
    return lax.dot_general(left, right, (((1,), (1,)), ((), ())), preferred_element_type=jnp.float32)

def expert_forward(rows, gate_w, up_w, down_w):
    gate = jnp.dot(rows, gate_w, preferred_element_type=jnp.float32)
    upper = jnp.dot(rows, up_w, preferred_element_type=jnp.float32)
    active = (gate * jax.nn.sigmoid(gate) * upper).astype(jnp.bfloat16)
    return jnp.dot(active, down_w, preferred_element_type=jnp.float32).astype(jnp.bfloat16)

def swiglu_backward(gate, upper, dactive):
    sigma = jax.nn.sigmoid(gate)
    dgate = (dactive * upper * sigma * (1.0 + gate * (1.0 - sigma))).astype(jnp.bfloat16)
    dupper = (dactive * gate * sigma).astype(jnp.bfloat16)
    return (dgate, dupper)

def expert_backward(rows, grads, gate_w, up_w, down_w):
    gate = jnp.dot(rows, gate_w, preferred_element_type=jnp.float32)
    upper = jnp.dot(rows, up_w, preferred_element_type=jnp.float32)
    dactive = contract_last(grads, down_w)
    dgate, dupper = swiglu_backward(gate, upper, dactive)
    return (contract_last(dgate, gate_w) + contract_last(dupper, up_w)).astype(jnp.bfloat16)

def destinations(routes, slots):
    blocks = (jnp.arange(TOKENS) // TOK_DEV).astype(jnp.int32)
    return routes * (TOKENS // TOK_DEV * CAP) + blocks[:, None] * CAP + slots

def place_rows(values, targets):
    count = EXPERTS * (TOKENS // TOK_DEV) * CAP
    placed = jnp.zeros((count, D), jnp.bfloat16).at[targets.reshape(-1)].set(values.reshape(-1, D))
    return placed.reshape(EXPERTS, -1, D)

def layer_forward(inputs, gain, gate_w, up_w, down_w, routes, slots, affinity):
    widened, inverse, normed = normalize(inputs, gain)
    targets = destinations(routes, slots)
    placed = place_rows(jnp.broadcast_to(normed[:, None, :], (TOKENS, TOPK, D)), targets)
    outputs = lax.map(lambda parts: expert_forward(parts[0], parts[1], parts[2], parts[3]), (placed, gate_w, up_w, down_w))
    picked = outputs.reshape(-1, D)[targets].astype(jnp.float32)
    mixing = affinity / lax.optimization_barrier(jnp.sum(affinity, axis=-1, keepdims=True))
    return (widened + ROUTE_SCALE * lax.optimization_barrier(jnp.sum(mixing[:, :, None] * picked, axis=1))).astype(jnp.bfloat16)

def layer_backward(inputs, grads, gain, gate_w, up_w, down_w, routes, slots, affinity):
    widened, inverse, normed = normalize(inputs, gain)
    targets = destinations(routes, slots)
    mixing = affinity / lax.optimization_barrier(jnp.sum(affinity, axis=-1, keepdims=True))
    wide_grads = grads.astype(jnp.float32)
    sent = (ROUTE_SCALE * mixing[:, :, None] * wide_grads[:, None, :]).astype(jnp.bfloat16)
    placed = place_rows(jnp.broadcast_to(normed[:, None, :], (TOKENS, TOPK, D)), targets)
    placed_grads = place_rows(sent, targets)
    results = lax.map(lambda parts: expert_backward(parts[0], parts[1], parts[2], parts[3], parts[4]), (placed, placed_grads, gate_w, up_w, down_w))
    dnormed = lax.optimization_barrier(jnp.sum(results.reshape(-1, D)[targets].astype(jnp.float32), axis=1))
    weighted = dnormed * gain
    project = lax.optimization_barrier(jnp.mean(weighted * widened, axis=-1, keepdims=True))
    return (wide_grads + inverse * (weighted - widened * inverse * inverse * project)).astype(jnp.bfloat16)

def reference(fwd_input, back_saved, back_grad, norm_gain, gate_weight, up_weight, down_weight, routes, slots, affinity):

    def forward_section(section, inputs, index):
        return layer_forward(inputs, norm_gain[section], gate_weight[section], up_weight[section], down_weight[section], routes[index, section], slots[index, section], affinity[index, section])

    def backward_section(section, inputs, grads, index):
        return layer_backward(inputs, grads, norm_gain[section], gate_weight[section], up_weight[section], down_weight[section], routes[index, section], slots[index, section], affinity[index, section])
    blank = jnp.zeros((TOKENS, D), jnp.bfloat16)
    first = [forward_section(section, fwd_input[section], 0) for section in range(N_SECTION)]
    back_first = [backward_section(section, back_saved[0, section], back_grad[section], 1) for section in range(N_SECTION)]
    moved = [blank] + first[:-1]
    moved_back = back_first[1:] + [blank]
    final = [forward_section(section, moved[section], 2) for section in range(N_SECTION)]
    final_back = [backward_section(section, back_saved[1, section], moved_back[section], 3) for section in range(N_SECTION)]
    return (jnp.stack(final), jnp.stack(final_back))
```

```python
import jax
import jax.numpy as jnp
from jax import lax
from jax.sharding import PartitionSpec as P

ROUTE_SCALE = 2.5
EPSILON = 1e-06
GROUP = 16
BF16 = jnp.bfloat16
F32 = jnp.float32


def swap_dp(value):
    return lax.ppermute(value, "dp", [(0, 1), (1, 0)])


def move_section(value, step, flip_dp=False):
    sections = lax.axis_size("section")
    halves = lax.axis_size("dp")
    route = []
    for s in range(sections):
        if 0 <= s + step < sections:
            for d in range(halves):
                to = 1 - d if flip_dp else d
                route.append((s * halves + d, (s + step) * halves + to))
    return lax.ppermute(value, ("section", "dp"), route)


def to_experts(rows):
    groups = rows.reshape(-1, GROUP, rows.shape[-1])
    moved = lax.all_to_all(groups, "expert", split_axis=0, concat_axis=0, tiled=True)
    return moved.reshape(rows.shape)


def contract_last(left, right):
    return lax.dot_general(left, right, (((1,), (1,)), ((), ())), preferred_element_type=F32)


def matmul(left, right):
    return jnp.dot(left, right, preferred_element_type=F32)


def pick(selector, rows):
    return lax.dot_general(selector, rows, (((0,), (0,)), ((), ())), preferred_element_type=F32)


def body(
    fwd_input,
    back_saved,
    back_grad,
    norm_gain,
    gate_weight,
    up_weight,
    down_weight,
    routes,
    slots,
    affinity,
):
    experts = lax.axis_size("expert")
    tokens = fwd_input.shape[1]
    width = fwd_input.shape[2]
    half = width // 2
    capacity = 7
    row_count = experts * GROUP
    side = lax.axis_index("dp")
    gate_w, up_w, down_w = gate_weight[0, 0], up_weight[0, 0], down_weight[0, 0]
    gain = norm_gain[0]
    gain_half = lax.dynamic_slice(gain, (side * half,), (half,))

    x0, s0, s1, g0 = fwd_input[0], back_saved[0, 0], back_saved[1, 0], back_grad[0]

    def inverse_of(value):
        wide = value.astype(F32)
        return lax.rsqrt(jnp.mean(wide * wide, axis=-1) + EPSILON)

    targets = routes[:, 0] * GROUP + slots[:, 0] + side * capacity
    mixing = affinity[:, 0] / jnp.sum(affinity[:, 0], axis=-1, keepdims=True)
    scalars = jnp.concatenate(
        [
            jnp.stack([inverse_of(x0), inverse_of(s0), inverse_of(s1)]),
            jnp.transpose(targets.astype(F32), (0, 2, 1)).reshape(8, tokens),
            jnp.transpose(mixing, (0, 2, 1)).reshape(8, tokens),
        ]
    )

    def in_order(own, other):
        first = jnp.where(side == 0, own, other)
        second = jnp.where(side == 0, other, own)
        return first, second

    first, second = in_order(scalars, swap_dp(scalars))
    table = jnp.concatenate([first, second], axis=1)
    inverses = table[:3]
    marks = table[3:11].astype(jnp.int32).reshape(4, 2, -1)
    mixes = table[11:].reshape(4, 2, -1)

    def exchange_halves(value):
        lead = value.shape[:-1]
        own = lax.dynamic_slice_in_dim(value, side * half, half, axis=-1)
        other = lax.dynamic_slice_in_dim(value, (1 - side) * half, half, axis=-1)
        a, b = in_order(own, swap_dp(other))
        return jnp.concatenate([a, b], axis=-2)

    def selectors(index):
        rows = lax.broadcasted_iota(jnp.int32, (row_count, 2 * tokens), 0)
        return [(rows == marks[index, k][None, :]).astype(BF16) for k in range(2)]

    def normed_of(value, inverse):
        return (value.astype(F32) * inverse[:, None] * gain_half).astype(BF16)

    def place_same(index, value):
        a, b = selectors(index)
        return matmul(a + b, value).astype(BF16)

    def place_pair(index, pair):
        a, b = selectors(index)
        return matmul(
            jnp.concatenate([a, b], axis=1), jnp.concatenate(pair, axis=0)
        ).astype(BF16)

    def dp_sum(parts):
        sent = jnp.concatenate([part.astype(BF16) for part in parts], axis=1)
        got = swap_dp(sent).astype(F32)
        hidden = parts[0].shape[1]
        return [p + got[:, i * hidden : (i + 1) * hidden] for i, p in enumerate(parts)]

    def gate_up_parts(rows):
        return [matmul(rows, gate_w), matmul(rows, up_w)]

    def expert_forward(rows):
        gate, upper = dp_sum(gate_up_parts(rows))
        active = (gate * jax.nn.sigmoid(gate) * upper).astype(BF16)
        return matmul(active, down_w).astype(BF16)

    def expert_backward(gate, upper, dactive):
        sigma = jax.nn.sigmoid(gate)
        dgate = (dactive * upper * sigma * (1.0 + gate * (1.0 - sigma))).astype(BF16)
        dupper = (dactive * gate * sigma).astype(BF16)
        return (contract_last(dgate, gate_w) + contract_last(dupper, up_w)).astype(BF16)

    def combine_forward(index, value, rows):
        a, b = selectors(index)
        m = mixes[index]
        total = m[0][:, None] * pick(a, rows) + m[1][:, None] * pick(b, rows)
        return (value.astype(F32) + ROUTE_SCALE * total).astype(BF16)

    def sent_pair(index, grads):
        wide = grads.astype(F32)
        return [
            (ROUTE_SCALE * mixes[index, k][:, None] * wide).astype(BF16) for k in range(2)
        ]

    def combine_backward(index, saved, inverse, grads, rows):
        a, b = selectors(index)
        dnormed = pick(a, rows) + pick(b, rows)
        weighted = dnormed * gain_half
        wide = saved.astype(F32)
        part = jnp.sum(weighted * wide, axis=-1)[None]
        project = ((part + swap_dp(part)) / width)[0][:, None]
        inv = inverse[:, None]
        return (
            grads.astype(F32) + inv * (weighted - wide * inv * inv * project)
        ).astype(BF16)

    x0h = exchange_halves(x0)
    x0_rows = to_experts(place_same(0, normed_of(x0h, inverses[0])))
    sg = exchange_halves(jnp.stack([s0, g0]))
    s0h, g0h = sg[0], sg[1]
    s0_rows = to_experts(place_same(1, normed_of(s0h, inverses[1])))
    g0_rows = to_experts(place_pair(1, sent_pair(1, g0h)))
    out0 = expert_forward(x0_rows)
    s1h = exchange_halves(s1)
    s1_rows = to_experts(place_same(3, normed_of(s1h, inverses[2])))
    gate0, upper0, dactive0 = dp_sum(gate_up_parts(s0_rows) + [contract_last(g0_rows, down_w)])
    dexp0 = expert_backward(gate0, upper0, dactive0)
    gate1, upper1 = dp_sum(gate_up_parts(s1_rows))

    first_out = combine_forward(0, x0h, to_experts(out0))
    wide_out = first_out.astype(F32)
    square = jnp.sum(wide_out * wide_out, axis=-1)[None]
    x2h = move_section(first_out, 1)
    square_own = move_section(square, 1)
    square_other = move_section(square, 1, flip_dp=True)
    inverse2 = lax.rsqrt((square_own + square_other)[0] / width + EPSILON)
    x2_rows = to_experts(place_same(2, normed_of(x2h, inverse2)))

    first_back = combine_backward(1, s0h, inverses[1], g0h, to_experts(dexp0))
    g3h = move_section(first_back, -1)
    g3_rows = to_experts(place_pair(3, sent_pair(3, g3h)))

    out2 = expert_forward(x2_rows)
    final_out = combine_forward(2, x2h, to_experts(out2))
    (dactive1,) = dp_sum([contract_last(g3_rows, down_w)])
    dexp1 = expert_backward(gate1, upper1, dactive1)
    final_back = combine_backward(3, s1h, inverses[2], g3h, to_experts(dexp1))

    def restore(value):
        first, second = value[:tokens], value[tokens:]
        mine = jnp.where(side == 0, first, second)
        theirs = jnp.where(side == 0, second, first)
        a, b = in_order(mine, swap_dp(theirs))
        return jnp.concatenate([a, b], axis=-1)

    return (restore(final_out)[None], restore(final_back)[None])


def solution(mesh):
    placed = (
        P("section", ("expert", "dp"), None),
        P(None, "section", ("expert", "dp"), None),
        P("section", ("expert", "dp"), None),
        P("section", None),
        P("section", "expert", "dp", None),
        P("section", "expert", "dp", None),
        P("section", "expert", None, "dp"),
        P(None, "section", ("expert", "dp"), None),
        P(None, "section", ("expert", "dp"), None),
        P(None, "section", ("expert", "dp"), None),
    )
    return jax.shard_map(
        body,
        mesh=mesh,
        in_specs=placed,
        out_specs=(P("section", ("expert", "dp"), None), P("section", ("expert", "dp"), None)),
        check_vma=False,
    )
```

```python
import jax
import jax.numpy as jnp
from jax import lax
from jax.sharding import PartitionSpec as P

ROUTE_SCALE = 2.5
EPSILON = 1e-06
BLOCK = 8
GROUP = 2 * BLOCK
BF16 = jnp.bfloat16
F32 = jnp.float32


def swap_dp(value):
    return lax.ppermute(value, "dp", [(0, 1), (1, 0)])


def move_section(value, step, flip_dp=False):
    sections = lax.axis_size("section")
    halves = lax.axis_size("dp")
    route = []
    for s in range(sections):
        if 0 <= s + step < sections:
            for d in range(halves):
                to = 1 - d if flip_dp else d
                route.append((s * halves + d, (s + step) * halves + to))
    return lax.ppermute(value, ("section", "dp"), route)


def route_rows(rows, axes="expert"):
    devices = lax.axis_size(axes)
    groups = rows.reshape(devices, -1, rows.shape[-1])
    moved = lax.all_to_all(groups, axes, split_axis=0, concat_axis=0, tiled=True)
    return moved.reshape(rows.shape)


def after(value, *earlier):
    return lax.optimization_barrier((value, *earlier))[0]


def contract_last(left, right):
    return lax.dot_general(left, right, (((1,), (1,)), ((), ())), preferred_element_type=F32)


def matmul(left, right):
    return jnp.dot(left, right, preferred_element_type=F32)


def pick(selector, rows):
    return lax.dot_general(selector, rows, (((0,), (0,)), ((), ())), preferred_element_type=F32)


def body(
    fwd_input,
    back_saved,
    back_grad,
    norm_gain,
    gate_weight,
    up_weight,
    down_weight,
    routes,
    slots,
    affinity,
):
    experts = lax.axis_size("expert")
    tokens = fwd_input.shape[1]
    width = fwd_input.shape[2]
    half = width // 2
    row_count = experts * GROUP
    side = lax.axis_index("dp")
    gate_w, up_w, down_w = gate_weight[0, 0], up_weight[0, 0], down_weight[0, 0]
    gain = norm_gain[0]
    gain_half = lax.dynamic_slice(gain, (side * half,), (half,))

    x0, s0, s1, g0 = fwd_input[0], back_saved[0, 0], back_saved[1, 0], back_grad[0]

    def inverse_of(value):
        wide = value.astype(F32)
        return lax.rsqrt(jnp.mean(wide * wide, axis=-1) + EPSILON)

    def in_order(own, other):
        return jnp.where(side == 0, own, other), jnp.where(side == 0, other, own)

    def split_halves(value):
        own = lax.dynamic_slice_in_dim(value, side * half, half, axis=-1)
        other = lax.dynamic_slice_in_dim(value, (1 - side) * half, half, axis=-1)
        return own, other

    def selector(marks):
        rows = lax.broadcasted_iota(jnp.int32, (row_count, marks.shape[-1]), 0)
        return (rows == marks[None, :]).astype(BF16)

    local = jnp.transpose(routes[:, 0] * GROUP + slots[:, 0], (0, 2, 1))
    local_mix = jnp.transpose(
        affinity[:, 0] / jnp.sum(affinity[:, 0], axis=-1, keepdims=True), (0, 2, 1)
    )

    def normed_of(value, inverse, scale):
        return (value.astype(F32) * inverse[:, None] * scale).astype(BF16)

    def spread(index, value):
        sides = [
            sum(selector(local[index, k] + h * BLOCK) for k in range(2)) for h in range(2)
        ]
        return matmul(
            jnp.concatenate(sides, axis=1),
            jnp.concatenate([value[:, :half], value[:, half:]], axis=0),
        ).astype(BF16)

    def gather_home(index, rows):
        return [
            jnp.concatenate(
                [pick(selector(local[index, k] + h * BLOCK), rows) for h in range(2)], axis=1
            )
            for k in range(2)
        ]

    scalars = jnp.concatenate(
        [
            jnp.stack([inverse_of(s0), inverse_of(s1)]),
            (local + side * BLOCK).astype(F32).reshape(8, tokens),
            local_mix.reshape(8, tokens),
        ]
    )
    table = jnp.concatenate(in_order(scalars, swap_dp(scalars)), axis=1)
    inverses = table[:2]
    marks = table[2:10].astype(jnp.int32).reshape(4, 2, -1)
    mixes = table[10:].reshape(4, 2, -1)

    def place_same(index, value):
        return matmul(selector(marks[index, 0]) + selector(marks[index, 1]), value).astype(BF16)

    def place_pair(index, pair):
        both = jnp.concatenate([selector(marks[index, k]) for k in range(2)], axis=1)
        return matmul(both, jnp.concatenate(pair, axis=0)).astype(BF16)

    def dp_sum(parts):
        sent = jnp.concatenate([part.astype(BF16) for part in parts], axis=1)
        got = swap_dp(sent).astype(F32)
        hidden = parts[0].shape[1]
        return [p + got[:, i * hidden : (i + 1) * hidden] for i, p in enumerate(parts)]

    def gate_up_parts(rows):
        return [matmul(rows, gate_w), matmul(rows, up_w)]

    def forward_rest(gate, upper):
        active = (gate * jax.nn.sigmoid(gate) * upper).astype(BF16)
        return matmul(active, down_w).astype(BF16)

    def backward_rest(gate, upper, dactive):
        sigma = jax.nn.sigmoid(gate)
        dgate = (dactive * upper * sigma * (1.0 + gate * (1.0 - sigma))).astype(BF16)
        dupper = (dactive * gate * sigma).astype(BF16)
        return (contract_last(dgate, gate_w) + contract_last(dupper, up_w)).astype(BF16)

    def forward_result(value, mix, picked):
        total = mix[0][:, None] * picked[0] + mix[1][:, None] * picked[1]
        return (value.astype(F32) + ROUTE_SCALE * total).astype(BF16)

    def sent_pair(index, grads):
        wide = grads.astype(F32)
        return [
            (ROUTE_SCALE * mixes[index, k][:, None] * wide).astype(BF16) for k in range(2)
        ]

    def backward_result(saved, inverse, grads, weighted, project):
        inv = inverse[:, None]
        return (
            grads.astype(F32)
            + inv * (weighted - saved.astype(F32) * inv * inv * project)
        ).astype(BF16)

    def pick_both(index, rows):
        return [pick(selector(marks[index, k]), rows) for k in range(2)]

    def side_by_side(first, second):
        shape = (experts, GROUP, half)
        joined = jnp.concatenate([first.reshape(shape), second.reshape(shape)], axis=1)
        moved = route_rows(joined.reshape(-1, half)).reshape(experts, 2 * GROUP, half)
        return moved[:, :GROUP].reshape(-1, half), moved[:, GROUP:].reshape(-1, half)

    def swap_halves(values):
        own, other = split_halves(jnp.stack(values))
        a, b = in_order(own, swap_dp(other))
        joined = jnp.concatenate([a, b], axis=1)
        return [joined[i] for i in range(len(values))]

    both_sides = ("expert", "dp")
    x0_sent = spread(0, normed_of(x0, inverse_of(x0), gain))
    x0_rows = route_rows(x0_sent, both_sides)
    s0h, g0h = swap_halves([s0, g0])
    x0h, s1h = swap_halves([x0, s1])
    s0_sent = place_same(1, normed_of(s0h, inverses[0], gain_half))
    g0_sent = place_pair(1, sent_pair(1, g0h))
    s0_sent = after(s0_sent, x0_rows)
    s0_rows, g0_rows = side_by_side(s0_sent, g0_sent)
    out0 = forward_rest(*dp_sum(gate_up_parts(x0_rows)))
    s1_sent = place_same(3, normed_of(s1h, inverses[1], gain_half))
    s1_sent = after(s1_sent, s0_rows)
    out0_back, s1_rows = side_by_side(out0, s1_sent)
    dexp0 = backward_rest(
        *dp_sum(gate_up_parts(s0_rows) + [contract_last(g0_rows, down_w)])
    )
    dexp0 = after(dexp0, out0_back)
    dexp0_back = route_rows(dexp0)

    first_out = forward_result(x0h, mixes[0], pick_both(0, out0_back))
    wide_out = first_out.astype(F32)
    square = jnp.sum(wide_out * wide_out, axis=-1)[None]
    x2h = move_section(first_out, 1)
    square_own = move_section(square, 1)
    square_other = move_section(square, 1, flip_dp=True)
    inverse2 = lax.rsqrt((square_own + square_other)[0] / width + EPSILON)
    x2_sent = place_same(2, normed_of(x2h, inverse2, gain_half))
    x2_sent = after(x2_sent, dexp0_back)
    x2_rows = route_rows(x2_sent)
    gate1, upper1 = dp_sum(gate_up_parts(s1_rows))

    back_picked = pick_both(1, dexp0_back)
    weighted = (back_picked[0] + back_picked[1]) * gain_half
    part = jnp.sum(weighted * s0h.astype(F32), axis=-1)[None]
    project = ((part + swap_dp(part)) / width)[0][:, None]
    first_back = backward_result(s0h, inverses[0], g0h, weighted, project)
    g3h = move_section(first_back, -1)
    g3_sent = place_pair(3, sent_pair(3, g3h))
    g3_sent = after(g3_sent, x2_rows)
    g3_rows = route_rows(g3_sent)

    def full_features(value):
        mine, theirs = in_order(value[:tokens], value[tokens:])
        return jnp.concatenate(in_order(mine, swap_dp(theirs)), axis=1)

    x2 = full_features(x2h)
    g3 = full_features(g3h)
    out2 = forward_rest(*dp_sum(gate_up_parts(x2_rows)))
    out2 = after(out2, g3_rows)
    out2_back = route_rows(out2, both_sides)
    (dactive1,) = dp_sum([contract_last(g3_rows, down_w)])
    dexp1 = backward_rest(gate1, upper1, dactive1)
    dexp1 = after(dexp1, out2_back)
    dexp1_back = route_rows(dexp1, both_sides)

    final_out = forward_result(x2, local_mix[2], gather_home(2, out2_back))
    back_picked = gather_home(3, dexp1_back)
    weighted = (back_picked[0] + back_picked[1]) * gain
    project = jnp.mean(weighted * s1.astype(F32), axis=-1, keepdims=True)
    final_back = backward_result(s1, inverse_of(s1), g3, weighted, project)
    return (final_out[None], final_back[None])


def solution(mesh):
    placed = (
        P("section", ("expert", "dp"), None),
        P(None, "section", ("expert", "dp"), None),
        P("section", ("expert", "dp"), None),
        P("section", None),
        P("section", "expert", "dp", None),
        P("section", "expert", "dp", None),
        P("section", "expert", None, "dp"),
        P(None, "section", ("expert", "dp"), None),
        P(None, "section", ("expert", "dp"), None),
        P(None, "section", ("expert", "dp"), None),
    )
    return jax.shard_map(
        body,
        mesh=mesh,
        in_specs=placed,
        out_specs=(P("section", ("expert", "dp"), None), P("section", ("expert", "dp"), None)),
        check_vma=False,
    )
```

```python
import functools

import jax
import jax.numpy as jnp
from jax import lax
from jax.experimental import pallas as pl
from jax.experimental.pallas import tpu as pltpu
from jax.sharding import PartitionSpec as P

ROUTE_SCALE = 2.5
EPSILON = 1e-06
BF16 = jnp.bfloat16
F32 = jnp.float32
SLOTS = 7
LANES = 128
STEP = 256
MARK = 2
MIX = 10


def ceil8(count):
    return -(-count // 8) * 8


def call(kernel, out_shape, scratch, operands, flops, in_hbm=(), name=None):
    specs = [
        pl.BlockSpec(memory_space=pl.ANY if i in in_hbm else pltpu.VMEM)
        for i in range(len(operands))
    ]
    moved = sum(x.size * x.dtype.itemsize for x in operands)
    return pl.pallas_call(
        kernel,
        out_shape=out_shape,
        in_specs=specs,
        out_specs=jax.tree.map(lambda _: pl.BlockSpec(memory_space=pltpu.VMEM), out_shape),
        scratch_shapes=scratch,
        compiler_params=pltpu.CompilerParams(vmem_limit_bytes=40 * 1024 * 1024),
        cost_estimate=pl.CostEstimate(flops=flops, bytes_accessed=moved, transcendentals=0),
        name=name,
    )(*operands)


def struct(shape, dtype):
    return jax.ShapeDtypeStruct(shape, dtype)


def dot(left, right):
    return jnp.dot(left, right, preferred_element_type=F32)


def dot_last(left, right):
    return lax.dot_general(left, right, (((1,), (1,)), ((), ())), preferred_element_type=F32)


def put_columns(pieces, step, value):
    for j in range(STEP // LANES):
        pieces[step * (STEP // LANES) + j] = value[:, j * LANES : (j + 1) * LANES]


def fold(pieces, message, count, base, groups):
    for group, first in groups:
        for c in range(pieces.shape[0]):
            message[group, base + c * count : base + (c + 1) * count, :] = pieces[
                c, first : first + count, :
            ]


def unfold(message, pieces, count, base, groups):
    for group, first in groups:
        for c in range(pieces.shape[0]):
            pieces[c, first : first + count, :] = message[
                group, base + c * count : base + (c + 1) * count, :
            ]


def clear_padding(message, count, base, size):
    used = base + count * size
    if ceil8(used) > used:
        shape = (message.shape[0], ceil8(used) - used, LANES)
        message[:, used : ceil8(used), :] = jnp.zeros(shape, F32)


def join(pieces, rows):
    for c in range(pieces.shape[0]):
        rows[:, c * LANES : (c + 1) * LANES] = pieces[c].astype(BF16)


def widen(source, message, low, high):
    for g in range(message.shape[0]):
        message[g] = source[g, low:high, :].astype(F32)


def narrow(message, out):
    for g in range(message.shape[0]):
        out[g] = message[g].astype(BF16)


def row_selector(marks, rows):
    places = lax.broadcasted_iota(jnp.int32, (rows, marks.shape[1]), 0).astype(F32)
    return jnp.where(places == marks, 1.0, 0.0).astype(BF16)


def token_selector(marks, rows):
    places = lax.broadcasted_iota(jnp.int32, (marks.shape[0], rows), 1).astype(F32)
    return jnp.where(places == marks, 1.0, 0.0).astype(BF16)


def spread_kernel(indices, scalars, gain, *refs):
    count = len(indices)
    values, (out, pieces, message, normed) = refs[:count], refs[count:]
    half = pieces.shape[0] * LANES
    rows = pieces.shape[1]
    size = ceil8(SLOTS * pieces.shape[0])
    for t, (index, value) in enumerate(zip(indices, values)):
        wide = value[...].astype(F32)
        inverse = lax.rsqrt(jnp.mean(wide * wide, axis=-1, keepdims=True) + EPSILON)
        normed[...] = (wide * inverse * gain[...]).astype(BF16)
        chosen = sum(
            row_selector(scalars[MARK + 2 * index + k : MARK + 2 * index + k + 1, :], rows)
            for k in range(2)
        )
        for h in range(2):
            for n in range(half // STEP):
                low = h * half + n * STEP
                put_columns(pieces, n, dot(chosen, normed[:, low : low + STEP]))
            fold(
                pieces,
                message,
                SLOTS,
                t * size,
                [(2 * e + h, e * SLOTS) for e in range(rows // SLOTS)],
            )
        clear_padding(message, SLOTS, t * size, pieces.shape[0])
    narrow(message, out)


def spread(indices, scalars, gain, values, experts):
    tokens, width = values[0].shape
    chunks = width // 2 // LANES
    rows = experts * SLOTS
    shape = (2 * experts, len(values) * ceil8(SLOTS * chunks), LANES)
    return call(
        functools.partial(spread_kernel, indices),
        struct(shape, BF16),
        [
            pltpu.VMEM((chunks, rows, LANES), F32),
            pltpu.VMEM(shape, F32),
            pltpu.VMEM((tokens, width), BF16),
        ],
        (scalars, gain, *values),
        2 * len(values) * rows * tokens * width * 4,
        name="spread",
    )


def place_kernel(parts, rows, table, columns, gain, *refs):
    *inputs, out, pieces, message, ready = refs
    chunks = pieces.shape[0]
    half = chunks * LANES
    count = 2 * SLOTS
    size = ceil8(count * chunks)
    inputs = iter(inputs)
    for t, (kind, index) in enumerate(parts):
        value = next(inputs)[...].astype(F32)
        tokens = value.shape[0]
        pick = [
            row_selector(table[MARK + 2 * index + k : MARK + 2 * index + k + 1, :], rows)
            for k in range(2)
        ]
        if kind == "grads":
            for k in range(2):
                mix = columns[:, MIX + 2 * index + k : MIX + 2 * index + k + 1]
                ready[k * tokens : (k + 1) * tokens, :] = (ROUTE_SCALE * mix * value).astype(BF16)
            chosen = jnp.concatenate(pick, axis=1)
        else:
            if kind == "saved":
                inverse = columns[:, 1:2]
            else:
                squares = next(inputs)[...] + next(inputs)[...]
                inverse = lax.rsqrt(squares / (2 * half) + EPSILON)
            ready[0:tokens, :] = (value * inverse * gain[...]).astype(BF16)
            chosen = pick[0] + pick[1]
        depth = chosen.shape[1]
        for n in range(half // STEP):
            put_columns(pieces, n, dot(chosen, ready[0:depth, n * STEP : (n + 1) * STEP]))
        fold(
            pieces, message, count, t * size, [(e, e * count) for e in range(rows // count)]
        )
        clear_padding(message, count, t * size, chunks)
    narrow(message, out)


def place(parts, table, columns, gain, inputs, experts):
    tokens, half = inputs[0].shape
    chunks = half // LANES
    rows = experts * 2 * SLOTS
    shape = (experts, len(parts) * ceil8(2 * SLOTS * chunks), LANES)
    return call(
        functools.partial(place_kernel, parts, rows),
        struct(shape, BF16),
        [
            pltpu.VMEM((chunks, rows, LANES), F32),
            pltpu.VMEM(shape, F32),
            pltpu.VMEM((2 * tokens, half), BF16),
        ],
        (table, columns, gain, *inputs),
        2 * len(parts) * rows * 2 * tokens * half * 2,
        name="place",
    )


def message_rows(message):
    array, part, parts = message
    size = array.shape[1] // parts
    low = part * size // 16 * 16
    high = min(array.shape[1], -(-(part + 1) * size // 16) * 16)
    return low, high, part * size - low


def expert_groups(groups, rows):
    return [(g, g * (rows // groups)) for g in range(groups)]


def partial_kernel(bounds, last, source, *refs):
    low, high, base = bounds
    count = (len(refs) - 6) // 2
    weights, refs = refs[:count], refs[count:]
    sent, own, message, pieces, rows = refs[:5]
    held, sems = refs[5:-1], refs[-1]
    hidden = sent.shape[1] // count
    copies = []
    for n in range(hidden // STEP):
        for w in range(count):
            at = pl.ds(n * STEP, STEP)
            where = (at, slice(None)) if last else (slice(None), at)
            copies.append(
                pltpu.make_async_copy(weights[w].at[where], held[w].at[where], sems.at[w, n])
            )
            copies[-1].start()
    widen(source, message, low, high)
    groups = message.shape[0]
    total = rows.shape[0]
    unfold(message, pieces, total // groups, base, expert_groups(groups, total))
    join(pieces, rows)
    copies = iter(copies)
    for n in range(hidden // STEP):
        for w in range(count):
            next(copies).wait()
            at = slice(n * STEP, (n + 1) * STEP)
            if last:
                result = dot_last(rows[...], held[w][at, :])
            else:
                result = dot(rows[...], held[w][:, at])
            place_at = slice(w * hidden + n * STEP, w * hidden + (n + 1) * STEP)
            own[:, place_at] = result
            sent[:, place_at] = result.astype(BF16)


def partial(message, weights, rows, last):
    source = message[0]
    low, high, base = message_rows(message)
    width, hidden = weights[0].shape[::-1] if last else weights[0].shape
    shape = (rows, len(weights) * hidden)
    return call(
        functools.partial(partial_kernel, (low, high, base), last),
        (struct(shape, BF16), struct(shape, F32)),
        [
            pltpu.VMEM((source.shape[0], high - low, LANES), F32),
            pltpu.VMEM((width // LANES, rows, LANES), F32),
            pltpu.VMEM((rows, width), BF16),
            *[pltpu.VMEM(w.shape, BF16) for w in weights],
            pltpu.SemaphoreType.DMA((len(weights), hidden // STEP)),
        ],
        (source, *weights),
        2 * rows * width * shape[1],
        in_hbm=range(1, 1 + len(weights)),
        name="partial",
    )


def finish(message, pieces, groups, out):
    total = pieces.shape[1]
    count = total // groups
    fold(pieces, message, count, 0, expert_groups(groups, total))
    clear_padding(message, count, 0, pieces.shape[0])
    narrow(message, out)


def forward_kernel(own, got, weight, out, active, pieces, message, held, sems):
    width = held.shape[1]
    hidden = held.shape[0]
    copies = []
    for n in range(width // STEP):
        at = (slice(None), pl.ds(n * STEP, STEP))
        copies.append(pltpu.make_async_copy(weight.at[at], held.at[at], sems.at[n]))
        copies[-1].start()
    for n in range(hidden // STEP):
        a = slice(n * STEP, (n + 1) * STEP)
        b = slice(hidden + n * STEP, hidden + (n + 1) * STEP)
        gate = own[:, a] + got[:, a].astype(F32)
        upper = own[:, b] + got[:, b].astype(F32)
        active[:, a] = (gate * jax.nn.sigmoid(gate) * upper).astype(BF16)
    for n in range(width // STEP):
        copies[n].wait()
        put_columns(pieces, n, dot(active[...], held[:, n * STEP : (n + 1) * STEP]))
    finish(message, pieces, out.shape[0], out)


def message_shape(groups, rows, chunks):
    return (groups, ceil8(rows // groups * chunks), LANES)


def forward_rest(own, got, weight, groups):
    rows = own.shape[0]
    hidden, width = weight.shape
    shape = message_shape(groups, rows, width // LANES)
    return call(
        forward_kernel,
        struct(shape, BF16),
        [
            pltpu.VMEM((rows, hidden), BF16),
            pltpu.VMEM((width // LANES, rows, LANES), F32),
            pltpu.VMEM(shape, F32),
            pltpu.VMEM(weight.shape, BF16),
            pltpu.SemaphoreType.DMA((width // STEP,)),
        ],
        (own, got, weight),
        2 * rows * width * hidden,
        in_hbm=(2,),
        name="forward_rest",
    )


def backward_kernel(
    own, got, down_own, down_got, gate_w, up_w, out, dgate, dupper, pieces, message, held_gate, held_up, sems
):
    width, hidden = held_gate.shape
    copies = []
    for n in range(width // STEP):
        at = pl.ds(n * STEP, STEP)
        for w, (weight, held) in enumerate(((gate_w, held_gate), (up_w, held_up))):
            copies.append(pltpu.make_async_copy(weight.at[at], held.at[at], sems.at[w, n]))
            copies[-1].start()
    for n in range(hidden // STEP):
        a = slice(n * STEP, (n + 1) * STEP)
        b = slice(hidden + n * STEP, hidden + (n + 1) * STEP)
        gate = own[:, a] + got[:, a].astype(F32)
        upper = own[:, b] + got[:, b].astype(F32)
        dactive = down_own[:, a] + down_got[:, a].astype(F32)
        sigma = jax.nn.sigmoid(gate)
        dgate[:, a] = (dactive * upper * sigma * (1.0 + gate * (1.0 - sigma))).astype(BF16)
        dupper[:, a] = (dactive * gate * sigma).astype(BF16)
    for n in range(width // STEP):
        copies[2 * n].wait()
        copies[2 * n + 1].wait()
        at = slice(n * STEP, (n + 1) * STEP)
        put_columns(
            pieces,
            n,
            dot_last(dgate[...], held_gate[at, :]) + dot_last(dupper[...], held_up[at, :]),
        )
    finish(message, pieces, out.shape[0], out)


def backward_rest(own, got, down_own, down_got, gate_w, up_w, groups):
    rows = own.shape[0]
    width, hidden = gate_w.shape
    shape = message_shape(groups, rows, width // LANES)
    return call(
        backward_kernel,
        struct(shape, BF16),
        [
            pltpu.VMEM((rows, hidden), BF16),
            pltpu.VMEM((rows, hidden), BF16),
            pltpu.VMEM((width // LANES, rows, LANES), F32),
            pltpu.VMEM(shape, F32),
            pltpu.VMEM(gate_w.shape, BF16),
            pltpu.VMEM(up_w.shape, BF16),
            pltpu.SemaphoreType.DMA((2, width // STEP)),
        ],
        (own, got, down_own, down_got, gate_w, up_w),
        4 * rows * width * hidden,
        in_hbm=(4, 5),
        name="backward_rest",
    )


def returned_rows(source, message, pieces, rows):
    widen(source, message, 0, source.shape[1])
    groups = message.shape[0]
    unfold(message, pieces, pieces.shape[1] // groups, 0, expert_groups(groups, pieces.shape[1]))
    join(pieces, rows)


def combine_forward_kernel(index, source, columns, value, out, square, message, pieces, rows):
    returned_rows(source, message, pieces, rows)
    picks, mixes = [], []
    for k in range(2):
        at = 2 * index + k
        picks.append(token_selector(columns[:, MARK + at : MARK + at + 1], rows.shape[0]))
        mixes.append(columns[:, MIX + at : MIX + at + 1])
    total = jnp.zeros((value.shape[0], 1), F32)
    for n in range(value.shape[1] // STEP):
        at = slice(n * STEP, (n + 1) * STEP)
        mixed = mixes[0] * dot(picks[0], rows[:, at]) + mixes[1] * dot(picks[1], rows[:, at])
        result = (value[:, at].astype(F32) + ROUTE_SCALE * mixed).astype(BF16)
        out[:, at] = result
        wide = result.astype(F32)
        total = total + jnp.sum(wide * wide, axis=1, keepdims=True)
    square[...] = total


def returned_scratch(source, rows, half):
    return [
        pltpu.VMEM(source.shape, F32),
        pltpu.VMEM((half // LANES, rows, LANES), F32),
        pltpu.VMEM((rows, half), BF16),
    ]


def combine_forward(index, source, columns, value):
    tokens, half = value.shape
    rows = source.shape[0] * 2 * SLOTS
    return call(
        functools.partial(combine_forward_kernel, index),
        (struct(value.shape, BF16), struct((tokens, 1), F32)),
        returned_scratch(source, rows, half),
        (source, columns, value),
        4 * tokens * rows * half,
        name="combine_forward",
    )


def combine_backward_kernel(
    index, source, columns, gain, saved, weighted, part, message, pieces, rows
):
    returned_rows(source, message, pieces, rows)
    chosen = sum(
        token_selector(columns[:, MARK + at : MARK + at + 1], rows.shape[0])
        for at in (2 * index, 2 * index + 1)
    )
    total = jnp.zeros((saved.shape[0], 1), F32)
    for n in range(saved.shape[1] // STEP):
        at = slice(n * STEP, (n + 1) * STEP)
        result = dot(chosen, rows[:, at]) * gain[:, at]
        weighted[:, at] = result
        total = total + jnp.sum(result * saved[:, at].astype(F32), axis=1, keepdims=True)
    part[...] = total


def combine_backward(index, source, columns, gain, saved):
    tokens, half = saved.shape
    rows = source.shape[0] * 2 * SLOTS
    return call(
        functools.partial(combine_backward_kernel, index),
        (struct(saved.shape, F32), struct((tokens, 1), F32)),
        returned_scratch(source, rows, half),
        (source, columns, gain, saved),
        4 * tokens * rows * half,
        name="combine_backward",
    )


def home_rows(source, message, pieces, rows, side):
    groups = [(2 * e + side, e * SLOTS) for e in range(message.shape[0] // 2)]
    unfold(message, pieces, SLOTS, 0, groups)
    join(pieces, rows)


def final_forward_kernel(index, source, columns, value, out, message, pieces, rows):
    widen(source, message, 0, source.shape[1])
    half = rows.shape[1]
    picks, mixes = [], []
    for k in range(2):
        at = 2 * index + k
        picks.append(token_selector(columns[:, MARK + at : MARK + at + 1], rows.shape[0]))
        mixes.append(columns[:, MIX + at : MIX + at + 1])
    for side in range(2):
        home_rows(source, message, pieces, rows, side)
        for n in range(half // STEP):
            low = n * STEP
            at = slice(low, low + STEP)
            to = slice(side * half + low, side * half + low + STEP)
            mixed = mixes[0] * dot(picks[0], rows[:, at]) + mixes[1] * dot(picks[1], rows[:, at])
            out[:, to] = (value[:, to].astype(F32) + ROUTE_SCALE * mixed).astype(BF16)


def final_forward(index, source, columns, value):
    tokens, width = value.shape
    rows = source.shape[0] // 2 * SLOTS
    return call(
        functools.partial(final_forward_kernel, index),
        struct(value.shape, BF16),
        returned_scratch(source, rows, width // 2),
        (source, columns, value),
        4 * tokens * rows * width,
        name="final_forward",
    )


def final_backward_kernel(
    index, source, columns, gain, saved, grads, out, message, pieces, rows, weighted
):
    widen(source, message, 0, source.shape[1])
    half = rows.shape[1]
    chosen = sum(
        token_selector(columns[:, MARK + at : MARK + at + 1], rows.shape[0])
        for at in (2 * index, 2 * index + 1)
    )
    total = jnp.zeros((saved.shape[0], 1), F32)
    for side in range(2):
        home_rows(source, message, pieces, rows, side)
        for n in range(half // STEP):
            low = n * STEP
            to = slice(side * half + low, side * half + low + STEP)
            result = dot(chosen, rows[:, low : low + STEP]) * gain[:, to]
            weighted[:, to] = result
            total = total + jnp.sum(result * saved[:, to].astype(F32), axis=1, keepdims=True)
    project = total / (2 * half)
    inverse = columns[:, 1:2]
    for n in range(2 * half // STEP):
        at = slice(n * STEP, (n + 1) * STEP)
        wide = saved[:, at].astype(F32)
        out[:, at] = (
            grads[:, at].astype(F32)
            + inverse * (weighted[:, at] - wide * inverse * inverse * project)
        ).astype(BF16)


def final_backward(index, source, columns, gain, saved, grads):
    tokens, width = saved.shape
    rows = source.shape[0] // 2 * SLOTS
    return call(
        functools.partial(final_backward_kernel, index),
        struct(saved.shape, BF16),
        [*returned_scratch(source, rows, width // 2), pltpu.VMEM((tokens, width), F32)],
        (source, columns, gain, saved, grads),
        4 * tokens * rows * width,
        name="final_backward",
    )


def swap_dp(value):
    return lax.ppermute(value, "dp", [(0, 1), (1, 0)])


def move_section(value, step, flip_dp=False):
    sections = lax.axis_size("section")
    halves = lax.axis_size("dp")
    route = []
    for s in range(sections):
        if 0 <= s + step < sections:
            for d in range(halves):
                to = 1 - d if flip_dp else d
                route.append((s * halves + d, (s + step) * halves + to))
    return lax.ppermute(value, ("section", "dp"), route)


def route(message, axes="expert"):
    return lax.all_to_all(message, axes, split_axis=0, concat_axis=0, tiled=True)


def after(value, *earlier):
    return lax.optimization_barrier((value, *earlier))[0]


def body(
    fwd_input,
    back_saved,
    back_grad,
    norm_gain,
    gate_weight,
    up_weight,
    down_weight,
    routes,
    slots,
    affinity,
):
    experts = lax.axis_size("expert")
    tokens = fwd_input.shape[1]
    width = fwd_input.shape[2]
    half = width // 2
    rows = experts * 2 * SLOTS
    side = lax.axis_index("dp")
    both = ("expert", "dp")
    gate_w, up_w, down_w = gate_weight[0, 0], up_weight[0, 0], down_weight[0, 0]
    gain = norm_gain
    gain_half = lax.dynamic_slice(gain, (0, side * half), (1, half))

    x0, s0, s1, g0 = fwd_input[0], back_saved[0, 0], back_saved[1, 0], back_grad[0]

    def inverse_of(value):
        wide = value.astype(F32)
        return lax.rsqrt(jnp.mean(wide * wide, axis=-1) + EPSILON)

    def in_order(own, other):
        return jnp.where(side == 0, own, other), jnp.where(side == 0, other, own)

    def flat(value):
        return jnp.transpose(value, (0, 2, 1)).reshape(8, tokens)

    chosen, held = routes[:, 0], slots[:, 0]
    mixing = affinity[:, 0] / jnp.sum(affinity[:, 0], axis=-1, keepdims=True)
    inverses = jnp.stack([inverse_of(s0), inverse_of(s1)])

    def scalars_of(marks):
        return jnp.concatenate([inverses, flat(marks.astype(F32)), flat(mixing)])

    local = scalars_of(chosen * SLOTS + held)
    own_scalars = scalars_of(chosen * (2 * SLOTS) + side * SLOTS + held)
    table = jnp.concatenate(in_order(own_scalars, swap_dp(own_scalars)), axis=1)
    local_columns = jnp.transpose(local)
    columns = jnp.transpose(table)

    def swap_halves(values):
        stacked = jnp.stack(values)
        own = lax.dynamic_slice_in_dim(stacked, side * half, half, axis=2)
        other = lax.dynamic_slice_in_dim(stacked, (1 - side) * half, half, axis=2)
        a, b = in_order(own, swap_dp(other))
        joined = jnp.concatenate([a, b], axis=1)
        return [joined[i] for i in range(len(values))]

    def full_features(value):
        mine, theirs = in_order(value[:tokens], value[tokens:])
        return jnp.concatenate(in_order(mine, swap_dp(theirs)), axis=1)

    first_sent = spread((0, 1), local, gain, (x0, s0), experts)
    first = route(first_sent, both)
    g0h, s1h = swap_halves([g0, s1])
    x0h, s0h = swap_halves([x0, s0])
    second_sent = place((("grads", 1), ("saved", 3)), table, columns, gain_half, (g0h, s1h), experts)
    second = route(after(second_sent, first))

    x0_sent, x0_own = partial((first, 0, 2), (gate_w, up_w), rows, False)
    out0 = forward_rest(x0_own, swap_dp(x0_sent), down_w, experts)
    s0_sent, s0_own = partial((after(first, x0_sent), 1, 2), (gate_w, up_w), rows, False)
    s0_got = swap_dp(s0_sent)
    out0_back = route(after(out0, second))

    g0_sent, g0_own = partial((second, 0, 2), (down_w,), rows, True)
    g0_got = swap_dp(g0_sent)
    s1_sent, s1_own = partial((after(second, g0_sent), 1, 2), (gate_w, up_w), rows, False)
    s1_got = swap_dp(s1_sent)
    dexp0 = backward_rest(s0_own, s0_got, g0_own, g0_got, gate_w, up_w, experts)
    dexp0_back = route(after(dexp0, out0_back))

    first_out, square = combine_forward(0, out0_back, columns, x0h)
    x2h = move_section(first_out, 1)
    square_own = move_section(square, 1)
    square_other = move_section(square, 1, flip_dp=True)
    x2_sent = place(
        (("moved", 2),), table, columns, gain_half, (x2h, square_own, square_other), experts
    )
    x2_rows = route(after(x2_sent, dexp0_back))

    weighted, part = combine_backward(1, dexp0_back, columns, gain_half, s0h)
    project = (part + swap_dp(part)) / width
    inverse = columns[:, 0:1]
    wide = s0h.astype(F32)
    first_back = (
        g0h.astype(F32) + inverse * (weighted - wide * inverse * inverse * project)
    ).astype(BF16)
    g3h = move_section(first_back, -1)
    g3_sent = place((("grads", 3),), table, columns, gain_half, (g3h,), experts)
    g3_rows = route(after(g3_sent, x2_rows))

    x2_part, x2_own = partial((x2_rows, 0, 1), (gate_w, up_w), rows, False)
    out2 = forward_rest(x2_own, swap_dp(x2_part), down_w, 2 * experts)
    out2_back = route(after(out2, g3_rows), both)
    g3_part, g3_own = partial((g3_rows, 0, 1), (down_w,), rows, True)
    dexp1 = backward_rest(s1_own, s1_got, g3_own, swap_dp(g3_part), gate_w, up_w, 2 * experts)
    dexp1_back = route(after(dexp1, out2_back), both)

    x2 = full_features(x2h)
    g3 = full_features(g3h)
    final_out = final_forward(2, out2_back, local_columns, x2)
    final_back = final_backward(3, dexp1_back, local_columns, gain, s1, g3)
    return (final_out[None], final_back[None])


def solution(mesh):
    placed = (
        P("section", ("expert", "dp"), None),
        P(None, "section", ("expert", "dp"), None),
        P("section", ("expert", "dp"), None),
        P("section", None),
        P("section", "expert", "dp", None),
        P("section", "expert", "dp", None),
        P("section", "expert", None, "dp"),
        P(None, "section", ("expert", "dp"), None),
        P(None, "section", ("expert", "dp"), None),
        P(None, "section", ("expert", "dp"), None),
    )
    return jax.shard_map(
        body,
        mesh=mesh,
        in_specs=placed,
        out_specs=(P("section", ("expert", "dp"), None), P("section", ("expert", "dp"), None)),
        check_vma=False,
    )
```

```python
import functools

import jax
import jax.numpy as jnp
from jax import lax
from jax.experimental import pallas as pl
from jax.experimental.pallas import tpu as pltpu
from jax.sharding import PartitionSpec as P

ROUTE_SCALE = 2.5
EPSILON = 1e-06
BF16 = jnp.bfloat16
F32 = jnp.float32
SLOTS = 7
LANES = 128
STEP = 256
MARK = 2
MIX = 10


def ceil8(count):
    return -(-count // 8) * 8


def call(kernel, out_shape, scratch, operands, flops, in_hbm=(), name=None):
    specs = [
        pl.BlockSpec(memory_space=pltpu.HBM if i in in_hbm else pltpu.VMEM)
        for i in range(len(operands))
    ]
    moved = sum(x.size * x.dtype.itemsize for x in operands)
    return pl.pallas_call(
        kernel,
        out_shape=out_shape,
        in_specs=specs,
        out_specs=jax.tree.map(lambda _: pl.BlockSpec(memory_space=pltpu.VMEM), out_shape),
        scratch_shapes=scratch,
        compiler_params=pltpu.CompilerParams(vmem_limit_bytes=40 * 1024 * 1024),
        cost_estimate=pl.CostEstimate(flops=flops, bytes_accessed=moved, transcendentals=0),
        name=name,
    )(*operands)


def struct(shape, dtype):
    return jax.ShapeDtypeStruct(shape, dtype)


def dot(left, right):
    return jnp.dot(left, right, preferred_element_type=F32)


def dot_last(left, right):
    return lax.dot_general(left, right, (((1,), (1,)), ((), ())), preferred_element_type=F32)


def put_columns(pieces, step, value):
    for j in range(STEP // LANES):
        pieces[step * (STEP // LANES) + j] = value[:, j * LANES : (j + 1) * LANES]


def fold(pieces, message, count, base, groups):
    for group, first in groups:
        for c in range(pieces.shape[0]):
            message[group, base + c * count : base + (c + 1) * count, :] = pieces[
                c, first : first + count, :
            ]


def unfold(message, pieces, count, base, groups):
    for group, first in groups:
        for c in range(pieces.shape[0]):
            pieces[c, first : first + count, :] = message[
                group, base + c * count : base + (c + 1) * count, :
            ]


def clear_padding(message, count, base, size):
    used = base + count * size
    if ceil8(used) > used:
        shape = (message.shape[0], ceil8(used) - used, LANES)
        message[:, used : ceil8(used), :] = jnp.zeros(shape, F32)


def join(pieces, rows):
    for c in range(pieces.shape[0]):
        rows[:, c * LANES : (c + 1) * LANES] = pieces[c].astype(BF16)


def widen(source, message, low, high):
    for g in range(message.shape[0]):
        message[g] = source[g, low:high, :].astype(F32)


def narrow(message, out):
    for g in range(message.shape[0]):
        out[g] = message[g].astype(BF16)


def row_selector(marks, rows):
    places = lax.broadcasted_iota(jnp.int32, (rows, marks.shape[1]), 0).astype(F32)
    return jnp.where(places == marks, 1.0, 0.0).astype(BF16)


def token_selector(marks, rows):
    places = lax.broadcasted_iota(jnp.int32, (marks.shape[0], rows), 1).astype(F32)
    return jnp.where(places == marks, 1.0, 0.0).astype(BF16)


def spread_kernel(indices, scalars, gain, *refs):
    count = len(indices)
    values, (out, pieces, message, normed) = refs[:count], refs[count:]
    half = pieces.shape[0] * LANES
    rows = pieces.shape[1]
    size = ceil8(SLOTS * pieces.shape[0])
    for t, (index, value) in enumerate(zip(indices, values)):
        wide = value[...].astype(F32)
        inverse = lax.rsqrt(jnp.mean(wide * wide, axis=-1, keepdims=True) + EPSILON)
        normed[...] = (wide * inverse * gain[...]).astype(BF16)
        chosen = sum(
            row_selector(scalars[MARK + 2 * index + k : MARK + 2 * index + k + 1, :], rows)
            for k in range(2)
        )
        for h in range(2):
            for n in range(half // STEP):
                low = h * half + n * STEP
                put_columns(pieces, n, dot(chosen, normed[:, low : low + STEP]))
            fold(
                pieces,
                message,
                SLOTS,
                t * size,
                [(2 * e + h, e * SLOTS) for e in range(rows // SLOTS)],
            )
        clear_padding(message, SLOTS, t * size, pieces.shape[0])
    narrow(message, out)


def spread(indices, scalars, gain, values, experts):
    tokens, width = values[0].shape
    chunks = width // 2 // LANES
    rows = experts * SLOTS
    shape = (2 * experts, len(values) * ceil8(SLOTS * chunks), LANES)
    return call(
        functools.partial(spread_kernel, indices),
        struct(shape, BF16),
        [
            pltpu.VMEM((chunks, rows, LANES), F32),
            pltpu.VMEM(shape, F32),
            pltpu.VMEM((tokens, width), BF16),
        ],
        (scalars, gain, *values),
        2 * len(values) * rows * tokens * width * 4,
        name="spread",
    )


def place_kernel(parts, rows, table, columns, gain, *refs):
    *inputs, out, pieces, message, ready = refs
    chunks = pieces.shape[0]
    half = chunks * LANES
    count = 2 * SLOTS
    size = ceil8(count * chunks)
    inputs = iter(inputs)
    for t, (kind, index) in enumerate(parts):
        value = next(inputs)[...].astype(F32)
        tokens = value.shape[0]
        pick = [
            row_selector(table[MARK + 2 * index + k : MARK + 2 * index + k + 1, :], rows)
            for k in range(2)
        ]
        if kind == "grads":
            for k in range(2):
                mix = columns[:, MIX + 2 * index + k : MIX + 2 * index + k + 1]
                ready[k * tokens : (k + 1) * tokens, :] = (ROUTE_SCALE * mix * value).astype(BF16)
            chosen = jnp.concatenate(pick, axis=1)
        else:
            if kind == "saved":
                inverse = columns[:, 1:2]
            else:
                squares = next(inputs)[...] + next(inputs)[...]
                inverse = lax.rsqrt(squares / (2 * half) + EPSILON)
            ready[0:tokens, :] = (value * inverse * gain[...]).astype(BF16)
            chosen = pick[0] + pick[1]
        depth = chosen.shape[1]
        for n in range(half // STEP):
            put_columns(pieces, n, dot(chosen, ready[0:depth, n * STEP : (n + 1) * STEP]))
        fold(
            pieces, message, count, t * size, [(e, e * count) for e in range(rows // count)]
        )
        clear_padding(message, count, t * size, chunks)
    narrow(message, out)


def place(parts, table, columns, gain, inputs, experts):
    tokens, half = inputs[0].shape
    chunks = half // LANES
    rows = experts * 2 * SLOTS
    shape = (experts, len(parts) * ceil8(2 * SLOTS * chunks), LANES)
    return call(
        functools.partial(place_kernel, parts, rows),
        struct(shape, BF16),
        [
            pltpu.VMEM((chunks, rows, LANES), F32),
            pltpu.VMEM(shape, F32),
            pltpu.VMEM((2 * tokens, half), BF16),
        ],
        (table, columns, gain, *inputs),
        2 * len(parts) * rows * 2 * tokens * half * 2,
        name="place",
    )


def message_rows(message):
    array, part, parts = message
    size = array.shape[1] // parts
    low = part * size // 16 * 16
    high = min(array.shape[1], -(-(part + 1) * size // 16) * 16)
    return low, high, part * size - low


def expert_groups(groups, rows):
    return [(g, g * (rows // groups)) for g in range(groups)]


def partial_kernel(bounds, count, last, source, *refs):
    parts = len(bounds)
    weights, refs = refs[:count], refs[count:]
    sent, own = refs[: 2 * parts : 2], refs[1 : 2 * parts : 2]
    message, pieces, *refs = refs[2 * parts :]
    rows, held, sems = refs[:parts], refs[parts:-1], refs[-1]
    hidden = sent[0].shape[1] // count
    copies = []
    for n in range(hidden // STEP):
        for w in range(count):
            at = pl.ds(n * STEP, STEP)
            where = (at, slice(None)) if last else (slice(None), at)
            copies.append(
                pltpu.make_async_copy(weights[w].at[where], held[w].at[where], sems.at[w, n])
            )
            copies[-1].start()
    groups = message.shape[0]
    total = rows[0].shape[0]
    for t, (low, high, base) in enumerate(bounds):
        widen(source, message, low, high)
        unfold(message, pieces, total // groups, base, expert_groups(groups, total))
        join(pieces, rows[t])
    copies = iter(copies)
    for n in range(hidden // STEP):
        for w in range(count):
            next(copies).wait()
            at = slice(n * STEP, (n + 1) * STEP)
            place_at = slice(w * hidden + n * STEP, w * hidden + (n + 1) * STEP)
            for t in range(parts):
                if last:
                    result = dot_last(rows[t][...], held[w][at, :])
                else:
                    result = dot(rows[t][...], held[w][:, at])
                own[t][:, place_at] = result
                sent[t][:, place_at] = result.astype(BF16)


def partial(source, numbers, of, weights, rows, last):
    bounds = [message_rows((source, number, of)) for number in numbers]
    width, hidden = weights[0].shape[::-1] if last else weights[0].shape
    shape = (rows, len(weights) * hidden)
    return call(
        functools.partial(partial_kernel, bounds, len(weights), last),
        (struct(shape, BF16), struct(shape, F32)) * len(numbers),
        [
            pltpu.VMEM((source.shape[0], bounds[0][1] - bounds[0][0], LANES), F32),
            pltpu.VMEM((width // LANES, rows, LANES), F32),
            *[pltpu.VMEM((rows, width), BF16) for _ in numbers],
            *[pltpu.VMEM(w.shape, BF16) for w in weights],
            pltpu.SemaphoreType.DMA((len(weights), hidden // STEP)),
        ],
        (source, *weights),
        2 * rows * width * shape[1] * len(numbers),
        in_hbm=range(1, 1 + len(weights)),
        name="partial",
    )


def finish(message, pieces, groups, out):
    total = pieces.shape[1]
    count = total // groups
    fold(pieces, message, count, 0, expert_groups(groups, total))
    clear_padding(message, count, 0, pieces.shape[0])
    narrow(message, out)


def forward_kernel(own, got, weight, out, active, pieces, message, held, sems):
    width = held.shape[1]
    hidden = held.shape[0]
    copies = []
    for n in range(width // STEP):
        at = (slice(None), pl.ds(n * STEP, STEP))
        copies.append(pltpu.make_async_copy(weight.at[at], held.at[at], sems.at[n]))
        copies[-1].start()
    for n in range(hidden // STEP):
        a = slice(n * STEP, (n + 1) * STEP)
        b = slice(hidden + n * STEP, hidden + (n + 1) * STEP)
        gate = own[:, a] + got[:, a].astype(F32)
        upper = own[:, b] + got[:, b].astype(F32)
        active[:, a] = (gate * jax.nn.sigmoid(gate) * upper).astype(BF16)
    for n in range(width // STEP):
        copies[n].wait()
        put_columns(pieces, n, dot(active[...], held[:, n * STEP : (n + 1) * STEP]))
    finish(message, pieces, out.shape[0], out)


def message_shape(groups, rows, chunks):
    return (groups, ceil8(rows // groups * chunks), LANES)


def forward_rest(own, got, weight, groups):
    rows = own.shape[0]
    hidden, width = weight.shape
    shape = message_shape(groups, rows, width // LANES)
    return call(
        forward_kernel,
        struct(shape, BF16),
        [
            pltpu.VMEM((rows, hidden), BF16),
            pltpu.VMEM((width // LANES, rows, LANES), F32),
            pltpu.VMEM(shape, F32),
            pltpu.VMEM(weight.shape, BF16),
            pltpu.SemaphoreType.DMA((width // STEP,)),
        ],
        (own, got, weight),
        2 * rows * width * hidden,
        in_hbm=(2,),
        name="forward_rest",
    )


def backward_kernel(
    own, got, down_own, down_got, gate_w, up_w, out, dgate, dupper, pieces, message, held_gate, held_up, sems
):
    width, hidden = held_gate.shape
    copies = []
    for n in range(width // STEP):
        at = pl.ds(n * STEP, STEP)
        for w, (weight, held) in enumerate(((gate_w, held_gate), (up_w, held_up))):
            copies.append(pltpu.make_async_copy(weight.at[at], held.at[at], sems.at[w, n]))
            copies[-1].start()
    for n in range(hidden // STEP):
        a = slice(n * STEP, (n + 1) * STEP)
        b = slice(hidden + n * STEP, hidden + (n + 1) * STEP)
        gate = own[:, a] + got[:, a].astype(F32)
        upper = own[:, b] + got[:, b].astype(F32)
        dactive = down_own[:, a] + down_got[:, a].astype(F32)
        sigma = jax.nn.sigmoid(gate)
        dgate[:, a] = (dactive * upper * sigma * (1.0 + gate * (1.0 - sigma))).astype(BF16)
        dupper[:, a] = (dactive * gate * sigma).astype(BF16)
    for n in range(width // STEP):
        copies[2 * n].wait()
        copies[2 * n + 1].wait()
        at = slice(n * STEP, (n + 1) * STEP)
        put_columns(
            pieces,
            n,
            dot_last(dgate[...], held_gate[at, :]) + dot_last(dupper[...], held_up[at, :]),
        )
    finish(message, pieces, out.shape[0], out)


def backward_rest(own, got, down_own, down_got, gate_w, up_w, groups):
    rows = own.shape[0]
    width, hidden = gate_w.shape
    shape = message_shape(groups, rows, width // LANES)
    return call(
        backward_kernel,
        struct(shape, BF16),
        [
            pltpu.VMEM((rows, hidden), BF16),
            pltpu.VMEM((rows, hidden), BF16),
            pltpu.VMEM((width // LANES, rows, LANES), F32),
            pltpu.VMEM(shape, F32),
            pltpu.VMEM(gate_w.shape, BF16),
            pltpu.VMEM(up_w.shape, BF16),
            pltpu.SemaphoreType.DMA((2, width // STEP)),
        ],
        (own, got, down_own, down_got, gate_w, up_w),
        4 * rows * width * hidden,
        in_hbm=(4, 5),
        name="backward_rest",
    )


def returned_rows(source, message, pieces, rows):
    widen(source, message, 0, source.shape[1])
    groups = message.shape[0]
    unfold(message, pieces, pieces.shape[1] // groups, 0, expert_groups(groups, pieces.shape[1]))
    join(pieces, rows)


def combine_forward_kernel(index, source, columns, value, out, square, message, pieces, rows):
    returned_rows(source, message, pieces, rows)
    picks, mixes = [], []
    for k in range(2):
        at = 2 * index + k
        picks.append(token_selector(columns[:, MARK + at : MARK + at + 1], rows.shape[0]))
        mixes.append(columns[:, MIX + at : MIX + at + 1])
    total = jnp.zeros((value.shape[0], 1), F32)
    for n in range(value.shape[1] // STEP):
        at = slice(n * STEP, (n + 1) * STEP)
        mixed = mixes[0] * dot(picks[0], rows[:, at]) + mixes[1] * dot(picks[1], rows[:, at])
        result = (value[:, at].astype(F32) + ROUTE_SCALE * mixed).astype(BF16)
        out[:, at] = result
        wide = result.astype(F32)
        total = total + jnp.sum(wide * wide, axis=1, keepdims=True)
    square[...] = total


def returned_scratch(source, rows, half):
    return [
        pltpu.VMEM(source.shape, F32),
        pltpu.VMEM((half // LANES, rows, LANES), F32),
        pltpu.VMEM((rows, half), BF16),
    ]


def combine_forward(index, source, columns, value):
    tokens, half = value.shape
    rows = source.shape[0] * 2 * SLOTS
    return call(
        functools.partial(combine_forward_kernel, index),
        (struct(value.shape, BF16), struct((tokens, 1), F32)),
        returned_scratch(source, rows, half),
        (source, columns, value),
        4 * tokens * rows * half,
        name="combine_forward",
    )


def combine_backward_kernel(
    index, source, columns, gain, saved, weighted, part, message, pieces, rows
):
    returned_rows(source, message, pieces, rows)
    chosen = sum(
        token_selector(columns[:, MARK + at : MARK + at + 1], rows.shape[0])
        for at in (2 * index, 2 * index + 1)
    )
    total = jnp.zeros((saved.shape[0], 1), F32)
    for n in range(saved.shape[1] // STEP):
        at = slice(n * STEP, (n + 1) * STEP)
        result = dot(chosen, rows[:, at]) * gain[:, at]
        weighted[:, at] = result
        total = total + jnp.sum(result * saved[:, at].astype(F32), axis=1, keepdims=True)
    part[...] = total


def combine_backward(index, source, columns, gain, saved):
    tokens, half = saved.shape
    rows = source.shape[0] * 2 * SLOTS
    return call(
        functools.partial(combine_backward_kernel, index),
        (struct(saved.shape, F32), struct((tokens, 1), F32)),
        returned_scratch(source, rows, half),
        (source, columns, gain, saved),
        4 * tokens * rows * half,
        name="combine_backward",
    )


def home_rows(source, message, pieces, rows, side):
    groups = [(2 * e + side, e * SLOTS) for e in range(message.shape[0] // 2)]
    unfold(message, pieces, SLOTS, 0, groups)
    join(pieces, rows)


def final_forward_kernel(index, source, columns, value, out, message, pieces, rows):
    widen(source, message, 0, source.shape[1])
    half = rows.shape[1]
    picks, mixes = [], []
    for k in range(2):
        at = 2 * index + k
        picks.append(token_selector(columns[:, MARK + at : MARK + at + 1], rows.shape[0]))
        mixes.append(columns[:, MIX + at : MIX + at + 1])
    for side in range(2):
        home_rows(source, message, pieces, rows, side)
        for n in range(half // STEP):
            low = n * STEP
            at = slice(low, low + STEP)
            to = slice(side * half + low, side * half + low + STEP)
            mixed = mixes[0] * dot(picks[0], rows[:, at]) + mixes[1] * dot(picks[1], rows[:, at])
            out[:, to] = (value[:, to].astype(F32) + ROUTE_SCALE * mixed).astype(BF16)


def final_forward(index, source, columns, value):
    tokens, width = value.shape
    rows = source.shape[0] // 2 * SLOTS
    return call(
        functools.partial(final_forward_kernel, index),
        struct(value.shape, BF16),
        returned_scratch(source, rows, width // 2),
        (source, columns, value),
        4 * tokens * rows * width,
        name="final_forward",
    )


def final_backward_kernel(
    index, source, columns, gain, saved, grads, out, message, pieces, rows, weighted
):
    widen(source, message, 0, source.shape[1])
    half = rows.shape[1]
    chosen = sum(
        token_selector(columns[:, MARK + at : MARK + at + 1], rows.shape[0])
        for at in (2 * index, 2 * index + 1)
    )
    total = jnp.zeros((saved.shape[0], 1), F32)
    for side in range(2):
        home_rows(source, message, pieces, rows, side)
        for n in range(half // STEP):
            low = n * STEP
            to = slice(side * half + low, side * half + low + STEP)
            result = dot(chosen, rows[:, low : low + STEP]) * gain[:, to]
            weighted[:, to] = result
            total = total + jnp.sum(result * saved[:, to].astype(F32), axis=1, keepdims=True)
    project = total / (2 * half)
    inverse = columns[:, 1:2]
    for n in range(2 * half // STEP):
        at = slice(n * STEP, (n + 1) * STEP)
        wide = saved[:, at].astype(F32)
        out[:, at] = (
            grads[:, at].astype(F32)
            + inverse * (weighted[:, at] - wide * inverse * inverse * project)
        ).astype(BF16)


def final_backward(index, source, columns, gain, saved, grads):
    tokens, width = saved.shape
    rows = source.shape[0] // 2 * SLOTS
    return call(
        functools.partial(final_backward_kernel, index),
        struct(saved.shape, BF16),
        [*returned_scratch(source, rows, width // 2), pltpu.VMEM((tokens, width), F32)],
        (source, columns, gain, saved, grads),
        4 * tokens * rows * width,
        name="final_backward",
    )


def swap_dp(value):
    return lax.ppermute(value, "dp", [(0, 1), (1, 0)])


def move_section(value, step, flip_dp=False):
    sections = lax.axis_size("section")
    halves = lax.axis_size("dp")
    route = []
    for s in range(sections):
        if 0 <= s + step < sections:
            for d in range(halves):
                to = 1 - d if flip_dp else d
                route.append((s * halves + d, (s + step) * halves + to))
    return lax.ppermute(value, ("section", "dp"), route)


def route(message, axes="expert"):
    return lax.all_to_all(message, axes, split_axis=0, concat_axis=0, tiled=True)


def after(value, *earlier):
    return lax.optimization_barrier((value, *earlier))[0]


def body(
    fwd_input,
    back_saved,
    back_grad,
    norm_gain,
    gate_weight,
    up_weight,
    down_weight,
    routes,
    slots,
    affinity,
):
    experts = lax.axis_size("expert")
    tokens = fwd_input.shape[1]
    width = fwd_input.shape[2]
    half = width // 2
    rows = experts * 2 * SLOTS
    side = lax.axis_index("dp")
    both = ("expert", "dp")
    gate_w, up_w, down_w = gate_weight[0, 0], up_weight[0, 0], down_weight[0, 0]
    gain = norm_gain
    gain_half = lax.dynamic_slice(gain, (0, side * half), (1, half))

    x0, s0, s1, g0 = fwd_input[0], back_saved[0, 0], back_saved[1, 0], back_grad[0]

    def inverse_of(value):
        wide = value.astype(F32)
        return lax.rsqrt(jnp.mean(wide * wide, axis=-1) + EPSILON)

    def in_order(own, other):
        return jnp.where(side == 0, own, other), jnp.where(side == 0, other, own)

    def flat(value):
        return jnp.transpose(value, (0, 2, 1)).reshape(8, tokens)

    chosen, held = routes[:, 0], slots[:, 0]
    mixing = affinity[:, 0] / jnp.sum(affinity[:, 0], axis=-1, keepdims=True)
    inverses = jnp.stack([inverse_of(s0), inverse_of(s1)])

    def scalars_of(marks):
        return jnp.concatenate([inverses, flat(marks.astype(F32)), flat(mixing)])

    local = scalars_of(chosen * SLOTS + held)
    own_scalars = scalars_of(chosen * (2 * SLOTS) + side * SLOTS + held)
    table = jnp.concatenate(in_order(own_scalars, swap_dp(own_scalars)), axis=1)
    local_columns = jnp.transpose(local)
    columns = jnp.transpose(table)

    def swap_halves(values):
        stacked = jnp.stack(values)
        own = lax.dynamic_slice_in_dim(stacked, side * half, half, axis=2)
        other = lax.dynamic_slice_in_dim(stacked, (1 - side) * half, half, axis=2)
        a, b = in_order(own, swap_dp(other))
        joined = jnp.concatenate([a, b], axis=1)
        return [joined[i] for i in range(len(values))]

    def full_features(value):
        mine, theirs = in_order(value[:tokens], value[tokens:])
        return jnp.concatenate(in_order(mine, swap_dp(theirs)), axis=1)

    first_sent = spread((0, 1), local, gain, (x0, s0), experts)
    first = route(first_sent, both)
    g0h, s1h = swap_halves([g0, s1])
    x0h, s0h = swap_halves([x0, s0])
    second_sent = place((("grads", 1), ("saved", 3)), table, columns, gain_half, (g0h, s1h), experts)
    second = route(after(second_sent, first))

    x0_sent, x0_own, s0_sent, s0_own = partial(
        first, (0, 1), 2, (gate_w, up_w), rows, False
    )
    x0_got = swap_dp(x0_sent)
    out0 = forward_rest(x0_own, x0_got, down_w, experts)
    s0_got = swap_dp(after(s0_sent, x0_got))
    g0_sent, g0_own = partial(second, (0,), 2, (down_w,), rows, True)
    g0_got = swap_dp(g0_sent)
    out0_back = route(after(out0, second, g0_sent))

    dexp0 = backward_rest(s0_own, s0_got, g0_own, g0_got, gate_w, up_w, experts)
    dexp0_back = route(after(dexp0, out0_back))
    s1_sent, s1_own = partial(after(second, dexp0), (1,), 2, (gate_w, up_w), rows, False)
    s1_got = swap_dp(s1_sent)

    first_out, square = combine_forward(0, out0_back, columns, x0h)
    x2h = move_section(first_out, 1)
    square_own = move_section(square, 1)
    square_other = move_section(square, 1, flip_dp=True)
    x2_sent = place(
        (("moved", 2),), table, columns, gain_half, (after(x2h, s1_sent), square_own, square_other), experts
    )
    x2_rows = route(after(x2_sent, dexp0_back))

    weighted, part = combine_backward(1, dexp0_back, columns, gain_half, s0h)
    project = (part + swap_dp(part)) / width
    inverse = columns[:, 0:1]
    wide = s0h.astype(F32)
    first_back = (
        g0h.astype(F32) + inverse * (weighted - wide * inverse * inverse * project)
    ).astype(BF16)
    g3h = move_section(first_back, -1)
    g3_sent = place((("grads", 3),), table, columns, gain_half, (g3h,), experts)
    x2_part, x2_own = partial(x2_rows, (0,), 1, (gate_w, up_w), rows, False)
    g3_rows = route(after(g3_sent, x2_part))

    out2 = forward_rest(x2_own, swap_dp(x2_part), down_w, 2 * experts)
    out2_back = route(after(out2, g3_rows), both)
    g3_part, g3_own = partial(g3_rows, (0,), 1, (down_w,), rows, True)
    dexp1 = backward_rest(s1_own, s1_got, g3_own, swap_dp(g3_part), gate_w, up_w, 2 * experts)
    dexp1_back = route(after(dexp1, out2_back), both)

    x2 = full_features(x2h)
    g3 = full_features(g3h)
    final_out = final_forward(2, out2_back, local_columns, x2)
    final_back = final_backward(3, dexp1_back, local_columns, gain, s1, g3)
    return (final_out[None], final_back[None])


def solution(mesh):
    placed = (
        P("section", ("expert", "dp"), None),
        P(None, "section", ("expert", "dp"), None),
        P("section", ("expert", "dp"), None),
        P("section", None),
        P("section", "expert", "dp", None),
        P("section", "expert", "dp", None),
        P("section", "expert", None, "dp"),
        P(None, "section", ("expert", "dp"), None),
        P(None, "section", ("expert", "dp"), None),
        P(None, "section", ("expert", "dp"), None),
    )
    return jax.shard_map(
        body,
        mesh=mesh,
        in_specs=placed,
        out_specs=(P("section", ("expert", "dp"), None), P("section", ("expert", "dp"), None)),
        check_vma=False,
    )
```

```python
import functools

import jax
import jax.numpy as jnp
from jax import lax
from jax.experimental import pallas as pl
from jax.experimental.pallas import tpu as pltpu
from jax.sharding import PartitionSpec as P

ROUTE_SCALE = 2.5
EPSILON = 1e-06
BF16 = jnp.bfloat16
F32 = jnp.float32
SLOTS = 7
LANES = 128
STEP = 256
FIRST_SAVED, SECOND_SAVED, TOKENS = 0, 1, 2
MARK = 3
MIX = 11


def ceil8(count):
    return -(-count // 8) * 8


def call(kernel, out_shape, scratch, operands, in_hbm=(), name=None):
    specs = [
        pl.BlockSpec(memory_space=pltpu.HBM if i in in_hbm else pltpu.VMEM)
        for i in range(len(operands))
    ]
    return pl.pallas_call(
        kernel,
        out_shape=out_shape,
        in_specs=specs,
        out_specs=jax.tree.map(lambda _: pl.BlockSpec(memory_space=pltpu.VMEM), out_shape),
        scratch_shapes=scratch,
        compiler_params=pltpu.CompilerParams(vmem_limit_bytes=60 * 1024 * 1024),
        cost_estimate=pl.CostEstimate(flops=1024, bytes_accessed=1024, transcendentals=0),
        name=name,
    )(*operands)


def struct(shape, dtype):
    return jax.ShapeDtypeStruct(shape, dtype)


def dot(left, right):
    return jnp.dot(left, right, preferred_element_type=F32)


def dot_last(left, right):
    return lax.dot_general(left, right, (((1,), (1,)), ((), ())), preferred_element_type=F32)


def put_columns(pieces, step, value):
    for j in range(STEP // LANES):
        pieces[step * (STEP // LANES) + j] = value[:, j * LANES : (j + 1) * LANES]


def fold(pieces, message, count, base, groups):
    for group, first in groups:
        for c in range(pieces.shape[0]):
            message[group, base + c * count : base + (c + 1) * count, :] = pieces[
                c, first : first + count, :
            ]


def unfold(message, pieces, count, base, groups):
    for group, first in groups:
        for c in range(pieces.shape[0]):
            pieces[c, first : first + count, :] = message[
                group, base + c * count : base + (c + 1) * count, :
            ]


def clear_padding(message, count, base, size):
    used = base + count * size
    if ceil8(used) > used:
        shape = (message.shape[0], ceil8(used) - used, LANES)
        message[:, used : ceil8(used), :] = jnp.zeros(shape, F32)


def join(pieces, rows):
    for c in range(pieces.shape[0]):
        rows[:, c * LANES : (c + 1) * LANES] = pieces[c].astype(BF16)


def widen(source, message, low, high):
    for g in range(message.shape[0]):
        message[g] = source[g, low:high, :].astype(F32)


def narrow(message, out):
    for g in range(message.shape[0]):
        out[g] = message[g].astype(BF16)


def row_selector(marks, rows):
    places = lax.broadcasted_iota(jnp.int32, (rows, marks.shape[1]), 0).astype(F32)
    return jnp.where(places == marks, 1.0, 0.0).astype(BF16)


def token_selector(marks, rows):
    places = lax.broadcasted_iota(jnp.int32, (marks.shape[0], rows), 1).astype(F32)
    return jnp.where(places == marks, 1.0, 0.0).astype(BF16)


def spread_kernel(parts, scalars, columns, gain, *refs):
    count = len(parts)
    values, (out, pieces, message, ready) = refs[:count], refs[count:]
    half = pieces.shape[0] * LANES
    rows = pieces.shape[1]
    size = ceil8(SLOTS * pieces.shape[0])
    for t, ((kind, index), value) in enumerate(zip(parts, values)):
        wide = value[...].astype(F32)
        tokens = wide.shape[0]
        at = MARK + 2 * index
        pick = [row_selector(scalars[at + k : at + k + 1, :], rows) for k in range(2)]
        if kind == "grads":
            chosen = jnp.concatenate(pick, axis=1)
            at = MIX + 2 * index
            for k in range(2):
                mix = columns[:, at + k : at + k + 1]
                ready[k * tokens : (k + 1) * tokens, :] = (ROUTE_SCALE * mix * wide).astype(BF16)
        else:
            chosen = pick[0] + pick[1]
            inverse = lax.rsqrt(jnp.mean(wide * wide, axis=-1, keepdims=True) + EPSILON)
            ready[0:tokens, :] = (wide * inverse * gain[...]).astype(BF16)
        depth = chosen.shape[1]
        for h in range(2):
            for n in range(half // STEP):
                low = h * half + n * STEP
                put_columns(pieces, n, dot(chosen, ready[0:depth, low : low + STEP]))
            fold(
                pieces,
                message,
                SLOTS,
                t * size,
                [(2 * e + h, e * SLOTS) for e in range(rows // SLOTS)],
            )
        clear_padding(message, SLOTS, t * size, pieces.shape[0])
    narrow(message, out)


def spread(parts, scalars, columns, gain, values, experts):
    tokens, width = values[0].shape
    chunks = width // 2 // LANES
    rows = experts * SLOTS
    shape = (2 * experts, len(values) * ceil8(SLOTS * chunks), LANES)
    return call(
        functools.partial(spread_kernel, parts),
        struct(shape, BF16),
        [
            pltpu.VMEM((chunks, rows, LANES), F32),
            pltpu.VMEM(shape, F32),
            pltpu.VMEM((2 * tokens, width), BF16),
        ],
        (scalars, columns, gain, *values),
        name="spread",
    )


def place_kernel(parts, rows, table, columns, gain, *refs):
    *inputs, out, pieces, message, ready = refs
    chunks = pieces.shape[0]
    half = chunks * LANES
    count = 2 * SLOTS
    size = ceil8(count * chunks)
    inputs = iter(inputs)
    for t, (kind, index, inverse_row) in enumerate(parts):
        value = next(inputs)[...].astype(F32)
        tokens = value.shape[0]
        pick = [
            row_selector(table[MARK + 2 * index + k : MARK + 2 * index + k + 1, :], rows)
            for k in range(2)
        ]
        if kind == "grads":
            for k in range(2):
                mix = columns[:, MIX + 2 * index + k : MIX + 2 * index + k + 1]
                ready[k * tokens : (k + 1) * tokens, :] = (ROUTE_SCALE * mix * value).astype(BF16)
            chosen = jnp.concatenate(pick, axis=1)
        else:
            if kind == "normed":
                inverse = columns[:, inverse_row : inverse_row + 1]
            else:
                squares = next(inputs)[...] + next(inputs)[...]
                inverse = lax.rsqrt(squares / (2 * half) + EPSILON)
            ready[0:tokens, :] = (value * inverse * gain[...]).astype(BF16)
            chosen = pick[0] + pick[1]
        depth = chosen.shape[1]
        for n in range(half // STEP):
            put_columns(pieces, n, dot(chosen, ready[0:depth, n * STEP : (n + 1) * STEP]))
        fold(
            pieces, message, count, t * size, [(e, e * count) for e in range(rows // count)]
        )
        clear_padding(message, count, t * size, chunks)
    narrow(message, out)


def place(parts, table, columns, gain, inputs, experts):
    tokens, half = inputs[0].shape
    chunks = half // LANES
    rows = experts * 2 * SLOTS
    shape = (experts, len(parts) * ceil8(2 * SLOTS * chunks), LANES)
    return call(
        functools.partial(place_kernel, parts, rows),
        struct(shape, BF16),
        [
            pltpu.VMEM((chunks, rows, LANES), F32),
            pltpu.VMEM(shape, F32),
            pltpu.VMEM((2 * tokens, half), BF16),
        ],
        (table, columns, gain, *inputs),
        name="place",
    )


def message_rows(message):
    array, part, parts = message
    size = array.shape[1] // parts
    low = part * size // 16 * 16
    high = min(array.shape[1], -(-(part + 1) * size // 16) * 16)
    return low, high, part * size - low


def expert_groups(groups, rows):
    return [(g, g * (rows // groups)) for g in range(groups)]


def partial_kernel(bounds, count, last, source, *refs):
    parts = len(bounds)
    weights, refs = refs[:count], refs[count:]
    sent, own = refs[: 2 * parts : 2], refs[1 : 2 * parts : 2]
    message, pieces, *refs = refs[2 * parts :]
    rows, held, sems = refs[:parts], refs[parts:-1], refs[-1]
    hidden = sent[0].shape[1] // count
    copies = []
    for n in range(hidden // STEP):
        for w in range(count):
            at = pl.ds(n * STEP, STEP)
            where = (at, slice(None)) if last else (slice(None), at)
            copies.append(
                pltpu.make_async_copy(weights[w].at[where], held[w].at[where], sems.at[w, n])
            )
            copies[-1].start()
    groups = message.shape[0]
    total = rows[0].shape[0]
    for t, (low, high, base) in enumerate(bounds):
        widen(source, message, low, high)
        unfold(message, pieces, total // groups, base, expert_groups(groups, total))
        join(pieces, rows[t])
    copies = iter(copies)
    for n in range(hidden // STEP):
        for w in range(count):
            next(copies).wait()
            at = slice(n * STEP, (n + 1) * STEP)
            place_at = slice(w * hidden + n * STEP, w * hidden + (n + 1) * STEP)
            for t in range(parts):
                if last:
                    result = dot_last(rows[t][...], held[w][at, :])
                else:
                    result = dot(rows[t][...], held[w][:, at])
                own[t][:, place_at] = result
                sent[t][:, place_at] = result.astype(BF16)


def partial(source, numbers, of, weights, rows, last):
    bounds = [message_rows((source, number, of)) for number in numbers]
    width, hidden = weights[0].shape[::-1] if last else weights[0].shape
    shape = (rows, len(weights) * hidden)
    return call(
        functools.partial(partial_kernel, bounds, len(weights), last),
        (struct(shape, BF16), struct(shape, F32)) * len(numbers),
        [
            pltpu.VMEM((source.shape[0], bounds[0][1] - bounds[0][0], LANES), F32),
            pltpu.VMEM((width // LANES, rows, LANES), F32),
            *[pltpu.VMEM((rows, width), BF16) for _ in numbers],
            *[pltpu.VMEM(w.shape, BF16) for w in weights],
            pltpu.SemaphoreType.DMA((len(weights), hidden // STEP)),
        ],
        (source, *weights),
        in_hbm=range(1, 1 + len(weights)),
        name="partial",
    )


def finish(message, pieces, groups, out):
    total = pieces.shape[1]
    count = total // groups
    fold(pieces, message, count, 0, expert_groups(groups, total))
    clear_padding(message, count, 0, pieces.shape[0])
    narrow(message, out)


def forward_kernel(own, got, weight, out, active, pieces, message, held, sems):
    width = held.shape[1]
    hidden = held.shape[0]
    copies = []
    for n in range(width // STEP):
        at = (slice(None), pl.ds(n * STEP, STEP))
        copies.append(pltpu.make_async_copy(weight.at[at], held.at[at], sems.at[n]))
        copies[-1].start()
    for n in range(hidden // STEP):
        a = slice(n * STEP, (n + 1) * STEP)
        b = slice(hidden + n * STEP, hidden + (n + 1) * STEP)
        gate = own[:, a] + got[:, a].astype(F32)
        upper = own[:, b] + got[:, b].astype(F32)
        active[:, a] = (gate * jax.nn.sigmoid(gate) * upper).astype(BF16)
    for n in range(width // STEP):
        copies[n].wait()
        put_columns(pieces, n, dot(active[...], held[:, n * STEP : (n + 1) * STEP]))
    finish(message, pieces, out.shape[0], out)


def message_shape(groups, rows, chunks):
    return (groups, ceil8(rows // groups * chunks), LANES)


def forward_rest(own, got, weight, groups):
    rows = own.shape[0]
    hidden, width = weight.shape
    shape = message_shape(groups, rows, width // LANES)
    return call(
        forward_kernel,
        struct(shape, BF16),
        [
            pltpu.VMEM((rows, hidden), BF16),
            pltpu.VMEM((width // LANES, rows, LANES), F32),
            pltpu.VMEM(shape, F32),
            pltpu.VMEM(weight.shape, BF16),
            pltpu.SemaphoreType.DMA((width // STEP,)),
        ],
        (own, got, weight),
        in_hbm=(2,),
        name="forward_rest",
    )


def backward_kernel(
    own, got, down_own, down_got, gate_w, up_w, out, dgate, dupper, pieces, message, held_gate, held_up, sems
):
    width, hidden = held_gate.shape
    copies = []
    for n in range(width // STEP):
        at = pl.ds(n * STEP, STEP)
        for w, (weight, held) in enumerate(((gate_w, held_gate), (up_w, held_up))):
            copies.append(pltpu.make_async_copy(weight.at[at], held.at[at], sems.at[w, n]))
            copies[-1].start()
    for n in range(hidden // STEP):
        a = slice(n * STEP, (n + 1) * STEP)
        b = slice(hidden + n * STEP, hidden + (n + 1) * STEP)
        gate = own[:, a] + got[:, a].astype(F32)
        upper = own[:, b] + got[:, b].astype(F32)
        dactive = down_own[:, a] + down_got[:, a].astype(F32)
        sigma = jax.nn.sigmoid(gate)
        dgate[:, a] = (dactive * upper * sigma * (1.0 + gate * (1.0 - sigma))).astype(BF16)
        dupper[:, a] = (dactive * gate * sigma).astype(BF16)
    for n in range(width // STEP):
        copies[2 * n].wait()
        copies[2 * n + 1].wait()
        at = slice(n * STEP, (n + 1) * STEP)
        put_columns(
            pieces,
            n,
            dot_last(dgate[...], held_gate[at, :]) + dot_last(dupper[...], held_up[at, :]),
        )
    finish(message, pieces, out.shape[0], out)


def backward_rest(own, got, down_own, down_got, gate_w, up_w, groups):
    rows = own.shape[0]
    width, hidden = gate_w.shape
    shape = message_shape(groups, rows, width // LANES)
    return call(
        backward_kernel,
        struct(shape, BF16),
        [
            pltpu.VMEM((rows, hidden), BF16),
            pltpu.VMEM((rows, hidden), BF16),
            pltpu.VMEM((width // LANES, rows, LANES), F32),
            pltpu.VMEM(shape, F32),
            pltpu.VMEM(gate_w.shape, BF16),
            pltpu.VMEM(up_w.shape, BF16),
            pltpu.SemaphoreType.DMA((2, width // STEP)),
        ],
        (own, got, down_own, down_got, gate_w, up_w),
        in_hbm=(4, 5),
        name="backward_rest",
    )


def returned_rows(source, message, pieces, rows):
    widen(source, message, 0, source.shape[1])
    groups = message.shape[0]
    unfold(message, pieces, pieces.shape[1] // groups, 0, expert_groups(groups, pieces.shape[1]))
    join(pieces, rows)


def combine_forward_kernel(index, source, columns, value, out, square, message, pieces, rows):
    returned_rows(source, message, pieces, rows)
    picks, mixes = [], []
    for k in range(2):
        at = 2 * index + k
        picks.append(token_selector(columns[:, MARK + at : MARK + at + 1], rows.shape[0]))
        mixes.append(columns[:, MIX + at : MIX + at + 1])
    total = jnp.zeros((value.shape[0], 1), F32)
    for n in range(value.shape[1] // STEP):
        at = slice(n * STEP, (n + 1) * STEP)
        mixed = mixes[0] * dot(picks[0], rows[:, at]) + mixes[1] * dot(picks[1], rows[:, at])
        result = (value[:, at].astype(F32) + ROUTE_SCALE * mixed).astype(BF16)
        out[:, at] = result
        wide = result.astype(F32)
        total = total + jnp.sum(wide * wide, axis=1, keepdims=True)
    square[...] = total


def returned_scratch(source, rows, half):
    return [
        pltpu.VMEM(source.shape, F32),
        pltpu.VMEM((half // LANES, rows, LANES), F32),
        pltpu.VMEM((rows, half), BF16),
    ]


def combine_forward(index, source, columns, value):
    tokens, half = value.shape
    rows = source.shape[0] * 2 * SLOTS
    return call(
        functools.partial(combine_forward_kernel, index),
        (struct(value.shape, BF16), struct((tokens, 1), F32)),
        returned_scratch(source, rows, half),
        (source, columns, value),
        name="combine_forward",
    )


def combine_backward_kernel(
    index, source, columns, gain, saved, weighted, part, message, pieces, rows
):
    returned_rows(source, message, pieces, rows)
    chosen = sum(
        token_selector(columns[:, MARK + at : MARK + at + 1], rows.shape[0])
        for at in (2 * index, 2 * index + 1)
    )
    total = jnp.zeros((saved.shape[0], 1), F32)
    for n in range(saved.shape[1] // STEP):
        at = slice(n * STEP, (n + 1) * STEP)
        result = dot(chosen, rows[:, at]) * gain[:, at]
        weighted[:, at] = result
        total = total + jnp.sum(result * saved[:, at].astype(F32), axis=1, keepdims=True)
    part[...] = total


def combine_backward(index, source, columns, gain, saved):
    tokens, half = saved.shape
    rows = source.shape[0] * 2 * SLOTS
    return call(
        functools.partial(combine_backward_kernel, index),
        (struct(saved.shape, F32), struct((tokens, 1), F32)),
        returned_scratch(source, rows, half),
        (source, columns, gain, saved),
        name="combine_backward",
    )


def home_rows(source, message, pieces, rows, side):
    groups = [(2 * e + side, e * SLOTS) for e in range(message.shape[0] // 2)]
    unfold(message, pieces, SLOTS, 0, groups)
    join(pieces, rows)


def final_forward_kernel(index, source, columns, value, out, message, pieces, rows):
    widen(source, message, 0, source.shape[1])
    half = rows.shape[1]
    picks, mixes = [], []
    for k in range(2):
        at = 2 * index + k
        picks.append(token_selector(columns[:, MARK + at : MARK + at + 1], rows.shape[0]))
        mixes.append(columns[:, MIX + at : MIX + at + 1])
    for side in range(2):
        home_rows(source, message, pieces, rows, side)
        for n in range(half // STEP):
            low = n * STEP
            at = slice(low, low + STEP)
            to = slice(side * half + low, side * half + low + STEP)
            mixed = mixes[0] * dot(picks[0], rows[:, at]) + mixes[1] * dot(picks[1], rows[:, at])
            out[:, to] = (value[:, to].astype(F32) + ROUTE_SCALE * mixed).astype(BF16)


def final_forward(index, source, columns, value):
    tokens, width = value.shape
    rows = source.shape[0] // 2 * SLOTS
    return call(
        functools.partial(final_forward_kernel, index),
        struct(value.shape, BF16),
        returned_scratch(source, rows, width // 2),
        (source, columns, value),
        name="final_forward",
    )


def swap_dp(value):
    return lax.ppermute(value, "dp", [(0, 1), (1, 0)])


def move_section(value, step, flip_dp=False):
    sections = lax.axis_size("section")
    halves = lax.axis_size("dp")
    route = []
    for s in range(sections):
        if 0 <= s + step < sections:
            for d in range(halves):
                to = 1 - d if flip_dp else d
                route.append((s * halves + d, (s + step) * halves + to))
    return lax.ppermute(value, ("section", "dp"), route)


def route(message, axes="expert"):
    return lax.all_to_all(message, axes, split_axis=0, concat_axis=0, tiled=True)


def after(value, *earlier):
    return lax.optimization_barrier((value, *earlier))[0]


def body(
    fwd_input,
    back_saved,
    back_grad,
    norm_gain,
    gate_weight,
    up_weight,
    down_weight,
    routes,
    slots,
    affinity,
):
    experts = lax.axis_size("expert")
    tokens = fwd_input.shape[1]
    width = fwd_input.shape[2]
    half = width // 2
    rows = experts * 2 * SLOTS
    side = lax.axis_index("dp")
    both = ("expert", "dp")
    gate_w, up_w, down_w = gate_weight[0, 0], up_weight[0, 0], down_weight[0, 0]
    gain = norm_gain
    gain_half = lax.dynamic_slice(gain, (0, side * half), (1, half))

    x0, s0, s1, g0 = fwd_input[0], back_saved[0, 0], back_saved[1, 0], back_grad[0]

    def inverse_of(value):
        wide = value.astype(F32)
        return lax.rsqrt(jnp.mean(wide * wide, axis=-1) + EPSILON)

    def in_order(own, other):
        return jnp.where(side == 0, own, other), jnp.where(side == 0, other, own)

    def flat(value):
        return jnp.transpose(value, (0, 2, 1)).reshape(8, tokens)

    chosen, held = routes[:, 0], slots[:, 0]
    mixing = affinity[:, 0] / jnp.sum(affinity[:, 0], axis=-1, keepdims=True)
    inverses = jnp.stack([inverse_of(s0), inverse_of(s1), inverse_of(x0)])

    def scalars_of(marks):
        return jnp.concatenate([inverses, flat(marks.astype(F32)), flat(mixing)])

    local = scalars_of(chosen * SLOTS + held)
    own_scalars = scalars_of(chosen * (2 * SLOTS) + side * SLOTS + held)
    table = jnp.concatenate(in_order(own_scalars, swap_dp(own_scalars)), axis=1)
    local_columns = jnp.transpose(local)
    columns = jnp.transpose(table)

    def swap_halves(values):
        stacked = jnp.stack(values)
        own = lax.dynamic_slice_in_dim(stacked, side * half, half, axis=2)
        other = lax.dynamic_slice_in_dim(stacked, (1 - side) * half, half, axis=2)
        a, b = in_order(own, swap_dp(other))
        joined = jnp.concatenate([a, b], axis=1)
        return [joined[i] for i in range(len(values))]

    def full_features(value):
        mine, theirs = in_order(value[:tokens], value[tokens:])
        return jnp.concatenate(in_order(mine, swap_dp(theirs)), axis=1)

    def gradient(saved, inverse_row, grads, weighted, part):
        project = (part + swap_dp(part)) / width
        inverse = columns[:, inverse_row : inverse_row + 1]
        wide = saved.astype(F32)
        return (
            grads.astype(F32) + inverse * (weighted - wide * inverse * inverse * project)
        ).astype(BF16)

    first = route(
        spread((("normed", 1), ("grads", 1)), local, local_columns, gain, (s0, g0), experts), both
    )
    x0h, s1h = swap_halves([x0, s1])
    s0h, g0h = swap_halves([s0, g0])
    second_sent = place(
        (("normed", 0, TOKENS), ("normed", 3, SECOND_SAVED)),
        table,
        columns,
        gain_half,
        (x0h, s1h),
        experts,
    )
    second = route(after(second_sent, first))

    s0_sent, s0_own = partial(first, (0,), 2, (gate_w, up_w), rows, False)
    s0_got = swap_dp(s0_sent)
    g0_sent, g0_own = partial(after(first, s0_sent), (1,), 2, (down_w,), rows, True)
    g0_got = swap_dp(g0_sent)
    x0_sent, x0_own = partial(second, (0,), 2, (gate_w, up_w), rows, False)
    x0_got = swap_dp(x0_sent)
    dexp0 = backward_rest(
        s0_own, after(s0_got, x0_sent), g0_own, g0_got, gate_w, up_w, experts
    )
    dexp0_back = route(after(dexp0, second))
    s1_sent, s1_own = partial(after(second, dexp0), (1,), 2, (gate_w, up_w), rows, False)
    out0 = forward_rest(x0_own, after(x0_got, s1_sent), down_w, experts)
    s1_got = swap_dp(after(s1_sent, x0_got))
    out0_back = route(after(out0, dexp0_back))

    weighted, part = combine_backward(1, dexp0_back, columns, gain_half, s0h)
    g3h = move_section(gradient(s0h, FIRST_SAVED, g0h, weighted, part), -1)
    g3_placed = place((("grads", 3, None),), table, columns, gain_half, (g3h,), experts)
    g3_rows = route(after(g3_placed, out0_back, s1_got))

    first_out, square = combine_forward(0, out0_back, columns, x0h)
    x2h = move_section(first_out, 1)
    square_own = move_section(square, 1)
    square_other = move_section(square, 1, flip_dp=True)
    x2_placed = place(
        (("moved", 2, None),), table, columns, gain_half, (x2h, square_own, square_other), experts
    )
    g3_sent, g3_own = partial(g3_rows, (0,), 1, (down_w,), rows, True)
    x2_rows = route(after(x2_placed, g3_rows, g3_sent))

    x2 = full_features(x2h)
    dexp1 = backward_rest(s1_own, s1_got, g3_own, swap_dp(g3_sent), gate_w, up_w, experts)
    x2_sent, x2_own = partial(x2_rows, (0,), 1, (gate_w, up_w), rows, False)
    dexp1_back = route(after(dexp1, x2_rows, x2_sent, x2))
    out2 = forward_rest(x2_own, swap_dp(x2_sent), down_w, 2 * experts)
    out2_back = route(after(out2, dexp1_back), both)

    weighted, part = combine_backward(3, dexp1_back, columns, gain_half, s1h)
    final_back = full_features(gradient(s1h, SECOND_SAVED, g3h, weighted, part))
    final_out = final_forward(2, out2_back, local_columns, x2)
    return (final_out[None], final_back[None])


def solution(mesh):
    placed = (
        P("section", ("expert", "dp"), None),
        P(None, "section", ("expert", "dp"), None),
        P("section", ("expert", "dp"), None),
        P("section", None),
        P("section", "expert", "dp", None),
        P("section", "expert", "dp", None),
        P("section", "expert", None, "dp"),
        P(None, "section", ("expert", "dp"), None),
        P(None, "section", ("expert", "dp"), None),
        P(None, "section", ("expert", "dp"), None),
    )
    return jax.shard_map(
        body,
        mesh=mesh,
        in_specs=placed,
        out_specs=(P("section", ("expert", "dp"), None), P("section", ("expert", "dp"), None)),
        check_vma=False,
    )
```

```python
import functools

import jax
import jax.numpy as jnp
from jax import lax
from jax.experimental import pallas as pl
from jax.experimental.pallas import tpu as pltpu
from jax.sharding import PartitionSpec as P

ROUTE_SCALE = 2.5
EPSILON = 1e-06
BF16 = jnp.bfloat16
F32 = jnp.float32
SLOTS = 7
LANES = 128
STEP = 256
FIRST_SAVED, SECOND_SAVED, TOKENS = 0, 1, 2
MARK = 3
MIX = 11


def ceil8(count):
    return -(-count // 8) * 8


def call(kernel, out_shape, scratch, operands, in_hbm=(), anywhere=(), out_hbm=False, name=None):
    def place_of(hbm, free=False):
        return pl.BlockSpec(memory_space=pl.ANY if free else pltpu.HBM if hbm else pltpu.VMEM)

    return pl.pallas_call(
        kernel,
        out_shape=out_shape,
        in_specs=[place_of(i in in_hbm, i in anywhere) for i in range(len(operands))],
        out_specs=jax.tree.map(lambda _: place_of(out_hbm), out_shape),
        scratch_shapes=scratch,
        compiler_params=pltpu.CompilerParams(vmem_limit_bytes=50 * 1024 * 1024),
        cost_estimate=pl.CostEstimate(flops=1024, bytes_accessed=1024, transcendentals=0),
        name=name,
    )(*operands)


def start_copy(source, target, sem):
    copy = pltpu.make_async_copy(source, target, sem)
    copy.start()
    return copy


def struct(shape, dtype):
    return jax.ShapeDtypeStruct(shape, dtype)


def dot(left, right):
    return jnp.dot(left, right, preferred_element_type=F32)


def dot_last(left, right):
    return lax.dot_general(left, right, (((1,), (1,)), ((), ())), preferred_element_type=F32)


def put_columns(pieces, step, value):
    for j in range(STEP // LANES):
        pieces[step * (STEP // LANES) + j] = value[:, j * LANES : (j + 1) * LANES]


def fold(pieces, message, count, base, groups):
    for group, first in groups:
        for c in range(pieces.shape[0]):
            message[group, base + c * count : base + (c + 1) * count, :] = pieces[
                c, first : first + count, :
            ]


def unfold(message, pieces, count, base, groups):
    for group, first in groups:
        for c in range(pieces.shape[0]):
            pieces[c, first : first + count, :] = message[
                group, base + c * count : base + (c + 1) * count, :
            ]


def clear_padding(message, count, base, size):
    used = base + count * size
    if ceil8(used) > used:
        shape = (message.shape[0], ceil8(used) - used, LANES)
        message[:, used : ceil8(used), :] = jnp.zeros(shape, F32)


def join(pieces, rows):
    for c in range(pieces.shape[0]):
        rows[:, c * LANES : (c + 1) * LANES] = pieces[c].astype(BF16)


def widen(source, message, low, high):
    for g in range(message.shape[0]):
        message[g] = source[g, low:high, :].astype(F32)


def narrow(message, out):
    for g in range(message.shape[0]):
        out[g] = message[g].astype(BF16)


def row_selector(marks, rows):
    places = lax.broadcasted_iota(jnp.int32, (rows, marks.shape[1]), 0).astype(F32)
    return jnp.where(places == marks, 1.0, 0.0).astype(BF16)


def token_selector(marks, rows):
    places = lax.broadcasted_iota(jnp.int32, (marks.shape[0], rows), 1).astype(F32)
    return jnp.where(places == marks, 1.0, 0.0).astype(BF16)


def spread_kernel(parts, scalars, columns, gain, *refs):
    count = len(parts)
    values, (out, pieces, message, ready) = refs[:count], refs[count:]
    half = pieces.shape[0] * LANES
    rows = pieces.shape[1]
    size = ceil8(SLOTS * pieces.shape[0])
    for t, ((kind, index), value) in enumerate(zip(parts, values)):
        wide = value[...].astype(F32)
        tokens = wide.shape[0]
        at = MARK + 2 * index
        pick = [row_selector(scalars[at + k : at + k + 1, :], rows) for k in range(2)]
        if kind == "grads":
            chosen = jnp.concatenate(pick, axis=1)
            at = MIX + 2 * index
            for k in range(2):
                mix = columns[:, at + k : at + k + 1]
                ready[k * tokens : (k + 1) * tokens, :] = (ROUTE_SCALE * mix * wide).astype(BF16)
        else:
            chosen = pick[0] + pick[1]
            inverse = lax.rsqrt(jnp.mean(wide * wide, axis=-1, keepdims=True) + EPSILON)
            ready[0:tokens, :] = (wide * inverse * gain[...]).astype(BF16)
        depth = chosen.shape[1]
        for h in range(2):
            for n in range(half // STEP):
                low = h * half + n * STEP
                put_columns(pieces, n, dot(chosen, ready[0:depth, low : low + STEP]))
            fold(
                pieces,
                message,
                SLOTS,
                t * size,
                [(2 * e + h, e * SLOTS) for e in range(rows // SLOTS)],
            )
        clear_padding(message, SLOTS, t * size, pieces.shape[0])
    narrow(message, out)


def spread(parts, scalars, columns, gain, values, experts):
    tokens, width = values[0].shape
    chunks = width // 2 // LANES
    rows = experts * SLOTS
    shape = (2 * experts, len(values) * ceil8(SLOTS * chunks), LANES)
    return call(
        functools.partial(spread_kernel, parts),
        struct(shape, BF16),
        [
            pltpu.VMEM((chunks, rows, LANES), F32),
            pltpu.VMEM(shape, F32),
            pltpu.VMEM((2 * tokens, width), BF16),
        ],
        (scalars, columns, gain, *values),
        name="spread",
    )


def place_kernel(parts, rows, table, columns, gain, *refs):
    *inputs, out, pieces, message, ready = refs
    chunks = pieces.shape[0]
    half = chunks * LANES
    count = 2 * SLOTS
    size = ceil8(count * chunks)
    inputs = iter(inputs)
    for t, (kind, index, inverse_row) in enumerate(parts):
        value = next(inputs)[...].astype(F32)
        tokens = value.shape[0]
        pick = [
            row_selector(table[MARK + 2 * index + k : MARK + 2 * index + k + 1, :], rows)
            for k in range(2)
        ]
        if kind == "grads":
            for k in range(2):
                mix = columns[:, MIX + 2 * index + k : MIX + 2 * index + k + 1]
                ready[k * tokens : (k + 1) * tokens, :] = (ROUTE_SCALE * mix * value).astype(BF16)
            chosen = jnp.concatenate(pick, axis=1)
        else:
            if kind == "normed":
                inverse = columns[:, inverse_row : inverse_row + 1]
            else:
                squares = next(inputs)[...] + next(inputs)[...]
                inverse = lax.rsqrt(squares / (2 * half) + EPSILON)
            ready[0:tokens, :] = (value * inverse * gain[...]).astype(BF16)
            chosen = pick[0] + pick[1]
        depth = chosen.shape[1]
        for n in range(half // STEP):
            put_columns(pieces, n, dot(chosen, ready[0:depth, n * STEP : (n + 1) * STEP]))
        fold(
            pieces, message, count, t * size, [(e, e * count) for e in range(rows // count)]
        )
        clear_padding(message, count, t * size, chunks)
    narrow(message, out)


def place(parts, table, columns, gain, inputs, experts):
    tokens, half = inputs[0].shape
    chunks = half // LANES
    rows = experts * 2 * SLOTS
    shape = (experts, len(parts) * ceil8(2 * SLOTS * chunks), LANES)
    return call(
        functools.partial(place_kernel, parts, rows),
        struct(shape, BF16),
        [
            pltpu.VMEM((chunks, rows, LANES), F32),
            pltpu.VMEM(shape, F32),
            pltpu.VMEM((2 * tokens, half), BF16),
        ],
        (table, columns, gain, *inputs),
        name="place",
    )


def message_rows(message):
    array, part, parts = message
    size = array.shape[1] // parts
    low = part * size // 16 * 16
    high = min(array.shape[1], -(-(part + 1) * size // 16) * 16)
    return low, high, part * size - low


def expert_groups(groups, rows):
    return [(g, g * (rows // groups)) for g in range(groups)]


def partial_kernel(bounds, count, last, source, *refs):
    low, high, base = bounds
    weights, (sent, own), refs = refs[:count], refs[count : count + 2], refs[count + 2 :]
    arrived, message, pieces, rows, sent_held, own_held, *held, source_sem, sems, out_sems = refs
    hidden = sent.shape[1] // count
    source_copy = start_copy(source.at[:, pl.ds(low, high - low), :], arrived, source_sem)
    copies, results = [], []
    for n in range(hidden // STEP):
        for w in range(count):
            at = pl.ds(n * STEP, STEP)
            where = (at, slice(None)) if last else (slice(None), at)
            copies.append(start_copy(weights[w].at[where], held[w].at[where], sems.at[w, n]))
    groups = message.shape[0]
    total = rows.shape[0]
    source_copy.wait()
    widen(arrived, message, 0, high - low)
    unfold(message, pieces, total // groups, base, expert_groups(groups, total))
    join(pieces, rows)
    copies = iter(copies)
    for n in range(hidden // STEP):
        for w in range(count):
            next(copies).wait()
            at = slice(n * STEP, (n + 1) * STEP)
            if last:
                result = dot_last(rows[...], held[w][at, :])
            else:
                result = dot(rows[...], held[w][:, at])
            to = (slice(None), pl.ds(w * hidden + n * STEP, STEP))
            own_held[to] = result
            sent_held[to] = result.astype(BF16)
            results.append(start_copy(sent_held.at[to], sent.at[to], out_sems.at[0, w, n]))
            results.append(start_copy(own_held.at[to], own.at[to], out_sems.at[1, w, n]))
    for result in results:
        result.wait()


def partial(source, number, of, weights, rows, last):
    low, high, base = message_rows((source, number, of))
    width, hidden = weights[0].shape[::-1] if last else weights[0].shape
    count = len(weights)
    shape = (rows, count * hidden)
    slab = (source.shape[0], high - low, LANES)
    return call(
        functools.partial(partial_kernel, (low, high, base), count, last),
        (struct(shape, BF16), struct(shape, F32)),
        [
            pltpu.VMEM(slab, BF16),
            pltpu.VMEM(slab, F32),
            pltpu.VMEM((width // LANES, rows, LANES), F32),
            pltpu.VMEM((rows, width), BF16),
            pltpu.VMEM(shape, BF16),
            pltpu.VMEM(shape, F32),
            *[pltpu.VMEM(w.shape, BF16) for w in weights],
            pltpu.SemaphoreType.DMA,
            pltpu.SemaphoreType.DMA((count, hidden // STEP)),
            pltpu.SemaphoreType.DMA((2, count, hidden // STEP)),
        ],
        (source, *weights),
        in_hbm=range(1, 1 + count),
        anywhere=(0,),
        out_hbm=True,
        name="partial",
    )


def finish(message, pieces, groups, out):
    total = pieces.shape[1]
    count = total // groups
    fold(pieces, message, count, 0, expert_groups(groups, total))
    clear_padding(message, count, 0, pieces.shape[0])
    narrow(message, out)


def forward_kernel(
    own, got, weight, out, active, pieces, message, own_held, got_held, held, act_sems, sems
):
    hidden, width = held.shape
    own_copy = start_copy(own, own_held, act_sems.at[0])
    got_copy = start_copy(got, got_held, act_sems.at[1])
    copies = []
    for n in range(width // STEP):
        at = (slice(None), pl.ds(n * STEP, STEP))
        copies.append(start_copy(weight.at[at], held.at[at], sems.at[n]))
    own_copy.wait()
    got_copy.wait()
    for n in range(hidden // STEP):
        a = slice(n * STEP, (n + 1) * STEP)
        b = slice(hidden + n * STEP, hidden + (n + 1) * STEP)
        gate = own_held[:, a] + got_held[:, a].astype(F32)
        upper = own_held[:, b] + got_held[:, b].astype(F32)
        active[:, a] = (gate * jax.nn.sigmoid(gate) * upper).astype(BF16)
    for n in range(width // STEP):
        copies[n].wait()
        put_columns(pieces, n, dot(active[...], held[:, n * STEP : (n + 1) * STEP]))
    finish(message, pieces, out.shape[0], out)


def message_shape(groups, rows, chunks):
    return (groups, ceil8(rows // groups * chunks), LANES)


def forward_rest(own, got, weight, groups):
    rows = own.shape[0]
    hidden, width = weight.shape
    shape = message_shape(groups, rows, width // LANES)
    return call(
        forward_kernel,
        struct(shape, BF16),
        [
            pltpu.VMEM((rows, hidden), BF16),
            pltpu.VMEM((width // LANES, rows, LANES), F32),
            pltpu.VMEM(shape, F32),
            pltpu.VMEM(own.shape, F32),
            pltpu.VMEM(got.shape, BF16),
            pltpu.VMEM(weight.shape, BF16),
            pltpu.SemaphoreType.DMA((2,)),
            pltpu.SemaphoreType.DMA((width // STEP,)),
        ],
        (own, got, weight),
        in_hbm=(0, 2),
        anywhere=(1,),
        name="forward_rest",
    )


def backward_kernel(*refs):
    activations, (gate_w, up_w, out, dgate, dupper, pieces, message), refs = (
        refs[:4],
        refs[4:11],
        refs[11:],
    )
    held, (held_gate, held_up, act_sems, sems) = refs[:4], refs[4:]
    width, hidden = held_gate.shape
    arrivals = [
        start_copy(activations[i], held[i], act_sems.at[i]) for i in range(len(activations))
    ]
    copies = []
    for n in range(width // STEP):
        at = pl.ds(n * STEP, STEP)
        copies.append(start_copy(gate_w.at[at], held_gate.at[at], sems.at[0, n]))
        copies.append(start_copy(up_w.at[at], held_up.at[at], sems.at[1, n]))
    for arrival in arrivals:
        arrival.wait()
    own, got, down_own, down_got = held
    for n in range(hidden // STEP):
        a = slice(n * STEP, (n + 1) * STEP)
        b = slice(hidden + n * STEP, hidden + (n + 1) * STEP)
        gate = own[:, a] + got[:, a].astype(F32)
        upper = own[:, b] + got[:, b].astype(F32)
        dactive = down_own[:, a] + down_got[:, a].astype(F32)
        sigma = jax.nn.sigmoid(gate)
        dgate[:, a] = (dactive * upper * sigma * (1.0 + gate * (1.0 - sigma))).astype(BF16)
        dupper[:, a] = (dactive * gate * sigma).astype(BF16)
    for n in range(width // STEP):
        copies[2 * n].wait()
        copies[2 * n + 1].wait()
        at = slice(n * STEP, (n + 1) * STEP)
        put_columns(
            pieces,
            n,
            dot_last(dgate[...], held_gate[at, :]) + dot_last(dupper[...], held_up[at, :]),
        )
    finish(message, pieces, out.shape[0], out)


def backward_rest(own, got, down_own, down_got, gate_w, up_w, groups):
    rows = own.shape[0]
    width, hidden = gate_w.shape
    shape = message_shape(groups, rows, width // LANES)
    return call(
        backward_kernel,
        struct(shape, BF16),
        [
            pltpu.VMEM((rows, hidden), BF16),
            pltpu.VMEM((rows, hidden), BF16),
            pltpu.VMEM((width // LANES, rows, LANES), F32),
            pltpu.VMEM(shape, F32),
            *[pltpu.VMEM(x.shape, x.dtype) for x in (own, got, down_own, down_got)],
            pltpu.VMEM(gate_w.shape, BF16),
            pltpu.VMEM(up_w.shape, BF16),
            pltpu.SemaphoreType.DMA((4,)),
            pltpu.SemaphoreType.DMA((2, width // STEP)),
        ],
        (own, got, down_own, down_got, gate_w, up_w),
        in_hbm=(0, 2, 4, 5),
        anywhere=(1, 3),
        name="backward_rest",
    )


def returned_rows(source, message, pieces, rows):
    widen(source, message, 0, source.shape[1])
    groups = message.shape[0]
    unfold(message, pieces, pieces.shape[1] // groups, 0, expert_groups(groups, pieces.shape[1]))
    join(pieces, rows)


def combine_forward_kernel(index, source, columns, value, out, square, message, pieces, rows):
    returned_rows(source, message, pieces, rows)
    picks, mixes = [], []
    for k in range(2):
        at = 2 * index + k
        picks.append(token_selector(columns[:, MARK + at : MARK + at + 1], rows.shape[0]))
        mixes.append(columns[:, MIX + at : MIX + at + 1])
    total = jnp.zeros((value.shape[0], 1), F32)
    for n in range(value.shape[1] // STEP):
        at = slice(n * STEP, (n + 1) * STEP)
        mixed = mixes[0] * dot(picks[0], rows[:, at]) + mixes[1] * dot(picks[1], rows[:, at])
        result = (value[:, at].astype(F32) + ROUTE_SCALE * mixed).astype(BF16)
        out[:, at] = result
        wide = result.astype(F32)
        total = total + jnp.sum(wide * wide, axis=1, keepdims=True)
    square[...] = total


def returned_scratch(source, rows, half):
    return [
        pltpu.VMEM(source.shape, F32),
        pltpu.VMEM((half // LANES, rows, LANES), F32),
        pltpu.VMEM((rows, half), BF16),
    ]


def combine_forward(index, source, columns, value):
    tokens, half = value.shape
    rows = source.shape[0] * 2 * SLOTS
    return call(
        functools.partial(combine_forward_kernel, index),
        (struct(value.shape, BF16), struct((tokens, 1), F32)),
        returned_scratch(source, rows, half),
        (source, columns, value),
        name="combine_forward",
    )


def combine_backward_kernel(
    index, source, columns, gain, saved, weighted, part, message, pieces, rows
):
    returned_rows(source, message, pieces, rows)
    chosen = sum(
        token_selector(columns[:, MARK + at : MARK + at + 1], rows.shape[0])
        for at in (2 * index, 2 * index + 1)
    )
    total = jnp.zeros((saved.shape[0], 1), F32)
    for n in range(saved.shape[1] // STEP):
        at = slice(n * STEP, (n + 1) * STEP)
        result = dot(chosen, rows[:, at]) * gain[:, at]
        weighted[:, at] = result
        total = total + jnp.sum(result * saved[:, at].astype(F32), axis=1, keepdims=True)
    part[...] = total


def combine_backward(index, source, columns, gain, saved):
    tokens, half = saved.shape
    rows = source.shape[0] * 2 * SLOTS
    return call(
        functools.partial(combine_backward_kernel, index),
        (struct(saved.shape, F32), struct((tokens, 1), F32)),
        returned_scratch(source, rows, half),
        (source, columns, gain, saved),
        name="combine_backward",
    )


def home_rows(source, message, pieces, rows, side):
    groups = [(2 * e + side, e * SLOTS) for e in range(message.shape[0] // 2)]
    unfold(message, pieces, SLOTS, 0, groups)
    join(pieces, rows)


def final_forward_kernel(index, source, columns, value, out, message, pieces, rows):
    widen(source, message, 0, source.shape[1])
    half = rows.shape[1]
    picks, mixes = [], []
    for k in range(2):
        at = 2 * index + k
        picks.append(token_selector(columns[:, MARK + at : MARK + at + 1], rows.shape[0]))
        mixes.append(columns[:, MIX + at : MIX + at + 1])
    for side in range(2):
        home_rows(source, message, pieces, rows, side)
        for n in range(half // STEP):
            low = n * STEP
            at = slice(low, low + STEP)
            to = slice(side * half + low, side * half + low + STEP)
            mixed = mixes[0] * dot(picks[0], rows[:, at]) + mixes[1] * dot(picks[1], rows[:, at])
            out[:, to] = (value[:, to].astype(F32) + ROUTE_SCALE * mixed).astype(BF16)


def final_forward(index, source, columns, value):
    tokens, width = value.shape
    rows = source.shape[0] // 2 * SLOTS
    return call(
        functools.partial(final_forward_kernel, index),
        struct(value.shape, BF16),
        returned_scratch(source, rows, width // 2),
        (source, columns, value),
        name="final_forward",
    )


def swap_dp(value):
    return lax.ppermute(value, "dp", [(0, 1), (1, 0)])


def move_section(value, step, flip_dp=False):
    sections = lax.axis_size("section")
    halves = lax.axis_size("dp")
    route = []
    for s in range(sections):
        if 0 <= s + step < sections:
            for d in range(halves):
                to = 1 - d if flip_dp else d
                route.append((s * halves + d, (s + step) * halves + to))
    return lax.ppermute(value, ("section", "dp"), route)


def route(message, axes="expert"):
    return lax.all_to_all(message, axes, split_axis=0, concat_axis=0, tiled=True)


def after(value, *earlier):
    return lax.optimization_barrier((value, *earlier))[0]


def body(
    fwd_input,
    back_saved,
    back_grad,
    norm_gain,
    gate_weight,
    up_weight,
    down_weight,
    routes,
    slots,
    affinity,
):
    experts = lax.axis_size("expert")
    tokens = fwd_input.shape[1]
    width = fwd_input.shape[2]
    half = width // 2
    rows = experts * 2 * SLOTS
    side = lax.axis_index("dp")
    both = ("expert", "dp")
    gate_w, up_w, down_w = gate_weight[0, 0], up_weight[0, 0], down_weight[0, 0]
    gain = norm_gain
    gain_half = lax.dynamic_slice(gain, (0, side * half), (1, half))

    x0, s0, s1, g0 = fwd_input[0], back_saved[0, 0], back_saved[1, 0], back_grad[0]

    def inverse_of(value):
        wide = value.astype(F32)
        return lax.rsqrt(jnp.mean(wide * wide, axis=-1) + EPSILON)

    def in_order(own, other):
        return jnp.where(side == 0, own, other), jnp.where(side == 0, other, own)

    def flat(value):
        return jnp.transpose(value, (0, 2, 1)).reshape(8, tokens)

    chosen, held = routes[:, 0], slots[:, 0]
    mixing = affinity[:, 0] / jnp.sum(affinity[:, 0], axis=-1, keepdims=True)
    inverses = jnp.stack([inverse_of(s0), inverse_of(s1), inverse_of(x0)])

    def scalars_of(marks):
        return jnp.concatenate([inverses, flat(marks.astype(F32)), flat(mixing)])

    local = scalars_of(chosen * SLOTS + held)
    own_scalars = scalars_of(chosen * (2 * SLOTS) + side * SLOTS + held)
    table = jnp.concatenate(in_order(own_scalars, swap_dp(own_scalars)), axis=1)
    local_columns = jnp.transpose(local)
    columns = jnp.transpose(table)

    def swap_halves(values):
        stacked = jnp.stack(values)
        own = lax.dynamic_slice_in_dim(stacked, side * half, half, axis=2)
        other = lax.dynamic_slice_in_dim(stacked, (1 - side) * half, half, axis=2)
        a, b = in_order(own, swap_dp(other))
        joined = jnp.concatenate([a, b], axis=1)
        return [joined[i] for i in range(len(values))]

    def full_features(value):
        mine, theirs = in_order(value[:tokens], value[tokens:])
        return jnp.concatenate(in_order(mine, swap_dp(theirs)), axis=1)

    def gradient(saved, inverse_row, grads, weighted, part):
        project = (part + swap_dp(part)) / width
        inverse = columns[:, inverse_row : inverse_row + 1]
        wide = saved.astype(F32)
        return (
            grads.astype(F32) + inverse * (weighted - wide * inverse * inverse * project)
        ).astype(BF16)

    first = route(
        spread((("normed", 1), ("grads", 1)), local, local_columns, gain, (s0, g0), experts), both
    )
    x0h, s1h = swap_halves([x0, s1])
    s0h, g0h = swap_halves([s0, g0])
    second_sent = place(
        (("normed", 0, TOKENS), ("normed", 3, SECOND_SAVED)),
        table,
        columns,
        gain_half,
        (x0h, s1h),
        experts,
    )
    s0_sent, s0_own = partial(first, 0, 2, (gate_w, up_w), rows, False)
    s0_got = swap_dp(s0_sent)
    second = route(after(second_sent, s0_sent))
    g0_sent, g0_own = partial(first, 1, 2, (down_w,), rows, True)
    g0_got = swap_dp(g0_sent)
    dexp0 = backward_rest(s0_own, s0_got, g0_own, g0_got, gate_w, up_w, experts)
    x0_sent, x0_own = partial(second, 0, 2, (gate_w, up_w), rows, False)
    x0_got = swap_dp(x0_sent)
    dexp0_back = route(after(dexp0, x0_sent))
    s1_sent, s1_own = partial(after(second, dexp0), 1, 2, (gate_w, up_w), rows, False)
    out0 = forward_rest(x0_own, after(x0_got, s1_sent), down_w, experts)
    out0_back = route(after(out0, dexp0_back))

    weighted, part = combine_backward(1, dexp0_back, columns, gain_half, s0h)
    g3h = move_section(gradient(s0h, FIRST_SAVED, g0h, weighted, part), -1)
    g3_placed = place((("grads", 3, None),), table, columns, gain_half, (g3h,), experts)
    s1_got = swap_dp(after(s1_sent, g3h))
    g3_rows = route(after(g3_placed, out0_back))

    first_out, square = combine_forward(0, out0_back, columns, x0h)
    x2h = move_section(first_out, 1)
    square_own = move_section(square, 1)
    square_other = move_section(square, 1, flip_dp=True)
    x2_placed = place(
        (("moved", 2, None),), table, columns, gain_half, (x2h, square_own, square_other), experts
    )
    g3_sent, g3_own = partial(g3_rows, 0, 1, (down_w,), rows, True)
    x2_rows = route(after(x2_placed, g3_sent, s1_got))

    dexp1 = backward_rest(s1_own, s1_got, g3_own, swap_dp(g3_sent), gate_w, up_w, experts)
    x2_sent, x2_own = partial(x2_rows, 0, 1, (gate_w, up_w), rows, False)
    dexp1_back = route(after(dexp1, x2_sent))
    out2 = forward_rest(x2_own, swap_dp(x2_sent), down_w, 2 * experts)
    out2_back = route(after(out2, dexp1_back), both)
    x2 = full_features(after(x2h, dexp1_back))

    weighted, part = combine_backward(3, dexp1_back, columns, gain_half, s1h)
    final_back = full_features(gradient(s1h, SECOND_SAVED, g3h, weighted, part))
    final_out = final_forward(2, out2_back, local_columns, x2)
    return (final_out[None], final_back[None])


def solution(mesh):
    placed = (
        P("section", ("expert", "dp"), None),
        P(None, "section", ("expert", "dp"), None),
        P("section", ("expert", "dp"), None),
        P("section", None),
        P("section", "expert", "dp", None),
        P("section", "expert", "dp", None),
        P("section", "expert", None, "dp"),
        P(None, "section", ("expert", "dp"), None),
        P(None, "section", ("expert", "dp"), None),
        P(None, "section", ("expert", "dp"), None),
    )
    return jax.shard_map(
        body,
        mesh=mesh,
        in_specs=placed,
        out_specs=(P("section", ("expert", "dp"), None), P("section", ("expert", "dp"), None)),
        check_vma=False,
    )
```

```python
import functools

import jax
import jax.numpy as jnp
from jax import lax
from jax.experimental import pallas as pl
from jax.experimental.pallas import tpu as pltpu
from jax.sharding import PartitionSpec as P

ROUTE_SCALE = 2.5
EPSILON = 1e-06
BF16 = jnp.bfloat16
F32 = jnp.float32
SLOTS = 7
LANES = 128
LONG = 200_000_000_000
STEP = 256
FIRST_SAVED, SECOND_SAVED, TOKENS = 0, 1, 2
MARK = 3
MIX = 11


def ceil8(count):
    return -(-count // 8) * 8


def call(kernel, out_shape, scratch, operands, in_hbm=(), anywhere=(), out_hbm=False, cost=1024, name=None):
    def place_of(hbm, free=False):
        return pl.BlockSpec(memory_space=pl.ANY if free else pltpu.HBM if hbm else pltpu.VMEM)

    return pl.pallas_call(
        kernel,
        out_shape=out_shape,
        in_specs=[place_of(i in in_hbm, i in anywhere) for i in range(len(operands))],
        out_specs=jax.tree.map(lambda _: place_of(out_hbm), out_shape),
        scratch_shapes=scratch,
        compiler_params=pltpu.CompilerParams(vmem_limit_bytes=50 * 1024 * 1024),
        cost_estimate=pl.CostEstimate(flops=cost, bytes_accessed=1024, transcendentals=0),
        name=name,
    )(*operands)


def start_copy(source, target, sem):
    copy = pltpu.make_async_copy(source, target, sem)
    copy.start()
    return copy


def struct(shape, dtype):
    return jax.ShapeDtypeStruct(shape, dtype)


def dot(left, right):
    return jnp.dot(left, right, preferred_element_type=F32)


def dot_last(left, right):
    return lax.dot_general(left, right, (((1,), (1,)), ((), ())), preferred_element_type=F32)


def put_columns(pieces, step, value):
    for j in range(STEP // LANES):
        pieces[step * (STEP // LANES) + j] = value[:, j * LANES : (j + 1) * LANES]


def fold(pieces, message, count, base, groups):
    for group, first in groups:
        for c in range(pieces.shape[0]):
            message[group, base + c * count : base + (c + 1) * count, :] = pieces[
                c, first : first + count, :
            ]


def unfold(message, pieces, count, base, groups):
    for group, first in groups:
        for c in range(pieces.shape[0]):
            pieces[c, first : first + count, :] = message[
                group, base + c * count : base + (c + 1) * count, :
            ]


def clear_padding(message, count, base, size):
    used = base + count * size
    if ceil8(used) > used:
        shape = (message.shape[0], ceil8(used) - used, LANES)
        message[:, used : ceil8(used), :] = jnp.zeros(shape, F32)


def join(pieces, rows):
    for c in range(pieces.shape[0]):
        rows[:, c * LANES : (c + 1) * LANES] = pieces[c].astype(BF16)


def widen(source, message, low, high):
    for g in range(message.shape[0]):
        message[g] = source[g, low:high, :].astype(F32)


def narrow(message, out):
    for g in range(message.shape[0]):
        out[g] = message[g].astype(BF16)


def row_selector(marks, rows):
    places = lax.broadcasted_iota(jnp.int32, (rows, marks.shape[1]), 0).astype(F32)
    return jnp.where(places == marks, 1.0, 0.0).astype(BF16)


def token_selector(marks, rows):
    places = lax.broadcasted_iota(jnp.int32, (marks.shape[0], rows), 1).astype(F32)
    return jnp.where(places == marks, 1.0, 0.0).astype(BF16)


def spread_kernel(parts, scalars, columns, gain, *refs):
    count = len(parts)
    values, (out, pieces, message, ready) = refs[:count], refs[count:]
    half = pieces.shape[0] * LANES
    rows = pieces.shape[1]
    size = ceil8(SLOTS * pieces.shape[0])
    for t, ((kind, index), value) in enumerate(zip(parts, values)):
        wide = value[...].astype(F32)
        tokens = wide.shape[0]
        at = MARK + 2 * index
        pick = [row_selector(scalars[at + k : at + k + 1, :], rows) for k in range(2)]
        if kind == "grads":
            chosen = jnp.concatenate(pick, axis=1)
            at = MIX + 2 * index
            for k in range(2):
                mix = columns[:, at + k : at + k + 1]
                ready[k * tokens : (k + 1) * tokens, :] = (ROUTE_SCALE * mix * wide).astype(BF16)
        else:
            chosen = pick[0] + pick[1]
            inverse = lax.rsqrt(jnp.mean(wide * wide, axis=-1, keepdims=True) + EPSILON)
            ready[0:tokens, :] = (wide * inverse * gain[...]).astype(BF16)
        depth = chosen.shape[1]
        for h in range(2):
            for n in range(half // STEP):
                low = h * half + n * STEP
                put_columns(pieces, n, dot(chosen, ready[0:depth, low : low + STEP]))
            fold(
                pieces,
                message,
                SLOTS,
                t * size,
                [(2 * e + h, e * SLOTS) for e in range(rows // SLOTS)],
            )
        clear_padding(message, SLOTS, t * size, pieces.shape[0])
    narrow(message, out)


def spread(parts, scalars, columns, gain, values, experts):
    tokens, width = values[0].shape
    chunks = width // 2 // LANES
    rows = experts * SLOTS
    shape = (2 * experts, len(values) * ceil8(SLOTS * chunks), LANES)
    return call(
        functools.partial(spread_kernel, parts),
        struct(shape, BF16),
        [
            pltpu.VMEM((chunks, rows, LANES), F32),
            pltpu.VMEM(shape, F32),
            pltpu.VMEM((2 * tokens, width), BF16),
        ],
        (scalars, columns, gain, *values),
        name="spread",
    )


def place_kernel(parts, rows, table, columns, gain, *refs):
    *inputs, out, pieces, message, ready = refs
    chunks = pieces.shape[0]
    half = chunks * LANES
    count = 2 * SLOTS
    size = ceil8(count * chunks)
    inputs = iter(inputs)
    for t, (kind, index, inverse_row) in enumerate(parts):
        value = next(inputs)[...].astype(F32)
        tokens = value.shape[0]
        pick = [
            row_selector(table[MARK + 2 * index + k : MARK + 2 * index + k + 1, :], rows)
            for k in range(2)
        ]
        if kind == "grads":
            for k in range(2):
                mix = columns[:, MIX + 2 * index + k : MIX + 2 * index + k + 1]
                ready[k * tokens : (k + 1) * tokens, :] = (ROUTE_SCALE * mix * value).astype(BF16)
            chosen = jnp.concatenate(pick, axis=1)
        else:
            if kind == "normed":
                inverse = columns[:, inverse_row : inverse_row + 1]
            else:
                squares = next(inputs)[...] + next(inputs)[...]
                inverse = lax.rsqrt(squares / (2 * half) + EPSILON)
            ready[0:tokens, :] = (value * inverse * gain[...]).astype(BF16)
            chosen = pick[0] + pick[1]
        depth = chosen.shape[1]
        for n in range(half // STEP):
            put_columns(pieces, n, dot(chosen, ready[0:depth, n * STEP : (n + 1) * STEP]))
        fold(
            pieces, message, count, t * size, [(e, e * count) for e in range(rows // count)]
        )
        clear_padding(message, count, t * size, chunks)
    narrow(message, out)


def place(parts, table, columns, gain, inputs, experts):
    tokens, half = inputs[0].shape
    chunks = half // LANES
    rows = experts * 2 * SLOTS
    shape = (experts, len(parts) * ceil8(2 * SLOTS * chunks), LANES)
    return call(
        functools.partial(place_kernel, parts, rows),
        struct(shape, BF16),
        [
            pltpu.VMEM((chunks, rows, LANES), F32),
            pltpu.VMEM(shape, F32),
            pltpu.VMEM((2 * tokens, half), BF16),
        ],
        (table, columns, gain, *inputs),
        name="place",
    )


def message_rows(message):
    array, part, parts = message
    size = array.shape[1] // parts
    low = part * size // 16 * 16
    high = min(array.shape[1], -(-(part + 1) * size // 16) * 16)
    return low, high, part * size - low


def expert_groups(groups, rows):
    return [(g, g * (rows // groups)) for g in range(groups)]


def partial_kernel(bounds, count, last, source, *refs):
    low, high, base = bounds
    weights, (sent, own), refs = refs[:count], refs[count : count + 2], refs[count + 2 :]
    arrived, message, pieces, rows, sent_held, own_held, *held, source_sem, sems, out_sems = refs
    hidden = sent.shape[1] // count
    source_copy = start_copy(source.at[:, pl.ds(low, high - low), :], arrived, source_sem)
    copies, results = [], []
    for n in range(hidden // STEP):
        for w in range(count):
            at = pl.ds(n * STEP, STEP)
            where = (at, slice(None)) if last else (slice(None), at)
            copies.append(start_copy(weights[w].at[where], held[w].at[where], sems.at[w, n]))
    groups = message.shape[0]
    total = rows.shape[0]
    source_copy.wait()
    widen(arrived, message, 0, high - low)
    unfold(message, pieces, total // groups, base, expert_groups(groups, total))
    join(pieces, rows)
    copies = iter(copies)
    for n in range(hidden // STEP):
        for w in range(count):
            next(copies).wait()
            at = slice(n * STEP, (n + 1) * STEP)
            if last:
                result = dot_last(rows[...], held[w][at, :])
            else:
                result = dot(rows[...], held[w][:, at])
            to = (slice(None), pl.ds(w * hidden + n * STEP, STEP))
            own_held[to] = result
            sent_held[to] = result.astype(BF16)
            results.append(start_copy(sent_held.at[to], sent.at[to], out_sems.at[0, w, n]))
            results.append(start_copy(own_held.at[to], own.at[to], out_sems.at[1, w, n]))
    for result in results:
        result.wait()


def partial(source, number, of, weights, rows, last):
    low, high, base = message_rows((source, number, of))
    width, hidden = weights[0].shape[::-1] if last else weights[0].shape
    count = len(weights)
    shape = (rows, count * hidden)
    slab = (source.shape[0], high - low, LANES)
    return call(
        functools.partial(partial_kernel, (low, high, base), count, last),
        (struct(shape, BF16), struct(shape, F32)),
        [
            pltpu.VMEM(slab, BF16),
            pltpu.VMEM(slab, F32),
            pltpu.VMEM((width // LANES, rows, LANES), F32),
            pltpu.VMEM((rows, width), BF16),
            pltpu.VMEM(shape, BF16),
            pltpu.VMEM(shape, F32),
            *[pltpu.VMEM(w.shape, BF16) for w in weights],
            pltpu.SemaphoreType.DMA,
            pltpu.SemaphoreType.DMA((count, hidden // STEP)),
            pltpu.SemaphoreType.DMA((2, count, hidden // STEP)),
        ],
        (source, *weights),
        in_hbm=range(1, 1 + count),
        anywhere=(0,),
        out_hbm=True,
        name="partial",
    )


def finish(message, pieces, groups, out):
    total = pieces.shape[1]
    count = total // groups
    fold(pieces, message, count, 0, expert_groups(groups, total))
    clear_padding(message, count, 0, pieces.shape[0])
    narrow(message, out)


def forward_kernel(
    own, got, weight, out, active, pieces, message, own_held, got_held, held, act_sems, sems
):
    hidden, width = held.shape
    own_copy = start_copy(own, own_held, act_sems.at[0])
    got_copy = start_copy(got, got_held, act_sems.at[1])
    copies = []
    for n in range(width // STEP):
        at = (slice(None), pl.ds(n * STEP, STEP))
        copies.append(start_copy(weight.at[at], held.at[at], sems.at[n]))
    own_copy.wait()
    got_copy.wait()
    for n in range(hidden // STEP):
        a = slice(n * STEP, (n + 1) * STEP)
        b = slice(hidden + n * STEP, hidden + (n + 1) * STEP)
        gate = own_held[:, a] + got_held[:, a].astype(F32)
        upper = own_held[:, b] + got_held[:, b].astype(F32)
        active[:, a] = (gate * jax.nn.sigmoid(gate) * upper).astype(BF16)
    for n in range(width // STEP):
        copies[n].wait()
        put_columns(pieces, n, dot(active[...], held[:, n * STEP : (n + 1) * STEP]))
    finish(message, pieces, out.shape[0], out)


def message_shape(groups, rows, chunks):
    return (groups, ceil8(rows // groups * chunks), LANES)


def forward_rest(own, got, weight, groups):
    rows = own.shape[0]
    hidden, width = weight.shape
    shape = message_shape(groups, rows, width // LANES)
    return call(
        forward_kernel,
        struct(shape, BF16),
        [
            pltpu.VMEM((rows, hidden), BF16),
            pltpu.VMEM((width // LANES, rows, LANES), F32),
            pltpu.VMEM(shape, F32),
            pltpu.VMEM(own.shape, F32),
            pltpu.VMEM(got.shape, BF16),
            pltpu.VMEM(weight.shape, BF16),
            pltpu.SemaphoreType.DMA((2,)),
            pltpu.SemaphoreType.DMA((width // STEP,)),
        ],
        (own, got, weight),
        in_hbm=(0, 2),
        anywhere=(1,),
        cost=LONG,
        name="forward_rest",
    )


def backward_kernel(*refs):
    activations, (gate_w, up_w, out, dgate, dupper, pieces, message), refs = (
        refs[:4],
        refs[4:11],
        refs[11:],
    )
    held, (held_gate, held_up, act_sems, sems) = refs[:4], refs[4:]
    width, hidden = held_gate.shape
    arrivals = [
        start_copy(activations[i], held[i], act_sems.at[i]) for i in range(len(activations))
    ]
    copies = []
    for n in range(width // STEP):
        at = pl.ds(n * STEP, STEP)
        copies.append(start_copy(gate_w.at[at], held_gate.at[at], sems.at[0, n]))
        copies.append(start_copy(up_w.at[at], held_up.at[at], sems.at[1, n]))
    for arrival in arrivals:
        arrival.wait()
    own, got, down_own, down_got = held
    for n in range(hidden // STEP):
        a = slice(n * STEP, (n + 1) * STEP)
        b = slice(hidden + n * STEP, hidden + (n + 1) * STEP)
        gate = own[:, a] + got[:, a].astype(F32)
        upper = own[:, b] + got[:, b].astype(F32)
        dactive = down_own[:, a] + down_got[:, a].astype(F32)
        sigma = jax.nn.sigmoid(gate)
        dgate[:, a] = (dactive * upper * sigma * (1.0 + gate * (1.0 - sigma))).astype(BF16)
        dupper[:, a] = (dactive * gate * sigma).astype(BF16)
    for n in range(width // STEP):
        copies[2 * n].wait()
        copies[2 * n + 1].wait()
        at = slice(n * STEP, (n + 1) * STEP)
        put_columns(
            pieces,
            n,
            dot_last(dgate[...], held_gate[at, :]) + dot_last(dupper[...], held_up[at, :]),
        )
    finish(message, pieces, out.shape[0], out)


def backward_rest(own, got, down_own, down_got, gate_w, up_w, groups, cost=1024):
    rows = own.shape[0]
    width, hidden = gate_w.shape
    shape = message_shape(groups, rows, width // LANES)
    return call(
        backward_kernel,
        struct(shape, BF16),
        [
            pltpu.VMEM((rows, hidden), BF16),
            pltpu.VMEM((rows, hidden), BF16),
            pltpu.VMEM((width // LANES, rows, LANES), F32),
            pltpu.VMEM(shape, F32),
            *[pltpu.VMEM(x.shape, x.dtype) for x in (own, got, down_own, down_got)],
            pltpu.VMEM(gate_w.shape, BF16),
            pltpu.VMEM(up_w.shape, BF16),
            pltpu.SemaphoreType.DMA((4,)),
            pltpu.SemaphoreType.DMA((2, width // STEP)),
        ],
        (own, got, down_own, down_got, gate_w, up_w),
        in_hbm=(0, 2, 4, 5),
        anywhere=(1, 3),
        cost=cost,
        name="backward_rest",
    )


def returned_rows(source, message, pieces, rows):
    widen(source, message, 0, source.shape[1])
    groups = message.shape[0]
    unfold(message, pieces, pieces.shape[1] // groups, 0, expert_groups(groups, pieces.shape[1]))
    join(pieces, rows)


def combine_forward_kernel(index, source, columns, value, out, square, message, pieces, rows):
    returned_rows(source, message, pieces, rows)
    picks, mixes = [], []
    for k in range(2):
        at = 2 * index + k
        picks.append(token_selector(columns[:, MARK + at : MARK + at + 1], rows.shape[0]))
        mixes.append(columns[:, MIX + at : MIX + at + 1])
    total = jnp.zeros((value.shape[0], 1), F32)
    for n in range(value.shape[1] // STEP):
        at = slice(n * STEP, (n + 1) * STEP)
        mixed = mixes[0] * dot(picks[0], rows[:, at]) + mixes[1] * dot(picks[1], rows[:, at])
        result = (value[:, at].astype(F32) + ROUTE_SCALE * mixed).astype(BF16)
        out[:, at] = result
        wide = result.astype(F32)
        total = total + jnp.sum(wide * wide, axis=1, keepdims=True)
    square[...] = total


def returned_scratch(source, rows, half):
    return [
        pltpu.VMEM(source.shape, F32),
        pltpu.VMEM((half // LANES, rows, LANES), F32),
        pltpu.VMEM((rows, half), BF16),
    ]


def combine_forward(index, source, columns, value):
    tokens, half = value.shape
    rows = source.shape[0] * 2 * SLOTS
    return call(
        functools.partial(combine_forward_kernel, index),
        (struct(value.shape, BF16), struct((tokens, 1), F32)),
        returned_scratch(source, rows, half),
        (source, columns, value),
        name="combine_forward",
    )


def combine_backward_kernel(
    index, source, columns, gain, saved, weighted, part, message, pieces, rows
):
    returned_rows(source, message, pieces, rows)
    chosen = sum(
        token_selector(columns[:, MARK + at : MARK + at + 1], rows.shape[0])
        for at in (2 * index, 2 * index + 1)
    )
    total = jnp.zeros((saved.shape[0], 1), F32)
    for n in range(saved.shape[1] // STEP):
        at = slice(n * STEP, (n + 1) * STEP)
        result = dot(chosen, rows[:, at]) * gain[:, at]
        weighted[:, at] = result
        total = total + jnp.sum(result * saved[:, at].astype(F32), axis=1, keepdims=True)
    part[...] = total


def combine_backward(index, source, columns, gain, saved):
    tokens, half = saved.shape
    rows = source.shape[0] * 2 * SLOTS
    return call(
        functools.partial(combine_backward_kernel, index),
        (struct(saved.shape, F32), struct((tokens, 1), F32)),
        returned_scratch(source, rows, half),
        (source, columns, gain, saved),
        name="combine_backward",
    )


def home_rows(source, message, pieces, rows, side):
    groups = [(2 * e + side, e * SLOTS) for e in range(message.shape[0] // 2)]
    unfold(message, pieces, SLOTS, 0, groups)
    join(pieces, rows)


def final_forward_kernel(index, source, columns, value, out, message, pieces, rows):
    widen(source, message, 0, source.shape[1])
    half = rows.shape[1]
    picks, mixes = [], []
    for k in range(2):
        at = 2 * index + k
        picks.append(token_selector(columns[:, MARK + at : MARK + at + 1], rows.shape[0]))
        mixes.append(columns[:, MIX + at : MIX + at + 1])
    for side in range(2):
        home_rows(source, message, pieces, rows, side)
        for n in range(half // STEP):
            low = n * STEP
            at = slice(low, low + STEP)
            to = slice(side * half + low, side * half + low + STEP)
            mixed = mixes[0] * dot(picks[0], rows[:, at]) + mixes[1] * dot(picks[1], rows[:, at])
            out[:, to] = (value[:, to].astype(F32) + ROUTE_SCALE * mixed).astype(BF16)


def final_forward(index, source, columns, value):
    tokens, width = value.shape
    rows = source.shape[0] // 2 * SLOTS
    return call(
        functools.partial(final_forward_kernel, index),
        struct(value.shape, BF16),
        returned_scratch(source, rows, width // 2),
        (source, columns, value),
        name="final_forward",
    )


def swap_dp(value):
    return lax.ppermute(value, "dp", [(0, 1), (1, 0)])


def move_section(value, step, flip_dp=False):
    sections = lax.axis_size("section")
    halves = lax.axis_size("dp")
    route = []
    for s in range(sections):
        if 0 <= s + step < sections:
            for d in range(halves):
                to = 1 - d if flip_dp else d
                route.append((s * halves + d, (s + step) * halves + to))
    return lax.ppermute(value, ("section", "dp"), route)


def route(message, axes="expert"):
    return lax.all_to_all(message, axes, split_axis=0, concat_axis=0, tiled=True)


def after(value, *earlier):
    return lax.optimization_barrier((value, *earlier))[0]


def body(
    fwd_input,
    back_saved,
    back_grad,
    norm_gain,
    gate_weight,
    up_weight,
    down_weight,
    routes,
    slots,
    affinity,
):
    experts = lax.axis_size("expert")
    tokens = fwd_input.shape[1]
    width = fwd_input.shape[2]
    half = width // 2
    rows = experts * 2 * SLOTS
    side = lax.axis_index("dp")
    both = ("expert", "dp")
    gate_w, up_w, down_w = gate_weight[0, 0], up_weight[0, 0], down_weight[0, 0]
    gain = norm_gain
    gain_half = lax.dynamic_slice(gain, (0, side * half), (1, half))

    x0, s0, s1, g0 = fwd_input[0], back_saved[0, 0], back_saved[1, 0], back_grad[0]

    def inverse_of(value):
        wide = value.astype(F32)
        return lax.rsqrt(jnp.mean(wide * wide, axis=-1) + EPSILON)

    def in_order(own, other):
        return jnp.where(side == 0, own, other), jnp.where(side == 0, other, own)

    def flat(value):
        return jnp.transpose(value, (0, 2, 1)).reshape(8, tokens)

    chosen, held = routes[:, 0], slots[:, 0]
    mixing = affinity[:, 0] / jnp.sum(affinity[:, 0], axis=-1, keepdims=True)
    inverses = jnp.stack([inverse_of(s0), inverse_of(s1), inverse_of(x0)])

    def scalars_of(marks):
        return jnp.concatenate([inverses, flat(marks.astype(F32)), flat(mixing)])

    local = scalars_of(chosen * SLOTS + held)
    own_scalars = scalars_of(chosen * (2 * SLOTS) + side * SLOTS + held)
    table = jnp.concatenate(in_order(own_scalars, swap_dp(own_scalars)), axis=1)
    local_columns = jnp.transpose(local)
    columns = jnp.transpose(table)

    def swap_halves(values):
        stacked = jnp.stack(values)
        own = lax.dynamic_slice_in_dim(stacked, side * half, half, axis=2)
        other = lax.dynamic_slice_in_dim(stacked, (1 - side) * half, half, axis=2)
        a, b = in_order(own, swap_dp(other))
        joined = jnp.concatenate([a, b], axis=1)
        return [joined[i] for i in range(len(values))]

    def full_features(value):
        mine, theirs = in_order(value[:tokens], value[tokens:])
        return jnp.concatenate(in_order(mine, swap_dp(theirs)), axis=1)

    def gradient(saved, inverse_row, grads, weighted, part):
        project = (part + swap_dp(part)) / width
        inverse = columns[:, inverse_row : inverse_row + 1]
        wide = saved.astype(F32)
        return (
            grads.astype(F32) + inverse * (weighted - wide * inverse * inverse * project)
        ).astype(BF16)

    first_sent = spread(
        (("normed", 1), ("grads", 1)), local, local_columns, gain, (s0, g0), experts
    )
    first = route(first_sent, both)
    x0h, s1h = swap_halves([after(x0, first_sent), s1])
    s0h, g0h = swap_halves([after(s0, x0h), g0])
    second_sent = place(
        (("normed", 0, TOKENS), ("normed", 3, SECOND_SAVED)),
        table,
        columns,
        gain_half,
        (x0h, s1h),
        experts,
    )
    second = route(after(second_sent, first, s0h))
    s0_sent, s0_own = partial(after(first, second_sent), 0, 2, (gate_w, up_w), rows, False)
    s0_got = swap_dp(s0_sent)
    g0_sent, g0_own = partial(after(first, s0_sent), 1, 2, (down_w,), rows, True)
    g0_got = swap_dp(g0_sent)
    dexp0 = backward_rest(s0_own, s0_got, g0_own, g0_got, gate_w, up_w, experts)
    x0_sent, x0_own = partial(after(second, g0_got), 0, 2, (gate_w, up_w), rows, False)
    x0_got = swap_dp(x0_sent)
    dexp0_back = route(after(dexp0, x0_sent))
    out0 = forward_rest(x0_own, x0_got, down_w, experts)
    out0_back = route(after(out0, dexp0_back))

    weighted, part = combine_backward(1, dexp0_back, columns, gain_half, s0h)
    first_back = gradient(s0h, FIRST_SAVED, g0h, weighted, part)
    g3h = move_section(first_back, -1)
    s1_sent, s1_own = partial(after(second, first_back), 1, 2, (gate_w, up_w), rows, False)
    g3_placed = place((("grads", 3, None),), table, columns, gain_half, (after(g3h, s1_sent),), experts)
    s1_got = swap_dp(after(s1_sent, g3h))
    g3_rows = route(after(g3_placed, out0_back))

    first_out, square = combine_forward(0, out0_back, columns, x0h)
    x2h = move_section(first_out, 1)
    square_own = move_section(square, 1)
    square_other = move_section(square, 1, flip_dp=True)
    x2_placed = place(
        (("moved", 2, None),), table, columns, gain_half, (x2h, square_own, square_other), experts
    )
    g3_sent, g3_own = partial(after(g3_rows, x2_placed), 0, 1, (down_w,), rows, True)
    x2_rows = route(after(x2_placed, g3_sent, s1_got))

    dexp1 = backward_rest(s1_own, s1_got, g3_own, swap_dp(g3_sent), gate_w, up_w, experts, LONG)
    x2_sent, x2_own = partial(after(x2_rows, dexp1), 0, 1, (gate_w, up_w), rows, False)
    dexp1_back = route(after(dexp1, x2_sent))
    out2 = forward_rest(x2_own, swap_dp(x2_sent), down_w, 2 * experts)
    out2_back = route(after(out2, dexp1_back), both)
    x2 = full_features(after(x2h, dexp1_back))

    weighted, part = combine_backward(3, dexp1_back, columns, gain_half, s1h)
    final_back = full_features(gradient(s1h, SECOND_SAVED, g3h, weighted, part))
    final_out = final_forward(2, out2_back, local_columns, x2)
    return (final_out[None], final_back[None])


def solution(mesh):
    placed = (
        P("section", ("expert", "dp"), None),
        P(None, "section", ("expert", "dp"), None),
        P("section", ("expert", "dp"), None),
        P("section", None),
        P("section", "expert", "dp", None),
        P("section", "expert", "dp", None),
        P("section", "expert", None, "dp"),
        P(None, "section", ("expert", "dp"), None),
        P(None, "section", ("expert", "dp"), None),
        P(None, "section", ("expert", "dp"), None),
    )
    return jax.shard_map(
        body,
        mesh=mesh,
        in_specs=placed,
        out_specs=(P("section", ("expert", "dp"), None), P("section", ("expert", "dp"), None)),
        check_vma=False,
    )
```

```python
import functools

import jax
import jax.numpy as jnp
from jax import lax
from jax.experimental import pallas as pl
from jax.experimental.pallas import tpu as pltpu
from jax.sharding import PartitionSpec as P

ROUTE_SCALE = 2.5
EPSILON = 1e-06
BF16 = jnp.bfloat16
F32 = jnp.float32
SLOTS = 7
LANES = 128
LONG = 200_000_000_000
STEP = 256
FIRST_SAVED, SECOND_SAVED, TOKENS = 0, 1, 2
MARK = 3
MIX = 11


def ceil8(count):
    return -(-count // 8) * 8


def call(kernel, out_shape, scratch, operands, in_hbm=(), anywhere=(), out_hbm=False, cost=1024, name=None):
    def place_of(hbm, free=False):
        return pl.BlockSpec(memory_space=pl.ANY if free else pltpu.HBM if hbm else pltpu.VMEM)

    return pl.pallas_call(
        kernel,
        out_shape=out_shape,
        in_specs=[place_of(i in in_hbm, i in anywhere) for i in range(len(operands))],
        out_specs=jax.tree.map(lambda _: place_of(out_hbm), out_shape),
        scratch_shapes=scratch,
        compiler_params=pltpu.CompilerParams(vmem_limit_bytes=50 * 1024 * 1024),
        cost_estimate=pl.CostEstimate(flops=cost, bytes_accessed=1024, transcendentals=0),
        name=name,
    )(*operands)


def start_copy(source, target, sem):
    copy = pltpu.make_async_copy(source, target, sem)
    copy.start()
    return copy


def struct(shape, dtype):
    return jax.ShapeDtypeStruct(shape, dtype)


def dot(left, right):
    return jnp.dot(left, right, preferred_element_type=F32)


def dot_last(left, right):
    return lax.dot_general(left, right, (((1,), (1,)), ((), ())), preferred_element_type=F32)


def put_columns(pieces, step, value):
    for j in range(STEP // LANES):
        pieces[step * (STEP // LANES) + j] = value[:, j * LANES : (j + 1) * LANES]


def fold(pieces, message, count, base, groups):
    for group, first in groups:
        for c in range(pieces.shape[0]):
            message[group, base + c * count : base + (c + 1) * count, :] = pieces[
                c, first : first + count, :
            ]


def unfold(message, pieces, count, base, groups):
    for group, first in groups:
        for c in range(pieces.shape[0]):
            pieces[c, first : first + count, :] = message[
                group, base + c * count : base + (c + 1) * count, :
            ]


def clear_padding(message, count, base, size):
    used = base + count * size
    if ceil8(used) > used:
        shape = (message.shape[0], ceil8(used) - used, LANES)
        message[:, used : ceil8(used), :] = jnp.zeros(shape, F32)


def join(pieces, rows):
    for c in range(pieces.shape[0]):
        rows[:, c * LANES : (c + 1) * LANES] = pieces[c].astype(BF16)


def widen(source, message, low, high):
    for g in range(message.shape[0]):
        message[g] = source[g, low:high, :].astype(F32)


def narrow(message, out):
    for g in range(message.shape[0]):
        out[g] = message[g].astype(BF16)


def row_selector(marks, rows):
    places = lax.broadcasted_iota(jnp.int32, (rows, marks.shape[1]), 0).astype(F32)
    return jnp.where(places == marks, 1.0, 0.0).astype(BF16)


def token_selector(marks, rows):
    places = lax.broadcasted_iota(jnp.int32, (marks.shape[0], rows), 1).astype(F32)
    return jnp.where(places == marks, 1.0, 0.0).astype(BF16)


def spread_kernel(parts, scalars, columns, gain, *refs):
    count = len(parts)
    values, (out, pieces, message, ready) = refs[:count], refs[count:]
    half = pieces.shape[0] * LANES
    rows = pieces.shape[1]
    size = ceil8(SLOTS * pieces.shape[0])
    for t, ((kind, index), value) in enumerate(zip(parts, values)):
        wide = value[...].astype(F32)
        tokens = wide.shape[0]
        at = MARK + 2 * index
        pick = [row_selector(scalars[at + k : at + k + 1, :], rows) for k in range(2)]
        if kind == "grads":
            chosen = jnp.concatenate(pick, axis=1)
            at = MIX + 2 * index
            for k in range(2):
                mix = columns[:, at + k : at + k + 1]
                ready[k * tokens : (k + 1) * tokens, :] = (ROUTE_SCALE * mix * wide).astype(BF16)
        else:
            chosen = pick[0] + pick[1]
            inverse = lax.rsqrt(jnp.mean(wide * wide, axis=-1, keepdims=True) + EPSILON)
            ready[0:tokens, :] = (wide * inverse * gain[...]).astype(BF16)
        depth = chosen.shape[1]
        for h in range(2):
            for n in range(half // STEP):
                low = h * half + n * STEP
                put_columns(pieces, n, dot(chosen, ready[0:depth, low : low + STEP]))
            fold(
                pieces,
                message,
                SLOTS,
                t * size,
                [(2 * e + h, e * SLOTS) for e in range(rows // SLOTS)],
            )
        clear_padding(message, SLOTS, t * size, pieces.shape[0])
    narrow(message, out)


def spread(parts, scalars, columns, gain, values, experts):
    tokens, width = values[0].shape
    chunks = width // 2 // LANES
    rows = experts * SLOTS
    shape = (2 * experts, len(values) * ceil8(SLOTS * chunks), LANES)
    return call(
        functools.partial(spread_kernel, parts),
        struct(shape, BF16),
        [
            pltpu.VMEM((chunks, rows, LANES), F32),
            pltpu.VMEM(shape, F32),
            pltpu.VMEM((2 * tokens, width), BF16),
        ],
        (scalars, columns, gain, *values),
        name="spread",
    )


def place_kernel(parts, rows, table, columns, gain, *refs):
    *inputs, out, pieces, message, ready = refs
    chunks = pieces.shape[0]
    half = chunks * LANES
    count = 2 * SLOTS
    size = ceil8(count * chunks)
    inputs = iter(inputs)
    for t, (kind, index, inverse_row) in enumerate(parts):
        value = next(inputs)[...].astype(F32)
        tokens = value.shape[0]
        pick = [
            row_selector(table[MARK + 2 * index + k : MARK + 2 * index + k + 1, :], rows)
            for k in range(2)
        ]
        if kind == "grads":
            for k in range(2):
                mix = columns[:, MIX + 2 * index + k : MIX + 2 * index + k + 1]
                ready[k * tokens : (k + 1) * tokens, :] = (ROUTE_SCALE * mix * value).astype(BF16)
            chosen = jnp.concatenate(pick, axis=1)
        else:
            if kind == "normed":
                inverse = columns[:, inverse_row : inverse_row + 1]
            else:
                squares = jnp.sum(value * value, axis=1, keepdims=True) + next(inputs)[...]
                inverse = lax.rsqrt(squares / (2 * half) + EPSILON)
            ready[0:tokens, :] = (value * inverse * gain[...]).astype(BF16)
            chosen = pick[0] + pick[1]
        depth = chosen.shape[1]
        for n in range(half // STEP):
            put_columns(pieces, n, dot(chosen, ready[0:depth, n * STEP : (n + 1) * STEP]))
        fold(
            pieces, message, count, t * size, [(e, e * count) for e in range(rows // count)]
        )
        clear_padding(message, count, t * size, chunks)
    narrow(message, out)


def place(parts, table, columns, gain, inputs, experts):
    tokens, half = inputs[0].shape
    chunks = half // LANES
    rows = experts * 2 * SLOTS
    shape = (experts, len(parts) * ceil8(2 * SLOTS * chunks), LANES)
    return call(
        functools.partial(place_kernel, parts, rows),
        struct(shape, BF16),
        [
            pltpu.VMEM((chunks, rows, LANES), F32),
            pltpu.VMEM(shape, F32),
            pltpu.VMEM((2 * tokens, half), BF16),
        ],
        (table, columns, gain, *inputs),
        name="place",
    )


def message_rows(message):
    array, part, parts = message
    size = array.shape[1] // parts
    low = part * size // 16 * 16
    high = min(array.shape[1], -(-(part + 1) * size // 16) * 16)
    return low, high, part * size - low


def expert_groups(groups, rows):
    return [(g, g * (rows // groups)) for g in range(groups)]


def partial_kernel(bounds, count, last, source, *refs):
    low, high, base = bounds
    weights, (sent, own), refs = refs[:count], refs[count : count + 2], refs[count + 2 :]
    arrived, message, pieces, rows, sent_held, own_held, *held, source_sem, sems, out_sems = refs
    hidden = sent.shape[1] // count
    source_copy = start_copy(source.at[:, pl.ds(low, high - low), :], arrived, source_sem)
    copies, results = [], []
    for n in range(hidden // STEP):
        for w in range(count):
            at = pl.ds(n * STEP, STEP)
            where = (at, slice(None)) if last else (slice(None), at)
            copies.append(start_copy(weights[w].at[where], held[w].at[where], sems.at[w, n]))
    groups = message.shape[0]
    total = rows.shape[0]
    source_copy.wait()
    widen(arrived, message, 0, high - low)
    unfold(message, pieces, total // groups, base, expert_groups(groups, total))
    join(pieces, rows)
    copies = iter(copies)
    for n in range(hidden // STEP):
        for w in range(count):
            next(copies).wait()
            at = slice(n * STEP, (n + 1) * STEP)
            if last:
                result = dot_last(rows[...], held[w][at, :])
            else:
                result = dot(rows[...], held[w][:, at])
            to = (slice(None), pl.ds(w * hidden + n * STEP, STEP))
            own_held[to] = result
            sent_held[to] = result.astype(BF16)
            results.append(start_copy(sent_held.at[to], sent.at[to], out_sems.at[0, w, n]))
            results.append(start_copy(own_held.at[to], own.at[to], out_sems.at[1, w, n]))
    for result in results:
        result.wait()


def partial(source, number, of, weights, rows, last):
    low, high, base = message_rows((source, number, of))
    width, hidden = weights[0].shape[::-1] if last else weights[0].shape
    count = len(weights)
    shape = (rows, count * hidden)
    slab = (source.shape[0], high - low, LANES)
    return call(
        functools.partial(partial_kernel, (low, high, base), count, last),
        (struct(shape, BF16), struct(shape, F32)),
        [
            pltpu.VMEM(slab, BF16),
            pltpu.VMEM(slab, F32),
            pltpu.VMEM((width // LANES, rows, LANES), F32),
            pltpu.VMEM((rows, width), BF16),
            pltpu.VMEM(shape, BF16),
            pltpu.VMEM(shape, F32),
            *[pltpu.VMEM(w.shape, BF16) for w in weights],
            pltpu.SemaphoreType.DMA,
            pltpu.SemaphoreType.DMA((count, hidden // STEP)),
            pltpu.SemaphoreType.DMA((2, count, hidden // STEP)),
        ],
        (source, *weights),
        in_hbm=range(1, 1 + count),
        anywhere=(0,),
        out_hbm=True,
        name="partial",
    )


def finish(message, pieces, groups, out):
    total = pieces.shape[1]
    count = total // groups
    fold(pieces, message, count, 0, expert_groups(groups, total))
    clear_padding(message, count, 0, pieces.shape[0])
    narrow(message, out)


def forward_kernel(
    own, got, weight, out, active, pieces, message, own_held, got_held, held, act_sems, sems
):
    hidden, width = held.shape
    own_copy = start_copy(own, own_held, act_sems.at[0])
    got_copy = start_copy(got, got_held, act_sems.at[1])
    copies = []
    for n in range(width // STEP):
        at = (slice(None), pl.ds(n * STEP, STEP))
        copies.append(start_copy(weight.at[at], held.at[at], sems.at[n]))
    own_copy.wait()
    got_copy.wait()
    for n in range(hidden // STEP):
        a = slice(n * STEP, (n + 1) * STEP)
        b = slice(hidden + n * STEP, hidden + (n + 1) * STEP)
        gate = own_held[:, a] + got_held[:, a].astype(F32)
        upper = own_held[:, b] + got_held[:, b].astype(F32)
        active[:, a] = (gate * jax.nn.sigmoid(gate) * upper).astype(BF16)
    for n in range(width // STEP):
        copies[n].wait()
        put_columns(pieces, n, dot(active[...], held[:, n * STEP : (n + 1) * STEP]))
    finish(message, pieces, out.shape[0], out)


def message_shape(groups, rows, chunks):
    return (groups, ceil8(rows // groups * chunks), LANES)


def forward_rest(own, got, weight, groups):
    rows = own.shape[0]
    hidden, width = weight.shape
    shape = message_shape(groups, rows, width // LANES)
    return call(
        forward_kernel,
        struct(shape, BF16),
        [
            pltpu.VMEM((rows, hidden), BF16),
            pltpu.VMEM((width // LANES, rows, LANES), F32),
            pltpu.VMEM(shape, F32),
            pltpu.VMEM(own.shape, F32),
            pltpu.VMEM(got.shape, BF16),
            pltpu.VMEM(weight.shape, BF16),
            pltpu.SemaphoreType.DMA((2,)),
            pltpu.SemaphoreType.DMA((width // STEP,)),
        ],
        (own, got, weight),
        in_hbm=(0, 2),
        anywhere=(1,),
        cost=LONG,
        name="forward_rest",
    )


def backward_kernel(*refs):
    activations, (gate_w, up_w, out, dgate, dupper, pieces, message), refs = (
        refs[:4],
        refs[4:11],
        refs[11:],
    )
    held, (held_gate, held_up, act_sems, sems) = refs[:4], refs[4:]
    width, hidden = held_gate.shape
    arrivals = [
        start_copy(activations[i], held[i], act_sems.at[i]) for i in range(len(activations))
    ]
    copies = []
    for n in range(width // STEP):
        at = pl.ds(n * STEP, STEP)
        copies.append(start_copy(gate_w.at[at], held_gate.at[at], sems.at[0, n]))
        copies.append(start_copy(up_w.at[at], held_up.at[at], sems.at[1, n]))
    for arrival in arrivals:
        arrival.wait()
    own, got, down_own, down_got = held
    for n in range(hidden // STEP):
        a = slice(n * STEP, (n + 1) * STEP)
        b = slice(hidden + n * STEP, hidden + (n + 1) * STEP)
        gate = own[:, a] + got[:, a].astype(F32)
        upper = own[:, b] + got[:, b].astype(F32)
        dactive = down_own[:, a] + down_got[:, a].astype(F32)
        sigma = jax.nn.sigmoid(gate)
        dgate[:, a] = (dactive * upper * sigma * (1.0 + gate * (1.0 - sigma))).astype(BF16)
        dupper[:, a] = (dactive * gate * sigma).astype(BF16)
    for n in range(width // STEP):
        copies[2 * n].wait()
        copies[2 * n + 1].wait()
        at = slice(n * STEP, (n + 1) * STEP)
        put_columns(
            pieces,
            n,
            dot_last(dgate[...], held_gate[at, :]) + dot_last(dupper[...], held_up[at, :]),
        )
    finish(message, pieces, out.shape[0], out)


def backward_rest(own, got, down_own, down_got, gate_w, up_w, groups, cost=1024):
    rows = own.shape[0]
    width, hidden = gate_w.shape
    shape = message_shape(groups, rows, width // LANES)
    return call(
        backward_kernel,
        struct(shape, BF16),
        [
            pltpu.VMEM((rows, hidden), BF16),
            pltpu.VMEM((rows, hidden), BF16),
            pltpu.VMEM((width // LANES, rows, LANES), F32),
            pltpu.VMEM(shape, F32),
            *[pltpu.VMEM(x.shape, x.dtype) for x in (own, got, down_own, down_got)],
            pltpu.VMEM(gate_w.shape, BF16),
            pltpu.VMEM(up_w.shape, BF16),
            pltpu.SemaphoreType.DMA((4,)),
            pltpu.SemaphoreType.DMA((2, width // STEP)),
        ],
        (own, got, down_own, down_got, gate_w, up_w),
        in_hbm=(0, 2, 4, 5),
        anywhere=(1, 3),
        cost=cost,
        name="backward_rest",
    )


def returned_rows(source, message, pieces, rows):
    widen(source, message, 0, source.shape[1])
    groups = message.shape[0]
    unfold(message, pieces, pieces.shape[1] // groups, 0, expert_groups(groups, pieces.shape[1]))
    join(pieces, rows)


def combine_forward_kernel(index, source, columns, value, out, square, message, pieces, rows):
    returned_rows(source, message, pieces, rows)
    picks, mixes = [], []
    for k in range(2):
        at = 2 * index + k
        picks.append(token_selector(columns[:, MARK + at : MARK + at + 1], rows.shape[0]))
        mixes.append(columns[:, MIX + at : MIX + at + 1])
    total = jnp.zeros((value.shape[0], 1), F32)
    for n in range(value.shape[1] // STEP):
        at = slice(n * STEP, (n + 1) * STEP)
        mixed = mixes[0] * dot(picks[0], rows[:, at]) + mixes[1] * dot(picks[1], rows[:, at])
        result = (value[:, at].astype(F32) + ROUTE_SCALE * mixed).astype(BF16)
        out[:, at] = result
        wide = result.astype(F32)
        total = total + jnp.sum(wide * wide, axis=1, keepdims=True)
    square[...] = total


def returned_scratch(source, rows, half):
    return [
        pltpu.VMEM(source.shape, F32),
        pltpu.VMEM((half // LANES, rows, LANES), F32),
        pltpu.VMEM((rows, half), BF16),
    ]


def combine_forward(index, source, columns, value):
    tokens, half = value.shape
    rows = source.shape[0] * 2 * SLOTS
    return call(
        functools.partial(combine_forward_kernel, index),
        (struct(value.shape, BF16), struct((tokens, 1), F32)),
        returned_scratch(source, rows, half),
        (source, columns, value),
        name="combine_forward",
    )


def combine_backward_kernel(
    index, source, columns, gain, saved, weighted, part, message, pieces, rows
):
    returned_rows(source, message, pieces, rows)
    chosen = sum(
        token_selector(columns[:, MARK + at : MARK + at + 1], rows.shape[0])
        for at in (2 * index, 2 * index + 1)
    )
    total = jnp.zeros((saved.shape[0], 1), F32)
    for n in range(saved.shape[1] // STEP):
        at = slice(n * STEP, (n + 1) * STEP)
        result = dot(chosen, rows[:, at]) * gain[:, at]
        weighted[:, at] = result
        total = total + jnp.sum(result * saved[:, at].astype(F32), axis=1, keepdims=True)
    part[...] = total


def combine_backward(index, source, columns, gain, saved):
    tokens, half = saved.shape
    rows = source.shape[0] * 2 * SLOTS
    return call(
        functools.partial(combine_backward_kernel, index),
        (struct(saved.shape, F32), struct((tokens, 1), F32)),
        returned_scratch(source, rows, half),
        (source, columns, gain, saved),
        name="combine_backward",
    )


def home_rows(source, message, pieces, rows, side):
    groups = [(2 * e + side, e * SLOTS) for e in range(message.shape[0] // 2)]
    unfold(message, pieces, SLOTS, 0, groups)
    join(pieces, rows)


def final_forward_kernel(index, source, columns, value, out, message, pieces, rows):
    widen(source, message, 0, source.shape[1])
    half = rows.shape[1]
    picks, mixes = [], []
    for k in range(2):
        at = 2 * index + k
        picks.append(token_selector(columns[:, MARK + at : MARK + at + 1], rows.shape[0]))
        mixes.append(columns[:, MIX + at : MIX + at + 1])
    for side in range(2):
        home_rows(source, message, pieces, rows, side)
        for n in range(half // STEP):
            low = n * STEP
            at = slice(low, low + STEP)
            to = slice(side * half + low, side * half + low + STEP)
            mixed = mixes[0] * dot(picks[0], rows[:, at]) + mixes[1] * dot(picks[1], rows[:, at])
            out[:, to] = (value[:, to].astype(F32) + ROUTE_SCALE * mixed).astype(BF16)


def final_forward(index, source, columns, value):
    tokens, width = value.shape
    rows = source.shape[0] // 2 * SLOTS
    return call(
        functools.partial(final_forward_kernel, index),
        struct(value.shape, BF16),
        returned_scratch(source, rows, width // 2),
        (source, columns, value),
        name="final_forward",
    )


def swap_dp(value):
    return lax.ppermute(value, "dp", [(0, 1), (1, 0)])


def move_section(value, step, flip_dp=False):
    sections = lax.axis_size("section")
    halves = lax.axis_size("dp")
    route = []
    for s in range(sections):
        if 0 <= s + step < sections:
            for d in range(halves):
                to = 1 - d if flip_dp else d
                route.append((s * halves + d, (s + step) * halves + to))
    return lax.ppermute(value, ("section", "dp"), route)


def route(message, axes="expert"):
    return lax.all_to_all(message, axes, split_axis=0, concat_axis=0, tiled=True)


def after(value, *earlier):
    return lax.optimization_barrier((value, *earlier))[0]


def body(
    fwd_input,
    back_saved,
    back_grad,
    norm_gain,
    gate_weight,
    up_weight,
    down_weight,
    routes,
    slots,
    affinity,
):
    experts = lax.axis_size("expert")
    tokens = fwd_input.shape[1]
    width = fwd_input.shape[2]
    half = width // 2
    rows = experts * 2 * SLOTS
    side = lax.axis_index("dp")
    both = ("expert", "dp")
    gate_w, up_w, down_w = gate_weight[0, 0], up_weight[0, 0], down_weight[0, 0]
    gain = norm_gain
    gain_half = lax.dynamic_slice(gain, (0, side * half), (1, half))

    x0, s0, s1, g0 = fwd_input[0], back_saved[0, 0], back_saved[1, 0], back_grad[0]

    def inverse_of(value):
        wide = value.astype(F32)
        return lax.rsqrt(jnp.mean(wide * wide, axis=-1) + EPSILON)

    def in_order(own, other):
        return jnp.where(side == 0, own, other), jnp.where(side == 0, other, own)

    def flat(value):
        return jnp.transpose(value, (0, 2, 1)).reshape(8, tokens)

    chosen, held = routes[:, 0], slots[:, 0]
    mixing = affinity[:, 0] / jnp.sum(affinity[:, 0], axis=-1, keepdims=True)
    inverses = jnp.stack([inverse_of(s0), inverse_of(s1), inverse_of(x0)])

    def scalars_of(first_rows, marks):
        return jnp.concatenate([first_rows, flat(marks.astype(F32)), flat(mixing)])

    local = scalars_of(jnp.zeros_like(inverses), chosen * SLOTS + held)
    own_scalars = scalars_of(
        after(inverses, local), chosen * (2 * SLOTS) + side * SLOTS + held
    )
    table = jnp.concatenate(in_order(own_scalars, swap_dp(own_scalars)), axis=1)
    local_columns = jnp.transpose(local)
    columns = jnp.transpose(table)

    def swap_halves(values):
        stacked = jnp.stack(values)
        own = lax.dynamic_slice_in_dim(stacked, side * half, half, axis=2)
        other = lax.dynamic_slice_in_dim(stacked, (1 - side) * half, half, axis=2)
        a, b = in_order(own, swap_dp(other))
        joined = jnp.concatenate([a, b], axis=1)
        return [joined[i] for i in range(len(values))]

    def full_features(value):
        mine, theirs = in_order(value[:tokens], value[tokens:])
        return jnp.concatenate(in_order(mine, swap_dp(theirs)), axis=1)

    def gradient(saved, inverse_row, grads, weighted, part):
        project = (part + swap_dp(part)) / width
        inverse = columns[:, inverse_row : inverse_row + 1]
        wide = saved.astype(F32)
        return (
            grads.astype(F32) + inverse * (weighted - wide * inverse * inverse * project)
        ).astype(BF16)

    first_sent = spread(
        (("normed", 1), ("grads", 1)), local, local_columns, gain, (s0, g0), experts
    )
    first = route(first_sent, both)
    x0h, s1h, s0h, g0h = swap_halves([after(x0, first_sent), s1, s0, g0])
    second_sent = place(
        (("normed", 0, TOKENS), ("normed", 3, SECOND_SAVED)),
        table,
        columns,
        gain_half,
        (x0h, s1h),
        experts,
    )
    second = route(after(second_sent, first))
    s0_sent, s0_own = partial(after(first, second_sent), 0, 2, (gate_w, up_w), rows, False)
    s0_got = swap_dp(s0_sent)
    g0_sent, g0_own = partial(after(first, s0_sent), 1, 2, (down_w,), rows, True)
    g0_got = swap_dp(g0_sent)
    dexp0 = backward_rest(s0_own, s0_got, g0_own, g0_got, gate_w, up_w, experts)
    x0_sent, x0_own = partial(after(second, g0_got), 0, 2, (gate_w, up_w), rows, False)
    x0_got = swap_dp(x0_sent)
    dexp0_back = route(after(dexp0, x0_sent))
    out0 = forward_rest(x0_own, x0_got, down_w, experts)
    out0_back = route(after(out0, dexp0_back))

    weighted, part = combine_backward(1, dexp0_back, columns, gain_half, s0h)
    first_back = gradient(s0h, FIRST_SAVED, g0h, weighted, part)
    g3h = move_section(first_back, -1)
    s1_sent, s1_own = partial(after(second, first_back), 1, 2, (gate_w, up_w), rows, False)
    g3_placed = place((("grads", 3, None),), table, columns, gain_half, (after(g3h, s1_sent),), experts)
    g3_rows = route(after(g3_placed, out0_back))

    first_out, square = combine_forward(0, out0_back, columns, x0h)
    x2h = move_section(first_out, 1)
    square_other = move_section(square, 1, flip_dp=True)
    x2_placed = place(
        (("moved", 2, None),), table, columns, gain_half, (x2h, square_other), experts
    )
    g3_sent, g3_own = partial(after(g3_rows, x2_placed), 0, 1, (down_w,), rows, True)
    s1_got = swap_dp(after(s1_sent, x2h, square_other))
    x2_rows = route(after(x2_placed, g3_sent))

    dexp1 = backward_rest(s1_own, s1_got, g3_own, swap_dp(g3_sent), gate_w, up_w, experts, LONG)
    x2_sent, x2_own = partial(after(x2_rows, dexp1), 0, 1, (gate_w, up_w), rows, False)
    dexp1_back = route(after(dexp1, x2_sent))
    out2 = forward_rest(x2_own, swap_dp(x2_sent), down_w, 2 * experts)
    out2_back = route(after(out2, dexp1_back), both)

    weighted, part = combine_backward(3, after(dexp1_back, out2), columns, gain_half, s1h)
    final_back = full_features(gradient(s1h, SECOND_SAVED, g3h, weighted, part))
    x2 = full_features(after(x2h, dexp1_back))
    final_out = final_forward(2, out2_back, local_columns, x2)
    return (final_out[None], final_back[None])


def solution(mesh):
    placed = (
        P("section", ("expert", "dp"), None),
        P(None, "section", ("expert", "dp"), None),
        P("section", ("expert", "dp"), None),
        P("section", None),
        P("section", "expert", "dp", None),
        P("section", "expert", "dp", None),
        P("section", "expert", None, "dp"),
        P(None, "section", ("expert", "dp"), None),
        P(None, "section", ("expert", "dp"), None),
        P(None, "section", ("expert", "dp"), None),
    )
    return jax.shard_map(
        body,
        mesh=mesh,
        in_specs=placed,
        out_specs=(P("section", ("expert", "dp"), None), P("section", ("expert", "dp"), None)),
        check_vma=False,
    )
```

```python
import functools

import jax
import jax.numpy as jnp
from jax import lax
from jax.experimental import pallas as pl
from jax.experimental.pallas import tpu as pltpu
from jax.sharding import PartitionSpec as P

ROUTE_SCALE = 2.5
EPSILON = 1e-06
BF16 = jnp.bfloat16
F32 = jnp.float32
SLOTS = 7
LANES = 128
LONG = 200_000_000_000
STEP = 256
FIRST_SAVED, SECOND_SAVED, TOKENS = 0, 1, 2
MARK = 3
MIX = 11


def ceil8(count):
    return -(-count // 8) * 8


def call(kernel, out_shape, scratch, operands, in_hbm=(), anywhere=(), out_hbm=False, cost=1024, name=None):
    def place_of(hbm, free=False):
        return pl.BlockSpec(memory_space=pl.ANY if free else pltpu.HBM if hbm else pltpu.VMEM)

    return pl.pallas_call(
        kernel,
        out_shape=out_shape,
        in_specs=[place_of(i in in_hbm, i in anywhere) for i in range(len(operands))],
        out_specs=jax.tree.map(lambda _: place_of(out_hbm), out_shape),
        scratch_shapes=scratch,
        compiler_params=pltpu.CompilerParams(vmem_limit_bytes=50 * 1024 * 1024),
        cost_estimate=pl.CostEstimate(flops=cost, bytes_accessed=1024, transcendentals=0),
        name=name,
    )(*operands)


def start_copy(source, target, sem):
    copy = pltpu.make_async_copy(source, target, sem)
    copy.start()
    return copy


def struct(shape, dtype):
    return jax.ShapeDtypeStruct(shape, dtype)


def dot(left, right):
    return jnp.dot(left, right, preferred_element_type=F32)


def dot_last(left, right):
    return lax.dot_general(left, right, (((1,), (1,)), ((), ())), preferred_element_type=F32)


def put_columns(pieces, step, value):
    for j in range(STEP // LANES):
        pieces[step * (STEP // LANES) + j] = value[:, j * LANES : (j + 1) * LANES]


def fold(pieces, message, count, base, groups):
    for group, first in groups:
        for c in range(pieces.shape[0]):
            message[group, base + c * count : base + (c + 1) * count, :] = pieces[
                c, first : first + count, :
            ]


def unfold(message, pieces, count, base, groups):
    for group, first in groups:
        for c in range(pieces.shape[0]):
            pieces[c, first : first + count, :] = message[
                group, base + c * count : base + (c + 1) * count, :
            ]


def clear_padding(message, count, base, size):
    used = base + count * size
    if ceil8(used) > used:
        shape = (message.shape[0], ceil8(used) - used, LANES)
        message[:, used : ceil8(used), :] = jnp.zeros(shape, F32)


def join(pieces, rows):
    for c in range(pieces.shape[0]):
        rows[:, c * LANES : (c + 1) * LANES] = pieces[c].astype(BF16)


def widen(source, message, low, high):
    for g in range(message.shape[0]):
        message[g] = source[g, low:high, :].astype(F32)


def narrow(message, out):
    for g in range(message.shape[0]):
        out[g] = message[g].astype(BF16)


def row_selector(marks, rows):
    places = lax.broadcasted_iota(jnp.int32, (rows, marks.shape[1]), 0).astype(F32)
    return jnp.where(places == marks, 1.0, 0.0).astype(BF16)


def token_selector(marks, rows):
    places = lax.broadcasted_iota(jnp.int32, (marks.shape[0], rows), 1).astype(F32)
    return jnp.where(places == marks, 1.0, 0.0).astype(BF16)


def spread_kernel(parts, scalars, columns, gain, *refs):
    count = len(parts)
    values, (out, pieces, message, ready) = refs[:count], refs[count:]
    half = pieces.shape[0] * LANES
    rows = pieces.shape[1]
    size = ceil8(SLOTS * pieces.shape[0])
    for t, ((kind, index), value) in enumerate(zip(parts, values)):
        wide = value[...].astype(F32)
        tokens = wide.shape[0]
        at = MARK + 2 * index
        pick = [row_selector(scalars[at + k : at + k + 1, :], rows) for k in range(2)]
        if kind == "grads":
            chosen = jnp.concatenate(pick, axis=1)
            at = MIX + 2 * index
            for k in range(2):
                mix = columns[:, at + k : at + k + 1]
                ready[k * tokens : (k + 1) * tokens, :] = (ROUTE_SCALE * mix * wide).astype(BF16)
        else:
            chosen = pick[0] + pick[1]
            inverse = lax.rsqrt(jnp.mean(wide * wide, axis=-1, keepdims=True) + EPSILON)
            ready[0:tokens, :] = (wide * inverse * gain[...]).astype(BF16)
        depth = chosen.shape[1]
        for h in range(2):
            for n in range(half // STEP):
                low = h * half + n * STEP
                put_columns(pieces, n, dot(chosen, ready[0:depth, low : low + STEP]))
            fold(
                pieces,
                message,
                SLOTS,
                t * size,
                [(2 * e + h, e * SLOTS) for e in range(rows // SLOTS)],
            )
        clear_padding(message, SLOTS, t * size, pieces.shape[0])
    narrow(message, out)


def spread(parts, scalars, columns, gain, values, experts):
    tokens, width = values[0].shape
    chunks = width // 2 // LANES
    rows = experts * SLOTS
    shape = (2 * experts, len(values) * ceil8(SLOTS * chunks), LANES)
    return call(
        functools.partial(spread_kernel, parts),
        struct(shape, BF16),
        [
            pltpu.VMEM((chunks, rows, LANES), F32),
            pltpu.VMEM(shape, F32),
            pltpu.VMEM((2 * tokens, width), BF16),
        ],
        (scalars, columns, gain, *values),
        name="spread",
    )


def place_kernel(parts, rows, table, columns, gain, *refs):
    *inputs, out, pieces, message, ready = refs
    chunks = pieces.shape[0]
    half = chunks * LANES
    count = 2 * SLOTS
    size = ceil8(count * chunks)
    inputs = iter(inputs)
    for t, (kind, index, inverse_row) in enumerate(parts):
        value = next(inputs)[...].astype(F32)
        tokens = value.shape[0]
        pick = [
            row_selector(table[MARK + 2 * index + k : MARK + 2 * index + k + 1, :], rows)
            for k in range(2)
        ]
        if kind == "grads":
            for k in range(2):
                mix = columns[:, MIX + 2 * index + k : MIX + 2 * index + k + 1]
                ready[k * tokens : (k + 1) * tokens, :] = (ROUTE_SCALE * mix * value).astype(BF16)
            chosen = jnp.concatenate(pick, axis=1)
        else:
            if kind == "normed":
                inverse = columns[:, inverse_row : inverse_row + 1]
            else:
                squares = jnp.sum(value * value, axis=1, keepdims=True) + next(inputs)[...]
                inverse = lax.rsqrt(squares / (2 * half) + EPSILON)
            ready[0:tokens, :] = (value * inverse * gain[...]).astype(BF16)
            chosen = pick[0] + pick[1]
        depth = chosen.shape[1]
        for n in range(half // STEP):
            put_columns(pieces, n, dot(chosen, ready[0:depth, n * STEP : (n + 1) * STEP]))
        fold(
            pieces, message, count, t * size, [(e, e * count) for e in range(rows // count)]
        )
        clear_padding(message, count, t * size, chunks)
    narrow(message, out)


def place(parts, table, columns, gain, inputs, experts):
    tokens, half = inputs[0].shape
    chunks = half // LANES
    rows = experts * 2 * SLOTS
    shape = (experts, len(parts) * ceil8(2 * SLOTS * chunks), LANES)
    return call(
        functools.partial(place_kernel, parts, rows),
        struct(shape, BF16),
        [
            pltpu.VMEM((chunks, rows, LANES), F32),
            pltpu.VMEM(shape, F32),
            pltpu.VMEM((2 * tokens, half), BF16),
        ],
        (table, columns, gain, *inputs),
        name="place",
    )


def message_rows(message):
    array, part, parts = message
    size = array.shape[1] // parts
    low = part * size // 16 * 16
    high = min(array.shape[1], -(-(part + 1) * size // 16) * 16)
    return low, high, part * size - low


def expert_groups(groups, rows):
    return [(g, g * (rows // groups)) for g in range(groups)]


def partial_kernel(bounds, count, last, source, *refs):
    low, high, base = bounds
    weights, (sent, own), refs = refs[:count], refs[count : count + 2], refs[count + 2 :]
    arrived, message, pieces, rows, sent_held, own_held, *held, source_sem, sems, out_sems = refs
    hidden = sent.shape[1] // count
    source_copy = start_copy(source.at[:, pl.ds(low, high - low), :], arrived, source_sem)
    copies, results = [], []
    for n in range(hidden // STEP):
        for w in range(count):
            at = pl.ds(n * STEP, STEP)
            where = (at, slice(None)) if last else (slice(None), at)
            copies.append(start_copy(weights[w].at[where], held[w].at[where], sems.at[w, n]))
    groups = message.shape[0]
    total = rows.shape[0]
    source_copy.wait()
    widen(arrived, message, 0, high - low)
    unfold(message, pieces, total // groups, base, expert_groups(groups, total))
    join(pieces, rows)
    copies = iter(copies)
    for n in range(hidden // STEP):
        for w in range(count):
            next(copies).wait()
            at = slice(n * STEP, (n + 1) * STEP)
            if last:
                result = dot_last(rows[...], held[w][at, :])
            else:
                result = dot(rows[...], held[w][:, at])
            to = (slice(None), pl.ds(w * hidden + n * STEP, STEP))
            own_held[to] = result
            sent_held[to] = result.astype(BF16)
            results.append(start_copy(sent_held.at[to], sent.at[to], out_sems.at[0, w, n]))
            results.append(start_copy(own_held.at[to], own.at[to], out_sems.at[1, w, n]))
    for result in results:
        result.wait()


def partial(source, number, of, weights, rows, last):
    low, high, base = message_rows((source, number, of))
    width, hidden = weights[0].shape[::-1] if last else weights[0].shape
    count = len(weights)
    shape = (rows, count * hidden)
    slab = (source.shape[0], high - low, LANES)
    return call(
        functools.partial(partial_kernel, (low, high, base), count, last),
        (struct(shape, BF16), struct(shape, F32)),
        [
            pltpu.VMEM(slab, BF16),
            pltpu.VMEM(slab, F32),
            pltpu.VMEM((width // LANES, rows, LANES), F32),
            pltpu.VMEM((rows, width), BF16),
            pltpu.VMEM(shape, BF16),
            pltpu.VMEM(shape, F32),
            *[pltpu.VMEM(w.shape, BF16) for w in weights],
            pltpu.SemaphoreType.DMA,
            pltpu.SemaphoreType.DMA((count, hidden // STEP)),
            pltpu.SemaphoreType.DMA((2, count, hidden // STEP)),
        ],
        (source, *weights),
        in_hbm=range(1, 1 + count),
        anywhere=(0,),
        out_hbm=True,
        name="partial",
    )


def finish(message, pieces, groups, out):
    total = pieces.shape[1]
    count = total // groups
    fold(pieces, message, count, 0, expert_groups(groups, total))
    clear_padding(message, count, 0, pieces.shape[0])
    narrow(message, out)


def forward_kernel(
    own, got, weight, out, active, pieces, message, own_held, got_held, held, act_sems, sems
):
    hidden, width = held.shape
    own_copy = start_copy(own, own_held, act_sems.at[0])
    got_copy = start_copy(got, got_held, act_sems.at[1])
    copies = []
    for n in range(width // STEP):
        at = (slice(None), pl.ds(n * STEP, STEP))
        copies.append(start_copy(weight.at[at], held.at[at], sems.at[n]))
    own_copy.wait()
    got_copy.wait()
    for n in range(hidden // STEP):
        a = slice(n * STEP, (n + 1) * STEP)
        b = slice(hidden + n * STEP, hidden + (n + 1) * STEP)
        gate = own_held[:, a] + got_held[:, a].astype(F32)
        upper = own_held[:, b] + got_held[:, b].astype(F32)
        active[:, a] = (gate * jax.nn.sigmoid(gate) * upper).astype(BF16)
    for n in range(width // STEP):
        copies[n].wait()
        put_columns(pieces, n, dot(active[...], held[:, n * STEP : (n + 1) * STEP]))
    finish(message, pieces, out.shape[0], out)


def message_shape(groups, rows, chunks):
    return (groups, ceil8(rows // groups * chunks), LANES)


def forward_rest(own, got, weight, groups, cost=1024):
    rows = own.shape[0]
    hidden, width = weight.shape
    shape = message_shape(groups, rows, width // LANES)
    return call(
        forward_kernel,
        struct(shape, BF16),
        [
            pltpu.VMEM((rows, hidden), BF16),
            pltpu.VMEM((width // LANES, rows, LANES), F32),
            pltpu.VMEM(shape, F32),
            pltpu.VMEM(own.shape, F32),
            pltpu.VMEM(got.shape, BF16),
            pltpu.VMEM(weight.shape, BF16),
            pltpu.SemaphoreType.DMA((2,)),
            pltpu.SemaphoreType.DMA((width // STEP,)),
        ],
        (own, got, weight),
        in_hbm=(0, 2),
        anywhere=(1,),
        cost=cost,
        name="forward_rest",
    )


def backward_kernel(*refs):
    activations, (gate_w, up_w, out, dgate, dupper, pieces, message), refs = (
        refs[:4],
        refs[4:11],
        refs[11:],
    )
    held, (held_gate, held_up, act_sems, sems) = refs[:4], refs[4:]
    width, hidden = held_gate.shape
    arrivals = [
        start_copy(activations[i], held[i], act_sems.at[i]) for i in range(len(activations))
    ]
    copies = []
    for n in range(width // STEP):
        at = pl.ds(n * STEP, STEP)
        copies.append(start_copy(gate_w.at[at], held_gate.at[at], sems.at[0, n]))
        copies.append(start_copy(up_w.at[at], held_up.at[at], sems.at[1, n]))
    for arrival in arrivals:
        arrival.wait()
    own, got, down_own, down_got = held
    for n in range(hidden // STEP):
        a = slice(n * STEP, (n + 1) * STEP)
        b = slice(hidden + n * STEP, hidden + (n + 1) * STEP)
        gate = own[:, a] + got[:, a].astype(F32)
        upper = own[:, b] + got[:, b].astype(F32)
        dactive = down_own[:, a] + down_got[:, a].astype(F32)
        sigma = jax.nn.sigmoid(gate)
        dgate[:, a] = (dactive * upper * sigma * (1.0 + gate * (1.0 - sigma))).astype(BF16)
        dupper[:, a] = (dactive * gate * sigma).astype(BF16)
    for n in range(width // STEP):
        copies[2 * n].wait()
        copies[2 * n + 1].wait()
        at = slice(n * STEP, (n + 1) * STEP)
        put_columns(
            pieces,
            n,
            dot_last(dgate[...], held_gate[at, :]) + dot_last(dupper[...], held_up[at, :]),
        )
    finish(message, pieces, out.shape[0], out)


def backward_rest(own, got, down_own, down_got, gate_w, up_w, groups, cost=1024):
    rows = own.shape[0]
    width, hidden = gate_w.shape
    shape = message_shape(groups, rows, width // LANES)
    return call(
        backward_kernel,
        struct(shape, BF16),
        [
            pltpu.VMEM((rows, hidden), BF16),
            pltpu.VMEM((rows, hidden), BF16),
            pltpu.VMEM((width // LANES, rows, LANES), F32),
            pltpu.VMEM(shape, F32),
            *[pltpu.VMEM(x.shape, x.dtype) for x in (own, got, down_own, down_got)],
            pltpu.VMEM(gate_w.shape, BF16),
            pltpu.VMEM(up_w.shape, BF16),
            pltpu.SemaphoreType.DMA((4,)),
            pltpu.SemaphoreType.DMA((2, width // STEP)),
        ],
        (own, got, down_own, down_got, gate_w, up_w),
        in_hbm=(0, 2, 4, 5),
        anywhere=(1, 3),
        cost=cost,
        name="backward_rest",
    )


def returned_rows(source, message, pieces, rows):
    widen(source, message, 0, source.shape[1])
    groups = message.shape[0]
    unfold(message, pieces, pieces.shape[1] // groups, 0, expert_groups(groups, pieces.shape[1]))
    join(pieces, rows)


def combine_forward_kernel(index, source, columns, value, out, square, message, pieces, rows):
    returned_rows(source, message, pieces, rows)
    picks, mixes = [], []
    for k in range(2):
        at = 2 * index + k
        picks.append(token_selector(columns[:, MARK + at : MARK + at + 1], rows.shape[0]))
        mixes.append(columns[:, MIX + at : MIX + at + 1])
    total = jnp.zeros((value.shape[0], 1), F32)
    for n in range(value.shape[1] // STEP):
        at = slice(n * STEP, (n + 1) * STEP)
        mixed = mixes[0] * dot(picks[0], rows[:, at]) + mixes[1] * dot(picks[1], rows[:, at])
        result = (value[:, at].astype(F32) + ROUTE_SCALE * mixed).astype(BF16)
        out[:, at] = result
        wide = result.astype(F32)
        total = total + jnp.sum(wide * wide, axis=1, keepdims=True)
    square[...] = total


def returned_scratch(source, rows, half):
    return [
        pltpu.VMEM(source.shape, F32),
        pltpu.VMEM((half // LANES, rows, LANES), F32),
        pltpu.VMEM((rows, half), BF16),
    ]


def combine_forward(index, source, columns, value):
    tokens, half = value.shape
    rows = source.shape[0] * 2 * SLOTS
    return call(
        functools.partial(combine_forward_kernel, index),
        (struct(value.shape, BF16), struct((tokens, 1), F32)),
        returned_scratch(source, rows, half),
        (source, columns, value),
        name="combine_forward",
    )


def combine_backward_kernel(
    index, source, columns, gain, saved, weighted, part, message, pieces, rows
):
    returned_rows(source, message, pieces, rows)
    chosen = sum(
        token_selector(columns[:, MARK + at : MARK + at + 1], rows.shape[0])
        for at in (2 * index, 2 * index + 1)
    )
    total = jnp.zeros((saved.shape[0], 1), F32)
    for n in range(saved.shape[1] // STEP):
        at = slice(n * STEP, (n + 1) * STEP)
        result = dot(chosen, rows[:, at]) * gain[:, at]
        weighted[:, at] = result
        total = total + jnp.sum(result * saved[:, at].astype(F32), axis=1, keepdims=True)
    part[...] = total


def combine_backward(index, source, columns, gain, saved):
    tokens, half = saved.shape
    rows = source.shape[0] * 2 * SLOTS
    return call(
        functools.partial(combine_backward_kernel, index),
        (struct(saved.shape, F32), struct((tokens, 1), F32)),
        returned_scratch(source, rows, half),
        (source, columns, gain, saved),
        name="combine_backward",
    )


def home_rows(source, message, pieces, rows, side):
    groups = [(2 * e + side, e * SLOTS) for e in range(message.shape[0] // 2)]
    unfold(message, pieces, SLOTS, 0, groups)
    join(pieces, rows)


def final_backward_kernel(
    index, source, columns, gain, saved, grads, out, message, pieces, rows, weighted
):
    widen(source, message, 0, source.shape[1])
    half = rows.shape[1]
    chosen = sum(
        token_selector(columns[:, MARK + at : MARK + at + 1], rows.shape[0])
        for at in (2 * index, 2 * index + 1)
    )
    total = jnp.zeros((saved.shape[0], 1), F32)
    squares = jnp.zeros((saved.shape[0], 1), F32)
    for side in range(2):
        home_rows(source, message, pieces, rows, side)
        for n in range(half // STEP):
            low = n * STEP
            to = slice(side * half + low, side * half + low + STEP)
            result = dot(chosen, rows[:, low : low + STEP]) * gain[:, to]
            weighted[:, to] = result
            wide = saved[:, to].astype(F32)
            total = total + jnp.sum(result * wide, axis=1, keepdims=True)
            squares = squares + jnp.sum(wide * wide, axis=1, keepdims=True)
    project = total / (2 * half)
    inverse = lax.rsqrt(squares / (2 * half) + EPSILON)
    for n in range(2 * half // STEP):
        at = slice(n * STEP, (n + 1) * STEP)
        wide = saved[:, at].astype(F32)
        out[:, at] = (
            grads[:, at].astype(F32)
            + inverse * (weighted[:, at] - wide * inverse * inverse * project)
        ).astype(BF16)


def final_backward(index, source, columns, gain, saved, grads):
    tokens, width = saved.shape
    rows = source.shape[0] // 2 * SLOTS
    return call(
        functools.partial(final_backward_kernel, index),
        struct(saved.shape, BF16),
        [*returned_scratch(source, rows, width // 2), pltpu.VMEM((tokens, width), F32)],
        (source, columns, gain, saved, grads),
        name="final_backward",
    )


def swap_dp(value):
    return lax.ppermute(value, "dp", [(0, 1), (1, 0)])


def move_section(value, step, flip_dp=False):
    sections = lax.axis_size("section")
    halves = lax.axis_size("dp")
    route = []
    for s in range(sections):
        if 0 <= s + step < sections:
            for d in range(halves):
                to = 1 - d if flip_dp else d
                route.append((s * halves + d, (s + step) * halves + to))
    return lax.ppermute(value, ("section", "dp"), route)


def route(message, axes="expert"):
    return lax.all_to_all(message, axes, split_axis=0, concat_axis=0, tiled=True)


def after(value, *earlier):
    return lax.optimization_barrier((value, *earlier))[0]


def body(
    fwd_input,
    back_saved,
    back_grad,
    norm_gain,
    gate_weight,
    up_weight,
    down_weight,
    routes,
    slots,
    affinity,
):
    experts = lax.axis_size("expert")
    tokens = fwd_input.shape[1]
    width = fwd_input.shape[2]
    half = width // 2
    rows = experts * 2 * SLOTS
    side = lax.axis_index("dp")
    both = ("expert", "dp")
    gate_w, up_w, down_w = gate_weight[0, 0], up_weight[0, 0], down_weight[0, 0]
    gain = norm_gain
    gain_half = lax.dynamic_slice(gain, (0, side * half), (1, half))

    x0, s0, s1, g0 = fwd_input[0], back_saved[0, 0], back_saved[1, 0], back_grad[0]

    def inverse_of(value):
        wide = value.astype(F32)
        return lax.rsqrt(jnp.mean(wide * wide, axis=-1) + EPSILON)

    def in_order(own, other):
        return jnp.where(side == 0, own, other), jnp.where(side == 0, other, own)

    def flat(value):
        return jnp.transpose(value, (0, 2, 1)).reshape(8, tokens)

    chosen, held = routes[:, 0], slots[:, 0]
    mixing = affinity[:, 0] / jnp.sum(affinity[:, 0], axis=-1, keepdims=True)
    inverses = jnp.stack([inverse_of(s0), inverse_of(s1), inverse_of(x0)])

    def scalars_of(first_rows, marks):
        return jnp.concatenate([first_rows, flat(marks.astype(F32)), flat(mixing)])

    local = scalars_of(jnp.zeros_like(inverses), chosen * SLOTS + held)
    own_scalars = scalars_of(
        after(inverses, local), chosen * (2 * SLOTS) + side * SLOTS + held
    )
    table = jnp.concatenate(in_order(own_scalars, swap_dp(own_scalars)), axis=1)
    local_columns = jnp.transpose(local)
    columns = jnp.transpose(table)

    def swap_halves(values):
        stacked = jnp.stack(values)
        own = lax.dynamic_slice_in_dim(stacked, side * half, half, axis=2)
        other = lax.dynamic_slice_in_dim(stacked, (1 - side) * half, half, axis=2)
        a, b = in_order(own, swap_dp(other))
        joined = jnp.concatenate([a, b], axis=1)
        return [joined[i] for i in range(len(values))]

    def full_features(value):
        mine, theirs = in_order(value[:tokens], value[tokens:])
        return jnp.concatenate(in_order(mine, swap_dp(theirs)), axis=1)

    def gradient(saved, inverse_row, grads, weighted, part):
        project = (part + swap_dp(part)) / width
        inverse = columns[:, inverse_row : inverse_row + 1]
        wide = saved.astype(F32)
        return (
            grads.astype(F32) + inverse * (weighted - wide * inverse * inverse * project)
        ).astype(BF16)

    first_sent = spread(
        (("normed", 0), ("normed", 1)), local, local_columns, gain, (x0, s0), experts
    )
    first = route(first_sent, both)
    g0h, s1h, x0h, s0h = swap_halves([after(g0, first_sent), s1, x0, s0])
    second_sent = place(
        (("grads", 1, None), ("normed", 3, SECOND_SAVED)),
        table,
        columns,
        gain_half,
        (g0h, s1h),
        experts,
    )
    second = route(after(second_sent, first))
    x0_sent, x0_own = partial(after(first, second_sent), 0, 2, (gate_w, up_w), rows, False)
    x0_got = swap_dp(x0_sent)
    s0_sent, s0_own = partial(after(first, x0_sent), 1, 2, (gate_w, up_w), rows, False)
    out0 = forward_rest(x0_own, after(x0_got, s0_sent), down_w, experts)
    s0_got = swap_dp(after(s0_sent, x0_got))
    out0_back = route(after(out0, second))
    g0_sent, g0_own = partial(after(second, out0), 0, 2, (down_w,), rows, True)
    g0_got = swap_dp(g0_sent)
    dexp0 = backward_rest(s0_own, s0_got, g0_own, g0_got, gate_w, up_w, experts, LONG)
    dexp0_back = route(after(dexp0, out0_back))

    first_out, square = combine_forward(0, after(out0_back, dexp0), columns, x0h)
    x2h = move_section(first_out, 1)
    square_other = move_section(square, 1, flip_dp=True)
    s1_sent, s1_own = partial(after(second, first_out), 1, 2, (gate_w, up_w), rows, False)
    x2_placed = place(
        (("moved", 2, None),),
        table,
        columns,
        gain_half,
        (after(x2h, s1_sent), square_other),
        experts,
    )
    s1_got = swap_dp(after(s1_sent, x2h, square_other))
    x2_rows = route(after(x2_placed, dexp0_back))

    weighted, part = combine_backward(
        1, after(dexp0_back, s1_got), columns, gain_half, s0h
    )
    g3h = move_section(gradient(s0h, FIRST_SAVED, g0h, weighted, part), -1)
    g3_placed = place((("grads", 3, None),), table, columns, gain_half, (g3h,), experts)
    x2_sent, x2_own = partial(after(x2_rows, g3_placed), 0, 1, (gate_w, up_w), rows, False)
    g3_rows = route(after(g3_placed, x2_sent))

    out2 = forward_rest(x2_own, swap_dp(x2_sent), down_w, experts, LONG)
    g3_sent, g3_own = partial(after(g3_rows, out2), 0, 1, (down_w,), rows, True)
    out2_back = route(after(out2, g3_sent))
    dexp1 = backward_rest(
        s1_own, s1_got, g3_own, swap_dp(g3_sent), gate_w, up_w, 2 * experts, LONG
    )
    dexp1_back = route(after(dexp1, out2_back), both)

    final_half, _ = combine_forward(2, after(out2_back, dexp1), columns, x2h)
    final_out = full_features(final_half)
    g3 = full_features(after(g3h, out2_back))
    final_back = final_backward(3, dexp1_back, local_columns, gain, s1, g3)
    return (final_out[None], final_back[None])


def solution(mesh):
    placed = (
        P("section", ("expert", "dp"), None),
        P(None, "section", ("expert", "dp"), None),
        P("section", ("expert", "dp"), None),
        P("section", None),
        P("section", "expert", "dp", None),
        P("section", "expert", "dp", None),
        P("section", "expert", None, "dp"),
        P(None, "section", ("expert", "dp"), None),
        P(None, "section", ("expert", "dp"), None),
        P(None, "section", ("expert", "dp"), None),
    )
    return jax.shard_map(
        body,
        mesh=mesh,
        in_specs=placed,
        out_specs=(P("section", ("expert", "dp"), None), P("section", ("expert", "dp"), None)),
        check_vma=False,
    )
```

```python
import functools

import jax
import jax.numpy as jnp
from jax import lax
from jax.experimental import pallas as pl
from jax.experimental.pallas import tpu as pltpu
from jax.sharding import PartitionSpec as P

ROUTE_SCALE = 2.5
EPSILON = 1e-06
BF16 = jnp.bfloat16
F32 = jnp.float32
SLOTS = 7
LANES = 128
LONG = 200_000_000_000
STEP = 256
FIRST_SAVED, SECOND_SAVED, TOKENS = 0, 1, 2
MARK = 3
MIX = 11


def ceil8(count):
    return -(-count // 8) * 8


def call(kernel, out_shape, scratch, operands, in_hbm=(), anywhere=(), out_hbm=False, cost=1024, name=None):
    def place_of(hbm, free=False):
        return pl.BlockSpec(memory_space=pl.ANY if free else pltpu.HBM if hbm else pltpu.VMEM)

    return pl.pallas_call(
        kernel,
        out_shape=out_shape,
        in_specs=[place_of(i in in_hbm, i in anywhere) for i in range(len(operands))],
        out_specs=jax.tree.map(lambda _: place_of(out_hbm), out_shape),
        scratch_shapes=scratch,
        compiler_params=pltpu.CompilerParams(vmem_limit_bytes=50 * 1024 * 1024),
        cost_estimate=pl.CostEstimate(flops=cost, bytes_accessed=1024, transcendentals=0),
        name=name,
    )(*operands)


def start_copy(source, target, sem):
    copy = pltpu.make_async_copy(source, target, sem)
    copy.start()
    return copy


def struct(shape, dtype):
    return jax.ShapeDtypeStruct(shape, dtype)


def dot(left, right):
    return jnp.dot(left, right, preferred_element_type=F32)


def dot_last(left, right):
    return lax.dot_general(left, right, (((1,), (1,)), ((), ())), preferred_element_type=F32)


def put_columns(pieces, step, value):
    for j in range(STEP // LANES):
        pieces[step * (STEP // LANES) + j] = value[:, j * LANES : (j + 1) * LANES]


def fold(pieces, message, count, base, groups):
    for group, first in groups:
        for c in range(pieces.shape[0]):
            message[group, base + c * count : base + (c + 1) * count, :] = pieces[
                c, first : first + count, :
            ]


def unfold(message, pieces, count, base, groups):
    for group, first in groups:
        for c in range(pieces.shape[0]):
            pieces[c, first : first + count, :] = message[
                group, base + c * count : base + (c + 1) * count, :
            ]


def clear_padding(message, count, base, size):
    used = base + count * size
    if ceil8(used) > used:
        shape = (message.shape[0], ceil8(used) - used, LANES)
        message[:, used : ceil8(used), :] = jnp.zeros(shape, F32)


def join(pieces, rows):
    for c in range(pieces.shape[0]):
        rows[:, c * LANES : (c + 1) * LANES] = pieces[c].astype(BF16)


def widen(source, message, low, high):
    for g in range(message.shape[0]):
        message[g] = source[g, low:high, :].astype(F32)


def narrow(message, out):
    for g in range(message.shape[0]):
        out[g] = message[g].astype(BF16)


def row_selector(marks, rows):
    places = lax.broadcasted_iota(jnp.int32, (rows, marks.shape[1]), 0).astype(F32)
    return jnp.where(places == marks, 1.0, 0.0).astype(BF16)


def token_selector(marks, rows):
    places = lax.broadcasted_iota(jnp.int32, (marks.shape[0], rows), 1).astype(F32)
    return jnp.where(places == marks, 1.0, 0.0).astype(BF16)


def spread_kernel(parts, scalars, columns, gain, *refs):
    count = len(parts)
    values, (out, pieces, message, ready) = refs[:count], refs[count:]
    half = pieces.shape[0] * LANES
    rows = pieces.shape[1]
    size = ceil8(SLOTS * pieces.shape[0])
    for t, ((kind, index), value) in enumerate(zip(parts, values)):
        wide = value[...].astype(F32)
        tokens = wide.shape[0]
        at = MARK + 2 * index
        pick = [row_selector(scalars[at + k : at + k + 1, :], rows) for k in range(2)]
        if kind == "grads":
            chosen = jnp.concatenate(pick, axis=1)
            at = MIX + 2 * index
            for k in range(2):
                mix = columns[:, at + k : at + k + 1]
                ready[k * tokens : (k + 1) * tokens, :] = (ROUTE_SCALE * mix * wide).astype(BF16)
        else:
            chosen = pick[0] + pick[1]
            inverse = lax.rsqrt(jnp.mean(wide * wide, axis=-1, keepdims=True) + EPSILON)
            ready[0:tokens, :] = (wide * inverse * gain[...]).astype(BF16)
        depth = chosen.shape[1]
        for h in range(2):
            for n in range(half // STEP):
                low = h * half + n * STEP
                put_columns(pieces, n, dot(chosen, ready[0:depth, low : low + STEP]))
            fold(
                pieces,
                message,
                SLOTS,
                t * size,
                [(2 * e + h, e * SLOTS) for e in range(rows // SLOTS)],
            )
        clear_padding(message, SLOTS, t * size, pieces.shape[0])
    narrow(message, out)


def spread(parts, scalars, columns, gain, values, experts):
    tokens, width = values[0].shape
    chunks = width // 2 // LANES
    rows = experts * SLOTS
    shape = (2 * experts, len(values) * ceil8(SLOTS * chunks), LANES)
    return call(
        functools.partial(spread_kernel, parts),
        struct(shape, BF16),
        [
            pltpu.VMEM((chunks, rows, LANES), F32),
            pltpu.VMEM(shape, F32),
            pltpu.VMEM((2 * tokens, width), BF16),
        ],
        (scalars, columns, gain, *values),
        name="spread",
    )


def place_kernel(parts, rows, table, columns, gain, *refs):
    *inputs, out, pieces, message, ready = refs
    chunks = pieces.shape[0]
    half = chunks * LANES
    count = 2 * SLOTS
    size = ceil8(count * chunks)
    inputs = iter(inputs)
    for t, (kind, index, inverse_row) in enumerate(parts):
        value = next(inputs)[...].astype(F32)
        tokens = value.shape[0]
        pick = [
            row_selector(table[MARK + 2 * index + k : MARK + 2 * index + k + 1, :], rows)
            for k in range(2)
        ]
        if kind == "grads":
            for k in range(2):
                mix = columns[:, MIX + 2 * index + k : MIX + 2 * index + k + 1]
                ready[k * tokens : (k + 1) * tokens, :] = (ROUTE_SCALE * mix * value).astype(BF16)
            chosen = jnp.concatenate(pick, axis=1)
        else:
            if kind == "normed":
                inverse = columns[:, inverse_row : inverse_row + 1]
            else:
                squares = jnp.sum(value * value, axis=1, keepdims=True) + next(inputs)[...]
                inverse = lax.rsqrt(squares / (2 * half) + EPSILON)
            ready[0:tokens, :] = (value * inverse * gain[...]).astype(BF16)
            chosen = pick[0] + pick[1]
        depth = chosen.shape[1]
        for n in range(half // STEP):
            put_columns(pieces, n, dot(chosen, ready[0:depth, n * STEP : (n + 1) * STEP]))
        fold(
            pieces, message, count, t * size, [(e, e * count) for e in range(rows // count)]
        )
        clear_padding(message, count, t * size, chunks)
    narrow(message, out)


def place(parts, table, columns, gain, inputs, experts):
    tokens, half = inputs[0].shape
    chunks = half // LANES
    rows = experts * 2 * SLOTS
    shape = (experts, len(parts) * ceil8(2 * SLOTS * chunks), LANES)
    return call(
        functools.partial(place_kernel, parts, rows),
        struct(shape, BF16),
        [
            pltpu.VMEM((chunks, rows, LANES), F32),
            pltpu.VMEM(shape, F32),
            pltpu.VMEM((2 * tokens, half), BF16),
        ],
        (table, columns, gain, *inputs),
        name="place",
    )


def message_rows(message):
    array, part, parts = message
    size = array.shape[1] // parts
    low = part * size // 16 * 16
    high = min(array.shape[1], -(-(part + 1) * size // 16) * 16)
    return low, high, part * size - low


def expert_groups(groups, rows):
    return [(g, g * (rows // groups)) for g in range(groups)]


def partial_kernel(bounds, count, last, source, *refs):
    low, high, base = bounds
    weights, (sent, own), refs = refs[:count], refs[count : count + 2], refs[count + 2 :]
    arrived, message, pieces, rows, sent_held, own_held, *held, source_sem, sems, out_sems = refs
    hidden = sent.shape[1] // count
    source_copy = start_copy(source.at[:, pl.ds(low, high - low), :], arrived, source_sem)
    copies, results = [], []
    for n in range(hidden // STEP):
        for w in range(count):
            at = pl.ds(n * STEP, STEP)
            where = (at, slice(None)) if last else (slice(None), at)
            copies.append(start_copy(weights[w].at[where], held[w].at[where], sems.at[w, n]))
    groups = message.shape[0]
    total = rows.shape[0]
    source_copy.wait()
    widen(arrived, message, 0, high - low)
    unfold(message, pieces, total // groups, base, expert_groups(groups, total))
    join(pieces, rows)
    copies = iter(copies)
    for n in range(hidden // STEP):
        for w in range(count):
            next(copies).wait()
            at = slice(n * STEP, (n + 1) * STEP)
            if last:
                result = dot_last(rows[...], held[w][at, :])
            else:
                result = dot(rows[...], held[w][:, at])
            to = (slice(None), pl.ds(w * hidden + n * STEP, STEP))
            own_held[to] = result
            sent_held[to] = result.astype(BF16)
            results.append(start_copy(sent_held.at[to], sent.at[to], out_sems.at[0, w, n]))
            results.append(start_copy(own_held.at[to], own.at[to], out_sems.at[1, w, n]))
    for result in results:
        result.wait()


def partial(source, number, of, weights, rows, last):
    low, high, base = message_rows((source, number, of))
    width, hidden = weights[0].shape[::-1] if last else weights[0].shape
    count = len(weights)
    shape = (rows, count * hidden)
    slab = (source.shape[0], high - low, LANES)
    return call(
        functools.partial(partial_kernel, (low, high, base), count, last),
        (struct(shape, BF16), struct(shape, F32)),
        [
            pltpu.VMEM(slab, BF16),
            pltpu.VMEM(slab, F32),
            pltpu.VMEM((width // LANES, rows, LANES), F32),
            pltpu.VMEM((rows, width), BF16),
            pltpu.VMEM(shape, BF16),
            pltpu.VMEM(shape, F32),
            *[pltpu.VMEM(w.shape, BF16) for w in weights],
            pltpu.SemaphoreType.DMA,
            pltpu.SemaphoreType.DMA((count, hidden // STEP)),
            pltpu.SemaphoreType.DMA((2, count, hidden // STEP)),
        ],
        (source, *weights),
        in_hbm=range(1, 1 + count),
        anywhere=(0,),
        out_hbm=True,
        name="partial",
    )


def finish(message, pieces, groups, out):
    total = pieces.shape[1]
    count = total // groups
    fold(pieces, message, count, 0, expert_groups(groups, total))
    clear_padding(message, count, 0, pieces.shape[0])
    narrow(message, out)


def forward_kernel(
    own, got, weight, out, active, pieces, message, own_held, got_held, held, act_sems, sems
):
    hidden, width = held.shape
    own_copy = start_copy(own, own_held, act_sems.at[0])
    got_copy = start_copy(got, got_held, act_sems.at[1])
    copies = []
    for n in range(width // STEP):
        at = (slice(None), pl.ds(n * STEP, STEP))
        copies.append(start_copy(weight.at[at], held.at[at], sems.at[n]))
    own_copy.wait()
    got_copy.wait()
    for n in range(hidden // STEP):
        a = slice(n * STEP, (n + 1) * STEP)
        b = slice(hidden + n * STEP, hidden + (n + 1) * STEP)
        gate = own_held[:, a] + got_held[:, a].astype(F32)
        upper = own_held[:, b] + got_held[:, b].astype(F32)
        active[:, a] = (gate * jax.nn.sigmoid(gate) * upper).astype(BF16)
    for n in range(width // STEP):
        copies[n].wait()
        put_columns(pieces, n, dot(active[...], held[:, n * STEP : (n + 1) * STEP]))
    finish(message, pieces, out.shape[0], out)


def message_shape(groups, rows, chunks):
    return (groups, ceil8(rows // groups * chunks), LANES)


def forward_rest(own, got, weight, groups, cost=1024):
    rows = own.shape[0]
    hidden, width = weight.shape
    shape = message_shape(groups, rows, width // LANES)
    return call(
        forward_kernel,
        struct(shape, BF16),
        [
            pltpu.VMEM((rows, hidden), BF16),
            pltpu.VMEM((width // LANES, rows, LANES), F32),
            pltpu.VMEM(shape, F32),
            pltpu.VMEM(own.shape, F32),
            pltpu.VMEM(got.shape, BF16),
            pltpu.VMEM(weight.shape, BF16),
            pltpu.SemaphoreType.DMA((2,)),
            pltpu.SemaphoreType.DMA((width // STEP,)),
        ],
        (own, got, weight),
        in_hbm=(0, 2),
        anywhere=(1,),
        cost=cost,
        name="forward_rest",
    )


def backward_kernel(*refs):
    activations, (gate_w, up_w, out, dgate, dupper, pieces, message), refs = (
        refs[:4],
        refs[4:11],
        refs[11:],
    )
    held, (held_gate, held_up, act_sems, sems) = refs[:4], refs[4:]
    width, hidden = held_gate.shape
    arrivals = [
        start_copy(activations[i], held[i], act_sems.at[i]) for i in range(len(activations))
    ]
    copies = []
    for n in range(width // STEP):
        at = pl.ds(n * STEP, STEP)
        copies.append(start_copy(gate_w.at[at], held_gate.at[at], sems.at[0, n]))
        copies.append(start_copy(up_w.at[at], held_up.at[at], sems.at[1, n]))
    for arrival in arrivals:
        arrival.wait()
    own, got, down_own, down_got = held
    for n in range(hidden // STEP):
        a = slice(n * STEP, (n + 1) * STEP)
        b = slice(hidden + n * STEP, hidden + (n + 1) * STEP)
        gate = own[:, a] + got[:, a].astype(F32)
        upper = own[:, b] + got[:, b].astype(F32)
        dactive = down_own[:, a] + down_got[:, a].astype(F32)
        sigma = jax.nn.sigmoid(gate)
        dgate[:, a] = (dactive * upper * sigma * (1.0 + gate * (1.0 - sigma))).astype(BF16)
        dupper[:, a] = (dactive * gate * sigma).astype(BF16)
    for n in range(width // STEP):
        copies[2 * n].wait()
        copies[2 * n + 1].wait()
        at = slice(n * STEP, (n + 1) * STEP)
        put_columns(
            pieces,
            n,
            dot_last(dgate[...], held_gate[at, :]) + dot_last(dupper[...], held_up[at, :]),
        )
    finish(message, pieces, out.shape[0], out)


def backward_rest(own, got, down_own, down_got, gate_w, up_w, groups, cost=1024):
    rows = own.shape[0]
    width, hidden = gate_w.shape
    shape = message_shape(groups, rows, width // LANES)
    return call(
        backward_kernel,
        struct(shape, BF16),
        [
            pltpu.VMEM((rows, hidden), BF16),
            pltpu.VMEM((rows, hidden), BF16),
            pltpu.VMEM((width // LANES, rows, LANES), F32),
            pltpu.VMEM(shape, F32),
            *[pltpu.VMEM(x.shape, x.dtype) for x in (own, got, down_own, down_got)],
            pltpu.VMEM(gate_w.shape, BF16),
            pltpu.VMEM(up_w.shape, BF16),
            pltpu.SemaphoreType.DMA((4,)),
            pltpu.SemaphoreType.DMA((2, width // STEP)),
        ],
        (own, got, down_own, down_got, gate_w, up_w),
        in_hbm=(0, 2, 4, 5),
        anywhere=(1, 3),
        cost=cost,
        name="backward_rest",
    )


def returned_rows(source, message, pieces, rows):
    widen(source, message, 0, source.shape[1])
    groups = message.shape[0]
    unfold(message, pieces, pieces.shape[1] // groups, 0, expert_groups(groups, pieces.shape[1]))
    join(pieces, rows)


def combine_forward_kernel(index, source, columns, value, out, square, message, pieces, rows):
    returned_rows(source, message, pieces, rows)
    picks, mixes = [], []
    for k in range(2):
        at = 2 * index + k
        picks.append(token_selector(columns[:, MARK + at : MARK + at + 1], rows.shape[0]))
        mixes.append(columns[:, MIX + at : MIX + at + 1])
    total = jnp.zeros((value.shape[0], 1), F32)
    for n in range(value.shape[1] // STEP):
        at = slice(n * STEP, (n + 1) * STEP)
        mixed = mixes[0] * dot(picks[0], rows[:, at]) + mixes[1] * dot(picks[1], rows[:, at])
        result = (value[:, at].astype(F32) + ROUTE_SCALE * mixed).astype(BF16)
        out[:, at] = result
        wide = result.astype(F32)
        total = total + jnp.sum(wide * wide, axis=1, keepdims=True)
    square[...] = total


def returned_scratch(source, rows, half):
    return [
        pltpu.VMEM(source.shape, F32),
        pltpu.VMEM((half // LANES, rows, LANES), F32),
        pltpu.VMEM((rows, half), BF16),
    ]


def combine_forward(index, source, columns, value):
    tokens, half = value.shape
    rows = source.shape[0] * 2 * SLOTS
    return call(
        functools.partial(combine_forward_kernel, index),
        (struct(value.shape, BF16), struct((tokens, 1), F32)),
        returned_scratch(source, rows, half),
        (source, columns, value),
        name="combine_forward",
    )


def combine_backward_kernel(
    index, source, columns, gain, saved, weighted, part, message, pieces, rows
):
    returned_rows(source, message, pieces, rows)
    chosen = sum(
        token_selector(columns[:, MARK + at : MARK + at + 1], rows.shape[0])
        for at in (2 * index, 2 * index + 1)
    )
    total = jnp.zeros((saved.shape[0], 1), F32)
    for n in range(saved.shape[1] // STEP):
        at = slice(n * STEP, (n + 1) * STEP)
        result = dot(chosen, rows[:, at]) * gain[:, at]
        weighted[:, at] = result
        total = total + jnp.sum(result * saved[:, at].astype(F32), axis=1, keepdims=True)
    part[...] = total


def combine_backward(index, source, columns, gain, saved):
    tokens, half = saved.shape
    rows = source.shape[0] * 2 * SLOTS
    return call(
        functools.partial(combine_backward_kernel, index),
        (struct(saved.shape, F32), struct((tokens, 1), F32)),
        returned_scratch(source, rows, half),
        (source, columns, gain, saved),
        name="combine_backward",
    )


def home_rows(source, message, pieces, rows, side):
    groups = [(2 * e + side, e * SLOTS) for e in range(message.shape[0] // 2)]
    unfold(message, pieces, SLOTS, 0, groups)
    join(pieces, rows)


def final_backward_kernel(
    index, source, columns, gain, saved, grads, out, message, pieces, rows, weighted
):
    widen(source, message, 0, source.shape[1])
    half = rows.shape[1]
    chosen = sum(
        token_selector(columns[:, MARK + at : MARK + at + 1], rows.shape[0])
        for at in (2 * index, 2 * index + 1)
    )
    total = jnp.zeros((saved.shape[0], 1), F32)
    squares = jnp.zeros((saved.shape[0], 1), F32)
    for side in range(2):
        home_rows(source, message, pieces, rows, side)
        for n in range(half // STEP):
            low = n * STEP
            to = slice(side * half + low, side * half + low + STEP)
            result = dot(chosen, rows[:, low : low + STEP]) * gain[:, to]
            weighted[:, to] = result
            wide = saved[:, to].astype(F32)
            total = total + jnp.sum(result * wide, axis=1, keepdims=True)
            squares = squares + jnp.sum(wide * wide, axis=1, keepdims=True)
    project = total / (2 * half)
    inverse = lax.rsqrt(squares / (2 * half) + EPSILON)
    for n in range(2 * half // STEP):
        at = slice(n * STEP, (n + 1) * STEP)
        wide = saved[:, at].astype(F32)
        out[:, at] = (
            grads[:, at].astype(F32)
            + inverse * (weighted[:, at] - wide * inverse * inverse * project)
        ).astype(BF16)


def final_backward(index, source, columns, gain, saved, grads):
    tokens, width = saved.shape
    rows = source.shape[0] // 2 * SLOTS
    return call(
        functools.partial(final_backward_kernel, index),
        struct(saved.shape, BF16),
        [*returned_scratch(source, rows, width // 2), pltpu.VMEM((tokens, width), F32)],
        (source, columns, gain, saved, grads),
        name="final_backward",
    )


def swap_dp(value):
    return lax.ppermute(value, "dp", [(0, 1), (1, 0)])


def move_section(value, step, flip_dp=False):
    sections = lax.axis_size("section")
    halves = lax.axis_size("dp")
    route = []
    for s in range(sections):
        if 0 <= s + step < sections:
            for d in range(halves):
                to = 1 - d if flip_dp else d
                route.append((s * halves + d, (s + step) * halves + to))
    return lax.ppermute(value, ("section", "dp"), route)


def route(message, axes="expert"):
    return lax.all_to_all(message, axes, split_axis=0, concat_axis=0, tiled=True)


def after(value, *earlier):
    return lax.optimization_barrier((value, *earlier))[0]


def body(
    fwd_input,
    back_saved,
    back_grad,
    norm_gain,
    gate_weight,
    up_weight,
    down_weight,
    routes,
    slots,
    affinity,
):
    experts = lax.axis_size("expert")
    tokens = fwd_input.shape[1]
    width = fwd_input.shape[2]
    half = width // 2
    rows = experts * 2 * SLOTS
    side = lax.axis_index("dp")
    both = ("expert", "dp")
    gate_w, up_w, down_w = gate_weight[0, 0], up_weight[0, 0], down_weight[0, 0]
    gain = norm_gain
    gain_half = lax.dynamic_slice(gain, (0, side * half), (1, half))

    x0, s0, s1, g0 = fwd_input[0], back_saved[0, 0], back_saved[1, 0], back_grad[0]

    def inverse_of(value):
        wide = value.astype(F32)
        return lax.rsqrt(jnp.mean(wide * wide, axis=-1) + EPSILON)

    def in_order(own, other):
        return jnp.where(side == 0, own, other), jnp.where(side == 0, other, own)

    def flat(value):
        return jnp.transpose(value, (0, 2, 1)).reshape(8, tokens)

    chosen, held = routes[:, 0], slots[:, 0]
    mixing = affinity[:, 0] / jnp.sum(affinity[:, 0], axis=-1, keepdims=True)
    inverses = jnp.stack([inverse_of(s0), inverse_of(s1), inverse_of(x0)])

    def scalars_of(first_rows, marks):
        return jnp.concatenate([first_rows, flat(marks.astype(F32)), flat(mixing)])

    local = scalars_of(jnp.zeros_like(inverses), chosen * SLOTS + held)
    own_scalars = scalars_of(
        after(inverses, local), chosen * (2 * SLOTS) + side * SLOTS + held
    )
    table = jnp.concatenate(in_order(own_scalars, swap_dp(own_scalars)), axis=1)
    local_columns = jnp.transpose(local)
    columns = jnp.transpose(table)

    def swap_halves(values):
        stacked = jnp.stack(values)
        own = lax.dynamic_slice_in_dim(stacked, side * half, half, axis=2)
        other = lax.dynamic_slice_in_dim(stacked, (1 - side) * half, half, axis=2)
        a, b = in_order(own, swap_dp(other))
        joined = jnp.concatenate([a, b], axis=1)
        return [joined[i] for i in range(len(values))]

    def full_features(value):
        mine, theirs = in_order(value[:tokens], value[tokens:])
        return jnp.concatenate(in_order(mine, swap_dp(theirs)), axis=1)

    def gradient(saved, inverse_row, grads, weighted, part):
        project = (part + swap_dp(part)) / width
        inverse = columns[:, inverse_row : inverse_row + 1]
        wide = saved.astype(F32)
        return (
            grads.astype(F32) + inverse * (weighted - wide * inverse * inverse * project)
        ).astype(BF16)

    first_sent = spread(
        (("normed", 0), ("normed", 1)), local, local_columns, gain, (x0, s0), experts
    )
    first = route(first_sent, both)
    g0h, s1h, x0h, s0h = swap_halves([after(g0, first_sent), s1, x0, s0])
    second_sent = place(
        (("grads", 1, None), ("normed", 3, SECOND_SAVED)),
        table,
        columns,
        gain_half,
        (g0h, s1h),
        experts,
    )
    second = route(after(second_sent, first))
    x0_sent, x0_own = partial(after(first, second_sent), 0, 2, (gate_w, up_w), rows, False)
    x0_got = swap_dp(x0_sent)
    s0_sent, s0_own = partial(after(first, x0_sent), 1, 2, (gate_w, up_w), rows, False)
    out0 = forward_rest(x0_own, after(x0_got, s0_sent), down_w, experts)
    s0_got = swap_dp(after(s0_sent, x0_got))
    out0_back = route(after(out0, second))
    g0_sent, g0_own = partial(after(second, out0), 0, 2, (down_w,), rows, True)
    g0_got = swap_dp(g0_sent)
    s1_sent, s1_own = partial(after(second, g0_sent), 1, 2, (gate_w, up_w), rows, False)
    dexp0 = backward_rest(
        s0_own, after(s0_got, s1_sent), g0_own, g0_got, gate_w, up_w, experts, LONG
    )
    s1_got = swap_dp(after(s1_sent, s0_got, g0_got))
    dexp0_back = route(after(dexp0, out0_back))

    first_out, square = combine_forward(0, after(out0_back, dexp0), columns, x0h)
    x2h = move_section(first_out, 1)
    square_other = move_section(square, 1, flip_dp=True)
    x2_placed = place(
        (("moved", 2, None),),
        table,
        columns,
        gain_half,
        (x2h, square_other),
        experts,
    )
    x2_rows = route(after(x2_placed, dexp0_back))

    weighted, part = combine_backward(1, after(dexp0_back, s1_got), columns, gain_half, s0h)
    g3h = move_section(gradient(s0h, FIRST_SAVED, g0h, weighted, part), -1)
    g3_placed = place((("grads", 3, None),), table, columns, gain_half, (g3h,), experts)
    x2_sent, x2_own = partial(after(x2_rows, g3_placed), 0, 1, (gate_w, up_w), rows, False)
    g3_rows = route(after(g3_placed, x2_sent))

    out2 = forward_rest(x2_own, swap_dp(x2_sent), down_w, experts, LONG)
    g3_sent, g3_own = partial(after(g3_rows, out2), 0, 1, (down_w,), rows, True)
    out2_back = route(after(out2, g3_sent))
    dexp1 = backward_rest(
        s1_own, s1_got, g3_own, swap_dp(g3_sent), gate_w, up_w, 2 * experts, LONG
    )
    dexp1_back = route(after(dexp1, out2_back), both)

    final_half, _ = combine_forward(2, after(out2_back, dexp1), columns, x2h)
    final_out = full_features(final_half)
    g3 = full_features(after(g3h, dexp1))
    final_back = final_backward(3, dexp1_back, local_columns, gain, s1, g3)
    return (final_out[None], final_back[None])


def solution(mesh):
    placed = (
        P("section", ("expert", "dp"), None),
        P(None, "section", ("expert", "dp"), None),
        P("section", ("expert", "dp"), None),
        P("section", None),
        P("section", "expert", "dp", None),
        P("section", "expert", "dp", None),
        P("section", "expert", None, "dp"),
        P(None, "section", ("expert", "dp"), None),
        P(None, "section", ("expert", "dp"), None),
        P(None, "section", ("expert", "dp"), None),
    )
    return jax.shard_map(
        body,
        mesh=mesh,
        in_specs=placed,
        out_specs=(P("section", ("expert", "dp"), None), P("section", ("expert", "dp"), None)),
        check_vma=False,
    )
```

```python
import functools

import jax
import jax.numpy as jnp
from jax import lax
from jax.experimental import pallas as pl
from jax.experimental.pallas import tpu as pltpu
from jax.sharding import PartitionSpec as P

ROUTE_SCALE = 2.5
EPSILON = 1e-06
BF16 = jnp.bfloat16
F32 = jnp.float32
SLOTS = 7
LANES = 128
LONG = 200_000_000_000
STEP = 256
FIRST_SAVED, SECOND_SAVED, TOKENS = 0, 1, 2
MARK = 3
MIX = 11


def ceil8(count):
    return -(-count // 8) * 8


def call(kernel, out_shape, scratch, operands, in_hbm=(), anywhere=(), out_hbm=False, cost=1024, name=None):
    def place_of(hbm, free=False):
        return pl.BlockSpec(memory_space=pl.ANY if free else pltpu.HBM if hbm else pltpu.VMEM)

    return pl.pallas_call(
        kernel,
        out_shape=out_shape,
        in_specs=[place_of(i in in_hbm, i in anywhere) for i in range(len(operands))],
        out_specs=jax.tree.map(lambda _: place_of(out_hbm), out_shape),
        scratch_shapes=scratch,
        compiler_params=pltpu.CompilerParams(vmem_limit_bytes=50 * 1024 * 1024),
        cost_estimate=pl.CostEstimate(flops=cost, bytes_accessed=1024, transcendentals=0),
        name=name,
    )(*operands)


def start_copy(source, target, sem):
    copy = pltpu.make_async_copy(source, target, sem)
    copy.start()
    return copy


def struct(shape, dtype):
    return jax.ShapeDtypeStruct(shape, dtype)


def dot(left, right):
    return jnp.dot(left, right, preferred_element_type=F32)


def dot_last(left, right):
    return lax.dot_general(left, right, (((1,), (1,)), ((), ())), preferred_element_type=F32)


def put_columns(pieces, step, value):
    for j in range(STEP // LANES):
        pieces[step * (STEP // LANES) + j] = value[:, j * LANES : (j + 1) * LANES]


def fold(pieces, message, count, base, groups):
    for group, first in groups:
        for c in range(pieces.shape[0]):
            message[group, base + c * count : base + (c + 1) * count, :] = pieces[
                c, first : first + count, :
            ]


def unfold(message, pieces, count, base, groups):
    for group, first in groups:
        for c in range(pieces.shape[0]):
            pieces[c, first : first + count, :] = message[
                group, base + c * count : base + (c + 1) * count, :
            ]


def clear_padding(message, count, base, size):
    used = base + count * size
    if ceil8(used) > used:
        shape = (message.shape[0], ceil8(used) - used, LANES)
        message[:, used : ceil8(used), :] = jnp.zeros(shape, F32)


def join(pieces, rows):
    for c in range(pieces.shape[0]):
        rows[:, c * LANES : (c + 1) * LANES] = pieces[c].astype(BF16)


def widen(source, message, low, high):
    for g in range(message.shape[0]):
        message[g] = source[g, low:high, :].astype(F32)


def narrow(message, out):
    for g in range(message.shape[0]):
        out[g] = message[g].astype(BF16)


def row_selector(marks, rows):
    places = lax.broadcasted_iota(jnp.int32, (rows, marks.shape[1]), 0).astype(F32)
    return jnp.where(places == marks, 1.0, 0.0).astype(BF16)


def token_selector(marks, rows):
    places = lax.broadcasted_iota(jnp.int32, (marks.shape[0], rows), 1).astype(F32)
    return jnp.where(places == marks, 1.0, 0.0).astype(BF16)


def spread_kernel(parts, scalars, columns, gain, *refs):
    count = len(parts)
    values, (out, pieces, message, ready) = refs[:count], refs[count:]
    half = pieces.shape[0] * LANES
    rows = pieces.shape[1]
    size = ceil8(SLOTS * pieces.shape[0])
    for t, ((kind, index), value) in enumerate(zip(parts, values)):
        wide = value[...].astype(F32)
        tokens = wide.shape[0]
        at = MARK + 2 * index
        pick = [row_selector(scalars[at + k : at + k + 1, :], rows) for k in range(2)]
        if kind == "grads":
            chosen = jnp.concatenate(pick, axis=1)
            at = MIX + 2 * index
            for k in range(2):
                mix = columns[:, at + k : at + k + 1]
                ready[k * tokens : (k + 1) * tokens, :] = (ROUTE_SCALE * mix * wide).astype(BF16)
        else:
            chosen = pick[0] + pick[1]
            inverse = lax.rsqrt(jnp.mean(wide * wide, axis=-1, keepdims=True) + EPSILON)
            ready[0:tokens, :] = (wide * inverse * gain[...]).astype(BF16)
        depth = chosen.shape[1]
        for h in range(2):
            for n in range(half // STEP):
                low = h * half + n * STEP
                put_columns(pieces, n, dot(chosen, ready[0:depth, low : low + STEP]))
            fold(
                pieces,
                message,
                SLOTS,
                t * size,
                [(2 * e + h, e * SLOTS) for e in range(rows // SLOTS)],
            )
        clear_padding(message, SLOTS, t * size, pieces.shape[0])
    narrow(message, out)


def spread(parts, scalars, columns, gain, values, experts):
    tokens, width = values[0].shape
    chunks = width // 2 // LANES
    rows = experts * SLOTS
    shape = (2 * experts, len(values) * ceil8(SLOTS * chunks), LANES)
    return call(
        functools.partial(spread_kernel, parts),
        struct(shape, BF16),
        [
            pltpu.VMEM((chunks, rows, LANES), F32),
            pltpu.VMEM(shape, F32),
            pltpu.VMEM((2 * tokens, width), BF16),
        ],
        (scalars, columns, gain, *values),
        name="spread",
    )


def place_kernel(parts, rows, table, columns, gain, *refs):
    *inputs, out, pieces, message, ready = refs
    chunks = pieces.shape[0]
    half = chunks * LANES
    count = 2 * SLOTS
    size = ceil8(count * chunks)
    inputs = iter(inputs)
    for t, (kind, index, inverse_row) in enumerate(parts):
        value = next(inputs)[...].astype(F32)
        tokens = value.shape[0]
        pick = [
            row_selector(table[MARK + 2 * index + k : MARK + 2 * index + k + 1, :], rows)
            for k in range(2)
        ]
        if kind == "grads":
            for k in range(2):
                mix = columns[:, MIX + 2 * index + k : MIX + 2 * index + k + 1]
                ready[k * tokens : (k + 1) * tokens, :] = (ROUTE_SCALE * mix * value).astype(BF16)
            chosen = jnp.concatenate(pick, axis=1)
        else:
            if kind == "normed":
                inverse = columns[:, inverse_row : inverse_row + 1]
            else:
                squares = jnp.sum(value * value, axis=1, keepdims=True) + next(inputs)[...]
                inverse = lax.rsqrt(squares / (2 * half) + EPSILON)
            ready[0:tokens, :] = (value * inverse * gain[...]).astype(BF16)
            chosen = pick[0] + pick[1]
        depth = chosen.shape[1]
        for n in range(half // STEP):
            put_columns(pieces, n, dot(chosen, ready[0:depth, n * STEP : (n + 1) * STEP]))
        fold(
            pieces, message, count, t * size, [(e, e * count) for e in range(rows // count)]
        )
        clear_padding(message, count, t * size, chunks)
    narrow(message, out)


def place(parts, table, columns, gain, inputs, experts):
    tokens, half = inputs[0].shape
    chunks = half // LANES
    rows = experts * 2 * SLOTS
    shape = (experts, len(parts) * ceil8(2 * SLOTS * chunks), LANES)
    return call(
        functools.partial(place_kernel, parts, rows),
        struct(shape, BF16),
        [
            pltpu.VMEM((chunks, rows, LANES), F32),
            pltpu.VMEM(shape, F32),
            pltpu.VMEM((2 * tokens, half), BF16),
        ],
        (table, columns, gain, *inputs),
        name="place",
    )


def message_rows(message):
    array, part, parts = message
    size = array.shape[1] // parts
    low = part * size // 16 * 16
    high = min(array.shape[1], -(-(part + 1) * size // 16) * 16)
    return low, high, part * size - low


def expert_groups(groups, rows):
    return [(g, g * (rows // groups)) for g in range(groups)]


def partial_kernel(bounds, count, last, source, *refs):
    low, high, base = bounds
    weights, (sent, own), refs = refs[:count], refs[count : count + 2], refs[count + 2 :]
    arrived, message, pieces, rows, sent_held, own_held, *held, source_sem, sems, out_sems = refs
    hidden = sent.shape[1] // count
    source_copy = start_copy(source.at[:, pl.ds(low, high - low), :], arrived, source_sem)
    copies, results = [], []
    for n in range(hidden // STEP):
        for w in range(count):
            at = pl.ds(n * STEP, STEP)
            where = (at, slice(None)) if last else (slice(None), at)
            copies.append(start_copy(weights[w].at[where], held[w].at[where], sems.at[w, n]))
    groups = message.shape[0]
    total = rows.shape[0]
    source_copy.wait()
    widen(arrived, message, 0, high - low)
    unfold(message, pieces, total // groups, base, expert_groups(groups, total))
    join(pieces, rows)
    copies = iter(copies)
    for n in range(hidden // STEP):
        for w in range(count):
            next(copies).wait()
            at = slice(n * STEP, (n + 1) * STEP)
            if last:
                result = dot_last(rows[...], held[w][at, :])
            else:
                result = dot(rows[...], held[w][:, at])
            to = (slice(None), pl.ds(w * hidden + n * STEP, STEP))
            own_held[to] = result
            sent_held[to] = result.astype(BF16)
            results.append(start_copy(sent_held.at[to], sent.at[to], out_sems.at[0, w, n]))
            results.append(start_copy(own_held.at[to], own.at[to], out_sems.at[1, w, n]))
    for result in results:
        result.wait()


def partial(source, number, of, weights, rows, last):
    low, high, base = message_rows((source, number, of))
    width, hidden = weights[0].shape[::-1] if last else weights[0].shape
    count = len(weights)
    shape = (rows, count * hidden)
    slab = (source.shape[0], high - low, LANES)
    return call(
        functools.partial(partial_kernel, (low, high, base), count, last),
        (struct(shape, BF16), struct(shape, F32)),
        [
            pltpu.VMEM(slab, BF16),
            pltpu.VMEM(slab, F32),
            pltpu.VMEM((width // LANES, rows, LANES), F32),
            pltpu.VMEM((rows, width), BF16),
            pltpu.VMEM(shape, BF16),
            pltpu.VMEM(shape, F32),
            *[pltpu.VMEM(w.shape, BF16) for w in weights],
            pltpu.SemaphoreType.DMA,
            pltpu.SemaphoreType.DMA((count, hidden // STEP)),
            pltpu.SemaphoreType.DMA((2, count, hidden // STEP)),
        ],
        (source, *weights),
        in_hbm=range(1, 1 + count),
        anywhere=(0,),
        out_hbm=True,
        name="partial",
    )


def finish(message, pieces, groups, out):
    total = pieces.shape[1]
    count = total // groups
    fold(pieces, message, count, 0, expert_groups(groups, total))
    clear_padding(message, count, 0, pieces.shape[0])
    narrow(message, out)


def forward_kernel(
    own, got, weight, out, active, pieces, message, own_held, got_held, held, act_sems, sems
):
    hidden, width = held.shape
    own_copy = start_copy(own, own_held, act_sems.at[0])
    got_copy = start_copy(got, got_held, act_sems.at[1])
    copies = []
    for n in range(width // STEP):
        at = (slice(None), pl.ds(n * STEP, STEP))
        copies.append(start_copy(weight.at[at], held.at[at], sems.at[n]))
    own_copy.wait()
    got_copy.wait()
    for n in range(hidden // STEP):
        a = slice(n * STEP, (n + 1) * STEP)
        b = slice(hidden + n * STEP, hidden + (n + 1) * STEP)
        gate = own_held[:, a] + got_held[:, a].astype(F32)
        upper = own_held[:, b] + got_held[:, b].astype(F32)
        active[:, a] = (gate * jax.nn.sigmoid(gate) * upper).astype(BF16)
    for n in range(width // STEP):
        copies[n].wait()
        put_columns(pieces, n, dot(active[...], held[:, n * STEP : (n + 1) * STEP]))
    finish(message, pieces, out.shape[0], out)


def message_shape(groups, rows, chunks):
    return (groups, ceil8(rows // groups * chunks), LANES)


def forward_rest(own, got, weight, groups, cost=1024):
    rows = own.shape[0]
    hidden, width = weight.shape
    shape = message_shape(groups, rows, width // LANES)
    return call(
        forward_kernel,
        struct(shape, BF16),
        [
            pltpu.VMEM((rows, hidden), BF16),
            pltpu.VMEM((width // LANES, rows, LANES), F32),
            pltpu.VMEM(shape, F32),
            pltpu.VMEM(own.shape, F32),
            pltpu.VMEM(got.shape, BF16),
            pltpu.VMEM(weight.shape, BF16),
            pltpu.SemaphoreType.DMA((2,)),
            pltpu.SemaphoreType.DMA((width // STEP,)),
        ],
        (own, got, weight),
        in_hbm=(0, 2),
        anywhere=(1,),
        cost=cost,
        name="forward_rest",
    )


def backward_kernel(*refs):
    activations, (gate_w, up_w, out, dgate, dupper, pieces, message), refs = (
        refs[:4],
        refs[4:11],
        refs[11:],
    )
    held, (held_gate, held_up, act_sems, sems) = refs[:4], refs[4:]
    width, hidden = held_gate.shape
    arrivals = [
        start_copy(activations[i], held[i], act_sems.at[i]) for i in range(len(activations))
    ]
    copies = []
    for n in range(width // STEP):
        at = pl.ds(n * STEP, STEP)
        copies.append(start_copy(gate_w.at[at], held_gate.at[at], sems.at[0, n]))
        copies.append(start_copy(up_w.at[at], held_up.at[at], sems.at[1, n]))
    for arrival in arrivals:
        arrival.wait()
    own, got, down_own, down_got = held
    for n in range(hidden // STEP):
        a = slice(n * STEP, (n + 1) * STEP)
        b = slice(hidden + n * STEP, hidden + (n + 1) * STEP)
        gate = own[:, a] + got[:, a].astype(F32)
        upper = own[:, b] + got[:, b].astype(F32)
        dactive = down_own[:, a] + down_got[:, a].astype(F32)
        sigma = jax.nn.sigmoid(gate)
        dgate[:, a] = (dactive * upper * sigma * (1.0 + gate * (1.0 - sigma))).astype(BF16)
        dupper[:, a] = (dactive * gate * sigma).astype(BF16)
    for n in range(width // STEP):
        copies[2 * n].wait()
        copies[2 * n + 1].wait()
        at = slice(n * STEP, (n + 1) * STEP)
        put_columns(
            pieces,
            n,
            dot_last(dgate[...], held_gate[at, :]) + dot_last(dupper[...], held_up[at, :]),
        )
    finish(message, pieces, out.shape[0], out)


def backward_rest(own, got, down_own, down_got, gate_w, up_w, groups, cost=1024):
    rows = own.shape[0]
    width, hidden = gate_w.shape
    shape = message_shape(groups, rows, width // LANES)
    return call(
        backward_kernel,
        struct(shape, BF16),
        [
            pltpu.VMEM((rows, hidden), BF16),
            pltpu.VMEM((rows, hidden), BF16),
            pltpu.VMEM((width // LANES, rows, LANES), F32),
            pltpu.VMEM(shape, F32),
            *[pltpu.VMEM(x.shape, x.dtype) for x in (own, got, down_own, down_got)],
            pltpu.VMEM(gate_w.shape, BF16),
            pltpu.VMEM(up_w.shape, BF16),
            pltpu.SemaphoreType.DMA((4,)),
            pltpu.SemaphoreType.DMA((2, width // STEP)),
        ],
        (own, got, down_own, down_got, gate_w, up_w),
        in_hbm=(0, 2, 4, 5),
        anywhere=(1, 3),
        cost=cost,
        name="backward_rest",
    )


def returned_rows(source, message, pieces, rows):
    widen(source, message, 0, source.shape[1])
    groups = message.shape[0]
    unfold(message, pieces, pieces.shape[1] // groups, 0, expert_groups(groups, pieces.shape[1]))
    join(pieces, rows)


def combine_forward_kernel(index, source, columns, value, out, square, message, pieces, rows):
    returned_rows(source, message, pieces, rows)
    picks, mixes = [], []
    for k in range(2):
        at = 2 * index + k
        picks.append(token_selector(columns[:, MARK + at : MARK + at + 1], rows.shape[0]))
        mixes.append(columns[:, MIX + at : MIX + at + 1])
    total = jnp.zeros((value.shape[0], 1), F32)
    for n in range(value.shape[1] // STEP):
        at = slice(n * STEP, (n + 1) * STEP)
        mixed = mixes[0] * dot(picks[0], rows[:, at]) + mixes[1] * dot(picks[1], rows[:, at])
        result = (value[:, at].astype(F32) + ROUTE_SCALE * mixed).astype(BF16)
        out[:, at] = result
        wide = result.astype(F32)
        total = total + jnp.sum(wide * wide, axis=1, keepdims=True)
    square[...] = total


def returned_scratch(source, rows, half):
    return [
        pltpu.VMEM(source.shape, F32),
        pltpu.VMEM((half // LANES, rows, LANES), F32),
        pltpu.VMEM((rows, half), BF16),
    ]


def combine_forward(index, source, columns, value):
    tokens, half = value.shape
    rows = source.shape[0] * 2 * SLOTS
    return call(
        functools.partial(combine_forward_kernel, index),
        (struct(value.shape, BF16), struct((tokens, 1), F32)),
        returned_scratch(source, rows, half),
        (source, columns, value),
        name="combine_forward",
    )


def combine_backward_kernel(
    index, source, columns, gain, saved, weighted, part, message, pieces, rows
):
    returned_rows(source, message, pieces, rows)
    chosen = sum(
        token_selector(columns[:, MARK + at : MARK + at + 1], rows.shape[0])
        for at in (2 * index, 2 * index + 1)
    )
    total = jnp.zeros((saved.shape[0], 1), F32)
    for n in range(saved.shape[1] // STEP):
        at = slice(n * STEP, (n + 1) * STEP)
        result = dot(chosen, rows[:, at]) * gain[:, at]
        weighted[:, at] = result
        total = total + jnp.sum(result * saved[:, at].astype(F32), axis=1, keepdims=True)
    part[...] = total


def combine_backward(index, source, columns, gain, saved):
    tokens, half = saved.shape
    rows = source.shape[0] * 2 * SLOTS
    return call(
        functools.partial(combine_backward_kernel, index),
        (struct(saved.shape, F32), struct((tokens, 1), F32)),
        returned_scratch(source, rows, half),
        (source, columns, gain, saved),
        name="combine_backward",
    )


def home_rows(source, message, pieces, rows, side):
    groups = [(2 * e + side, e * SLOTS) for e in range(message.shape[0] // 2)]
    unfold(message, pieces, SLOTS, 0, groups)
    join(pieces, rows)


def final_backward_kernel(
    index, source, columns, gain, saved, grads, out, message, pieces, rows, weighted
):
    widen(source, message, 0, source.shape[1])
    half = rows.shape[1]
    chosen = sum(
        token_selector(columns[:, MARK + at : MARK + at + 1], rows.shape[0])
        for at in (2 * index, 2 * index + 1)
    )
    total = jnp.zeros((saved.shape[0], 1), F32)
    squares = jnp.zeros((saved.shape[0], 1), F32)
    for side in range(2):
        home_rows(source, message, pieces, rows, side)
        for n in range(half // STEP):
            low = n * STEP
            to = slice(side * half + low, side * half + low + STEP)
            result = dot(chosen, rows[:, low : low + STEP]) * gain[:, to]
            weighted[:, to] = result
            wide = saved[:, to].astype(F32)
            total = total + jnp.sum(result * wide, axis=1, keepdims=True)
            squares = squares + jnp.sum(wide * wide, axis=1, keepdims=True)
    project = total / (2 * half)
    inverse = lax.rsqrt(squares / (2 * half) + EPSILON)
    for n in range(2 * half // STEP):
        at = slice(n * STEP, (n + 1) * STEP)
        wide = saved[:, at].astype(F32)
        out[:, at] = (
            grads[:, at].astype(F32)
            + inverse * (weighted[:, at] - wide * inverse * inverse * project)
        ).astype(BF16)


def final_backward(index, source, columns, gain, saved, grads):
    tokens, width = saved.shape
    rows = source.shape[0] // 2 * SLOTS
    return call(
        functools.partial(final_backward_kernel, index),
        struct(saved.shape, BF16),
        [*returned_scratch(source, rows, width // 2), pltpu.VMEM((tokens, width), F32)],
        (source, columns, gain, saved, grads),
        name="final_backward",
    )


def swap_dp(value):
    return lax.ppermute(value, "dp", [(0, 1), (1, 0)])


def move_section(value, step, flip_dp=False):
    sections = lax.axis_size("section")
    halves = lax.axis_size("dp")
    route = []
    for s in range(sections):
        if 0 <= s + step < sections:
            for d in range(halves):
                to = 1 - d if flip_dp else d
                route.append((s * halves + d, (s + step) * halves + to))
    return lax.ppermute(value, ("section", "dp"), route)


def route(message, axes="expert"):
    return lax.all_to_all(message, axes, split_axis=0, concat_axis=0, tiled=True)


def after(value, *earlier):
    return lax.optimization_barrier((value, *earlier))[0]


def body(
    fwd_input,
    back_saved,
    back_grad,
    norm_gain,
    gate_weight,
    up_weight,
    down_weight,
    routes,
    slots,
    affinity,
):
    experts = lax.axis_size("expert")
    tokens = fwd_input.shape[1]
    width = fwd_input.shape[2]
    half = width // 2
    rows = experts * 2 * SLOTS
    side = lax.axis_index("dp")
    both = ("expert", "dp")
    gate_w, up_w, down_w = gate_weight[0, 0], up_weight[0, 0], down_weight[0, 0]
    gain = norm_gain
    gain_half = lax.dynamic_slice(gain, (0, side * half), (1, half))

    x0, s0, s1, g0 = fwd_input[0], back_saved[0, 0], back_saved[1, 0], back_grad[0]

    def inverse_of(value):
        wide = value.astype(F32)
        return lax.rsqrt(jnp.mean(wide * wide, axis=-1) + EPSILON)

    def in_order(own, other):
        return jnp.where(side == 0, own, other), jnp.where(side == 0, other, own)

    def flat(value):
        return jnp.transpose(value, (0, 2, 1)).reshape(8, tokens)

    chosen, held = routes[:, 0], slots[:, 0]
    mixing = affinity[:, 0] / jnp.sum(affinity[:, 0], axis=-1, keepdims=True)
    inverses = jnp.stack([inverse_of(s0), inverse_of(s1), inverse_of(x0)])

    def scalars_of(first_rows, marks):
        return jnp.concatenate([first_rows, flat(marks.astype(F32)), flat(mixing)])

    local = scalars_of(jnp.zeros_like(inverses), chosen * SLOTS + held)
    own_scalars = scalars_of(
        after(inverses, local), chosen * (2 * SLOTS) + side * SLOTS + held
    )
    table = jnp.concatenate(in_order(own_scalars, swap_dp(own_scalars)), axis=1)
    local_columns = jnp.transpose(local)
    columns = jnp.transpose(table)

    def swap_halves(values):
        stacked = jnp.stack(values)
        own = lax.dynamic_slice_in_dim(stacked, side * half, half, axis=2)
        other = lax.dynamic_slice_in_dim(stacked, (1 - side) * half, half, axis=2)
        a, b = in_order(own, swap_dp(other))
        joined = jnp.concatenate([a, b], axis=1)
        return [joined[i] for i in range(len(values))]

    def full_features(value):
        mine, theirs = in_order(value[:tokens], value[tokens:])
        return jnp.concatenate(in_order(mine, swap_dp(theirs)), axis=1)

    def gradient(saved, inverse_row, grads, weighted, part):
        project = (part + swap_dp(part)) / width
        inverse = columns[:, inverse_row : inverse_row + 1]
        wide = saved.astype(F32)
        return (
            grads.astype(F32) + inverse * (weighted - wide * inverse * inverse * project)
        ).astype(BF16)

    first_sent = spread(
        (("normed", 0), ("normed", 1)), local, local_columns, gain, (x0, s0), experts
    )
    first = route(first_sent, both)
    g0h, s1h, x0h, s0h = swap_halves([after(g0, first_sent), s1, x0, s0])
    second_sent = place(
        (("grads", 1, None), ("normed", 3, SECOND_SAVED)),
        table,
        columns,
        gain_half,
        (g0h, s1h),
        experts,
    )
    second = route(after(second_sent, first))
    x0_sent, x0_own = partial(after(first, second_sent), 0, 2, (gate_w, up_w), rows, False)
    x0_got = swap_dp(x0_sent)
    s0_sent, s0_own = partial(after(first, x0_sent), 1, 2, (gate_w, up_w), rows, False)
    out0 = forward_rest(x0_own, after(x0_got, s0_sent), down_w, experts)
    s0_got = swap_dp(after(s0_sent, x0_got))
    out0_back = route(after(out0, second))
    g0_sent, g0_own = partial(after(second, out0), 0, 2, (down_w,), rows, True)
    g0_got = swap_dp(g0_sent)
    s1_sent, s1_own = partial(after(second, g0_sent), 1, 2, (gate_w, up_w), rows, False)
    dexp0 = backward_rest(
        s0_own, after(s0_got, s1_sent), g0_own, g0_got, gate_w, up_w, experts, LONG
    )
    dexp0_back = route(after(dexp0, out0_back))

    first_out, square = combine_forward(0, after(out0_back, dexp0), columns, x0h)
    x2h = move_section(first_out, 1)
    square_other = move_section(square, 1, flip_dp=True)
    s1_got = swap_dp(after(s1_sent, x2h, square_other))
    x2_placed = place(
        (("moved", 2, None),),
        table,
        columns,
        gain_half,
        (x2h, square_other),
        experts,
    )
    x2_rows = route(after(x2_placed, dexp0_back))

    weighted, part = combine_backward(1, after(dexp0_back, s1_got), columns, gain_half, s0h)
    g3h = move_section(gradient(s0h, FIRST_SAVED, g0h, weighted, part), -1)
    g3_placed = place((("grads", 3, None),), table, columns, gain_half, (g3h,), experts)
    x2_sent, x2_own = partial(after(x2_rows, g3_placed), 0, 1, (gate_w, up_w), rows, False)
    g3_rows = route(after(g3_placed, x2_sent))

    out2 = forward_rest(x2_own, swap_dp(x2_sent), down_w, experts, LONG)
    g3_sent, g3_own = partial(after(g3_rows, out2), 0, 1, (down_w,), rows, True)
    out2_back = route(after(out2, g3_sent))
    dexp1 = backward_rest(
        s1_own, s1_got, g3_own, swap_dp(g3_sent), gate_w, up_w, 2 * experts, LONG
    )
    dexp1_back = route(after(dexp1, out2_back), both)

    final_half, _ = combine_forward(2, after(out2_back, dexp1), columns, x2h)
    final_out = full_features(final_half)
    g3 = full_features(after(g3h, dexp1))
    final_back = final_backward(3, dexp1_back, local_columns, gain, s1, g3)
    return (final_out[None], final_back[None])


def solution(mesh):
    placed = (
        P("section", ("expert", "dp"), None),
        P(None, "section", ("expert", "dp"), None),
        P("section", ("expert", "dp"), None),
        P("section", None),
        P("section", "expert", "dp", None),
        P("section", "expert", "dp", None),
        P("section", "expert", None, "dp"),
        P(None, "section", ("expert", "dp"), None),
        P(None, "section", ("expert", "dp"), None),
        P(None, "section", ("expert", "dp"), None),
    )
    return jax.shard_map(
        body,
        mesh=mesh,
        in_specs=placed,
        out_specs=(P("section", ("expert", "dp"), None), P("section", ("expert", "dp"), None)),
        check_vma=False,
    )
```
